32 devices in a mesh: groups: 2 (over y), hid: 4 (over z), emb: 4 (over x, core).
Axes of the slice: x: 2, y: 2, z: 4, core: 2. Of those that a mesh axis runs over, the one named last changes fastest.
Arguments:
- inputs: float32 [256, 6144], P(('groups', 'hid'), 'emb'), parts along dimension 0, may hold values from -160 to 160
- out_grad: float32 [256, 6144], P(('groups', 'hid'), 'emb'), parts along dimension 0, may hold values from -6 to 6
- in_weight: float32 [6144, 24576], P('emb', 'hid'), may hold values from -0.078125 to 0.078125
- in_bias: float32 [24576], P('hid'), may hold values from -4 to 4
- out_weight: float32 [24576, 6144], P('hid', 'emb'), may hold values from -0.0390625 to 0.0390625
- norm_gain: float32 [6144], P('emb'), may hold values from 0.25 to 2.7
Outputs:
- input_grad: float32 [256, 6144], P(('groups', 'hid'), 'emb'), parts along dimension 0
The draws below stay inside these ranges and needn't reach their ends.
There are 2 independent parts, one for each index of `groups`. The reference program is written for one: setup_inputs(seed, part) draws one part's arguments, and reference() takes and returns one part's arrays. A program takes and returns all parts, laid end to end along the dimension named above; an argument that names none is the same for every part. Nothing has to cross between parts.
All inputs are finite; a program needn't handle non-finite values.
Results may differ from the reference program's by a relative error of at most 0.00018.
Values sent between devices are 32-bit elements; how exact they have to be, the bound alone decides.
No kernel may reach another device: no remote copies, remote signals or barrier semaphores. Data moves between devices by JAX's collectives and lax.ppermute only.
A program may use at most 192 MiB of HBM per device.

```python
import math
import jax
import jax.numpy as jnp
from jax import lax

D = 6144
FF = 24576
TOKENS = 128


def draw_inputs(key, part):
    key = jax.random.fold_in(key, 11)
    key_base, key_col, key_row = jax.random.split(key, 3)
    position = jnp.arange(D, dtype=jnp.float32) / D
    column = jnp.exp(position * math.log(3.0) + jax.random.uniform(key_col, (D,), jnp.float32) * math.log(10.0)) / 7.0
    row = jnp.exp((jax.random.uniform(key_row, (TOKENS, 1), jnp.float32) - 0.5) * math.log(10.0))
    base = jnp.clip(jax.random.normal(key_base, (TOKENS, D), jnp.float32), -6.0, 6.0)
    return (row * base * column).astype(jnp.float32)


def draw_norm_gain(key, part):
    key = jax.random.fold_in(key, 23)
    position = jnp.arange(D, dtype=jnp.float32) / D - 0.5
    trend = jnp.exp(position * math.log(3.0))
    factor = jax.random.uniform(key, (D,), jnp.float32, 0.6, 1.4)
    return (trend * factor).astype(jnp.float32)


def strengthened(values, stream_key, source, target, shards_of, factor):
    def block_of(dim):
        return (jnp.arange(values.shape[dim]) // (values.shape[dim] // shards_of)).reshape((-1,) + (1,) * (values.ndim - 1 - dim))

    one_side = jax.random.permutation(stream_key, shards_of)[block_of(target)]
    second = (block_of(target) + shards_of // 2) % shards_of
    return jnp.where((block_of(source) == one_side) | (block_of(source) == second), factor * values, values)


def levels(key, shape, shards, smallest, top_value):
    level = 1.0
    for axis_at, blocks in shards:
        steps = jax.random.uniform(jax.random.fold_in(jax.random.fold_in(key, 6), axis_at), (blocks,), jnp.float32, smallest / len(shards), top_value / len(shards))
        level = level * jnp.repeat(jnp.exp(steps), shape[axis_at] // blocks).reshape((-1,) + (1,) * (len(shape) - 1 - axis_at))
    return level


def scatter_about(stream_key, extent, spread, limit, cuts=(), kind=jnp.bfloat16):
    result = spread * jax.random.normal(stream_key, extent, jnp.float32)
    if cuts:
        result = result * levels(stream_key, extent, cuts, -0.22, 0.18)
    return jnp.clip(result, -limit, limit).astype(kind)


def gaussian_with(own_key, dims, width, limit, shards, heavy, kind=jnp.bfloat16):
    entries = width * jax.random.normal(own_key, dims, jnp.float32)
    if shards:
        entries = entries * levels(own_key, dims, shards, -0.22, 0.18)
    return jnp.clip(strengthened(entries, jax.random.fold_in(own_key, 3), *heavy), -limit, limit).astype(kind)


def setup_inputs(seed: int = 0, part: int = 0) -> dict:
    splits = jax.random.split(jax.random.key(seed), 7)
    part_splits = jax.random.split(jax.random.fold_in(splits[6], part), 7)
    return {
        "inputs": draw_inputs(jax.random.fold_in(jax.random.fold_in(splits[6], part), 71), part),
        "out_grad": gaussian_with(part_splits[1], (TOKENS, D), 1.0, 6.0, ((0, 4), (1, 4)), (1, 0, 4, 2.0), jnp.float32),
        "in_weight": scatter_about(splits[2], (D, FF), D ** -0.5, 0.078125, ((0, 4), (1, 4)), jnp.float32),
        "in_bias": scatter_about(splits[3], (FF,), 1.0, 4.0, ((0, 4),), jnp.float32),
        "out_weight": scatter_about(splits[4], (FF, D), FF ** -0.5, 0.0390625, ((0, 4), (1, 4)), jnp.float32),
        "norm_gain": draw_norm_gain(jax.random.fold_in(splits[6], 71), part),
    }


def gelu_slope(values):
    cdf = 0.5 * (1.0 + lax.erf(values * (1.0 / math.sqrt(2.0))))
    density = jnp.exp(-0.5 * values * values) * (1.0 / math.sqrt(2.0 * math.pi))
    return cdf + values * density

def reference(inputs, out_grad, in_weight, in_bias, out_weight, norm_gain):
    highest = lax.Precision.HIGHEST
    row_mean = lax.optimization_barrier(jnp.mean(inputs, axis=-1, keepdims=True))
    centred = inputs - row_mean
    variance = lax.optimization_barrier(jnp.mean(centred * centred, axis=-1, keepdims=True))
    inv_std = 1.0 / jnp.sqrt(variance + 1e-06)
    normed = centred * inv_std
    scaled = normed * norm_gain
    pre_act = jnp.dot(scaled, in_weight, precision=highest, preferred_element_type=jnp.float32) + in_bias
    back = jnp.dot(out_grad, out_weight.T, precision=highest, preferred_element_type=jnp.float32)
    act_grad = back * gelu_slope(pre_act)
    scaled_grad = jnp.dot(act_grad, in_weight.T, precision=highest, preferred_element_type=jnp.float32)
    normed_grad = scaled_grad * norm_gain
    first = lax.optimization_barrier(jnp.mean(normed_grad, axis=-1, keepdims=True))
    second = lax.optimization_barrier(jnp.mean(normed_grad * normed, axis=-1, keepdims=True))
    return inv_std * (normed_grad - first - normed * second)
```

```python
import functools
import math

import jax
import jax.numpy as jnp
from jax import lax
from jax.experimental import pallas as pl
from jax.experimental.pallas import tpu as pltpu
from jax.sharding import PartitionSpec as P

VMEM_LIMIT = 40 * 1024 * 1024
CHUNKS = 2


def gelu_slope(values):
    cdf = 0.5 * (1.0 + lax.erf(values * (1.0 / math.sqrt(2.0))))
    density = jnp.exp(-0.5 * values * values) * (1.0 / math.sqrt(2.0 * math.pi))
    return cdf + values * density


def split(values):
    high = values.astype(jnp.bfloat16)
    return high, (values - high.astype(jnp.float32)).astype(jnp.bfloat16)


def divisor(extent, *choices):
    return next(c for c in choices if extent % c == 0)


def three_pass(both, weight, dims):
    rows = both.shape[0] // 2
    high, low = split(weight)
    dot = functools.partial(
        lax.dot_general,
        dimension_numbers=((dims[:1], dims[1:]), ((), ())),
        preferred_element_type=jnp.float32,
    )
    first = dot(both, high)
    return first[:rows] + first[rows:] + dot(both[:rows], low)


def forward_kernel(slots, contract, place_ref, *refs):
    slot_refs, (weight_ref, send_ref, keep_ref, both) = refs[:slots], refs[slots:]
    block = slot_refs[0].shape[0]
    total = block * slots

    @pl.when(pl.program_id(0) == 0)
    def _():
        for b in range(slots):
            high, low = split(slot_refs[b][...])
            row = pl.multiple_of(place_ref[b] * block, block)
            both[pl.ds(row, block), :] = high
            both[pl.ds(total + row, block), :] = low

    result = three_pass(both[...], weight_ref[...], (1, contract))
    keep_ref[...] = result[: total // 2]
    send_ref[...] = result[total // 2 :]


def forward(blocks, weight, place, chunk, chunks, by_column):
    slots, (block, depth) = len(blocks), blocks[0].shape
    hidden = weight.shape[1 if by_column else 0] // chunks
    width = divisor(hidden, 512, 384, 256, 128)
    steps = hidden // width
    whole = pl.BlockSpec((block, depth), lambda i, place: (0, 0))
    if by_column:
        weight_spec = pl.BlockSpec((depth, width), lambda i, place: (0, chunk * steps + i))
    else:
        weight_spec = pl.BlockSpec((width, depth), lambda i, place: (chunk * steps + i, 0))
    half = block * slots // 2
    out = jax.ShapeDtypeStruct((half, hidden), jnp.float32)
    return pl.pallas_call(
        functools.partial(forward_kernel, slots, 0 if by_column else 1),
        out_shape=(out, out),
        grid_spec=pltpu.PrefetchScalarGridSpec(
            num_scalar_prefetch=1,
            grid=(steps,),
            in_specs=[whole] * slots + [weight_spec],
            out_specs=[pl.BlockSpec((half, width), lambda i, place: (0, i))] * 2,
            scratch_shapes=[pltpu.VMEM((2 * block * slots, depth), jnp.bfloat16)],
        ),
        compiler_params=pltpu.CompilerParams(vmem_limit_bytes=VMEM_LIMIT),
        cost_estimate=pl.CostEstimate(
            flops=6 * block * slots * depth * hidden,
            bytes_accessed=4 * depth * hidden + 8 * half * hidden,
            transcendentals=0,
        ),
    )(place, *blocks, weight)


def backward_kernel(slots, earlier, place_ref, *refs):
    act_refs, weight_ref = refs[:slots], refs[slots]
    earlier_refs = refs[slots + 1 : slots + 1 + earlier]
    out_refs = refs[slots + 1 + earlier : -2]
    both, result = refs[-2:]
    block = act_refs[0].shape[0]
    total = block * slots

    @pl.when(pl.program_id(0) == 0)
    def _():
        for p in range(slots):
            high, low = split(act_refs[p][...])
            both[p * block : (p + 1) * block, :] = high
            both[total + p * block : total + (p + 1) * block, :] = low

    result[...] = three_pass(both[...], weight_ref[...], (1, 1))
    for b in range(slots):
        row = pl.multiple_of(place_ref[b] * block, block)
        rows = result[pl.ds(row, block), :]
        out_refs[b][...] = rows + earlier_refs[b][...] if earlier else rows


def backward(acts, weight, place, earlier, chunk):
    slots, (block, hidden) = len(acts), acts[0].shape
    depth = weight.shape[0]
    width = divisor(depth, 256, 128)
    tile = pl.BlockSpec((block, width), lambda i, place: (0, i))
    out = jax.ShapeDtypeStruct((block, depth), jnp.float32)
    return pl.pallas_call(
        functools.partial(backward_kernel, slots, len(earlier)),
        out_shape=[out] * slots,
        grid_spec=pltpu.PrefetchScalarGridSpec(
            num_scalar_prefetch=1,
            grid=(depth // width,),
            in_specs=[pl.BlockSpec((block, hidden), lambda i, place: (0, 0))] * slots
            + [pl.BlockSpec((width, hidden), lambda i, place: (i, chunk))]
            + [tile] * len(earlier),
            out_specs=[tile] * slots,
            scratch_shapes=[
                pltpu.VMEM((2 * block * slots, hidden), jnp.bfloat16),
                pltpu.VMEM((block * slots, width), jnp.float32),
            ],
        ),
        compiler_params=pltpu.CompilerParams(vmem_limit_bytes=VMEM_LIMIT),
        cost_estimate=pl.CostEstimate(
            flops=6 * block * slots * depth * hidden,
            bytes_accessed=4 * depth * hidden + 8 * block * slots * depth,
            transcendentals=0,
        ),
    )(place, *acts, weight, *earlier)


def body(hid_size, emb_size, inputs, out_grad, in_weight, in_bias, out_weight, norm_gain):
    chips = emb_size // 2
    tokens, depth = inputs.shape
    model_width = depth * emb_size
    hidden = in_weight.shape[1]
    me = lax.axis_index("emb")
    chip, core = me // 2, me % 2

    def along_hid(values):
        return lax.ppermute(values, "hid", [(i, (i + 1) % hid_size) for i in range(hid_size)])

    def other_core(values):
        return lax.ppermute(values, "emb", [(i, i ^ 1) for i in range(emb_size)])

    def next_chip(values):
        return lax.ppermute(values, "emb", [(i, (i + 2) % emb_size) for i in range(emb_size)])

    owner = jnp.arange(emb_size, dtype=jnp.int32)
    place = ((owner % 2) ^ core) * chips + (owner // 2 - chip) % chips

    def gathered(values):
        blocks = [values]
        for _ in range(hid_size - 1):
            blocks.append(along_hid(blocks[-1]))
        return blocks

    grads = gathered(out_grad)

    local_mean = jnp.mean(inputs, axis=-1, keepdims=True)
    local_square = jnp.sum(jnp.square(inputs - local_mean), axis=-1)
    stats = lax.all_gather(jnp.stack([local_mean[:, 0], local_square]), "emb")
    row_mean = jnp.mean(stats[:, 0], axis=0)
    spread = jnp.sum(stats[:, 1] + depth * jnp.square(stats[:, 0] - row_mean), axis=0)
    inv_std = (1.0 / jnp.sqrt(spread / model_width + 1e-06))[:, None]
    normed = (inputs - row_mean[:, None]) * inv_std
    scaled = gathered(normed * norm_gain)

    def reduced(partial):
        send, keep = partial
        summed = keep + other_core(send)
        terms = [summed[d * tokens : (d + 1) * tokens] for d in range(chips)]
        running = terms[chips - 1]
        for step in range(1, chips):
            running = next_chip(running) + terms[chips - 1 - step]
        return running

    back_parts = [forward(grads, out_weight, place, c, CHUNKS, False) for c in range(CHUNKS)]
    backs = [reduced(part) for part in back_parts]
    pre_parts = [forward(scaled, in_weight, place, c, CHUNKS, True) for c in range(CHUNKS)]
    pres = [reduced(part) for part in pre_parts]

    sums = ()
    for c in range(CHUNKS):
        piece = hidden // CHUNKS
        act = backs[c] * gelu_slope(pres[c] + in_bias[c * piece : (c + 1) * piece])
        mine = [None] * chips
        mine[0] = act
        for step in range(1, chips):
            act = next_chip(act)
            mine[(chips - step) % chips] = act
        theirs = [other_core(block) for block in mine]
        sums = backward(mine + theirs, in_weight, place, sums, c)

    running = sums[1 % hid_size]
    for step in range(1, hid_size):
        running = along_hid(running) + sums[(step + 1) % hid_size]
    normed_grad = running * norm_gain
    totals = lax.psum(
        jnp.stack([jnp.sum(normed_grad, axis=-1), jnp.sum(normed_grad * normed, axis=-1)]), "emb"
    )
    first, second = (totals / model_width)[:, :, None]
    return inv_std * (normed_grad - first - normed * second)


def solution(mesh):
    hid_size, emb_size = mesh.shape["hid"], mesh.shape["emb"]
    assert hid_size == emb_size and emb_size % 2 == 0
    return jax.shard_map(
        functools.partial(body, hid_size, emb_size),
        mesh=mesh,
        in_specs=(
            P(("groups", "hid"), "emb"),
            P(("groups", "hid"), "emb"),
            P("emb", "hid"),
            P("hid"),
            P("hid", "emb"),
            P("emb"),
        ),
        out_specs=P(("groups", "hid"), "emb"),
        check_vma=False,
    )
```

```python
import functools
import math

import jax
import jax.numpy as jnp
from jax import lax
from jax.experimental import pallas as pl
from jax.experimental.pallas import tpu as pltpu
from jax.sharding import PartitionSpec as P

VMEM_LIMIT = 40 * 1024 * 1024
CHUNKS = 2


def gelu_slope(values):
    cdf = 0.5 * (1.0 + lax.erf(values * (1.0 / math.sqrt(2.0))))
    density = jnp.exp(-0.5 * values * values) * (1.0 / math.sqrt(2.0 * math.pi))
    return cdf + values * density


def split(values):
    high = values.astype(jnp.bfloat16)
    return high, (values - high.astype(jnp.float32)).astype(jnp.bfloat16)


def divisor(extent, *choices):
    return next(c for c in choices if extent % c == 0)


def three_pass(both, weight_ref, contract, tile, streamed):
    rows = both.shape[0] // 2
    extent = weight_ref.shape
    tiles = [
        (i, j)
        for i in range(0, extent[0], min(tile[0], extent[0]))
        for j in range(0, extent[1], min(tile[1], extent[1]))
    ]
    tile = tuple(min(t, e) for t, e in zip(tile, extent))
    sums = {}

    def loaded(at):
        return split(weight_ref[at[0] : at[0] + tile[0], at[1] : at[1] + tile[1]])

    def multiply(at, parts):
        high, low = parts
        start = at[contract]
        pair = both[:, start : start + tile[contract]]
        if streamed:
            dot = functools.partial(
                lax.dot_general,
                dimension_numbers=(((contract,), (1,)), ((), ())),
                preferred_element_type=jnp.float32,
            )
            first = dot(high, pair)
            value = first[:, :rows] + first[:, rows:] + dot(low, pair[:rows])
        else:
            dot = functools.partial(
                lax.dot_general,
                dimension_numbers=(((1,), (contract,)), ((), ())),
                preferred_element_type=jnp.float32,
            )
            first = dot(pair, high)
            value = first[:rows] + first[rows:] + dot(pair[:rows], low)
        key = at[1 - contract]
        sums[key] = sums[key] + value if key in sums else value

    ready = loaded(tiles[0])
    for n, at in enumerate(tiles):
        following = loaded(tiles[n + 1]) if n + 1 < len(tiles) else None
        multiply(at, ready)
        ready = following
    return [sums[key].T if streamed else sums[key] for key in sorted(sums)]


def forward_kernel(slots, contract, tile, streamed, place_ref, *refs):
    slot_refs, weight_ref, (send_ref, keep_ref, both) = refs[:slots], refs[slots], refs[-3:]
    block = slot_refs[0].shape[0]
    total = block * slots

    @pl.when(pl.program_id(0) == 0)
    def _():
        for b in range(slots):
            high, low = split(slot_refs[b][...])
            row = pl.multiple_of(place_ref[b] * block, block)
            both[pl.ds(row, block), :] = high
            both[pl.ds(total + row, block), :] = low

    column = 0
    for part in three_pass(both, weight_ref, contract, tile, streamed):
        width = part.shape[1]
        keep_ref[:, column : column + width] = part[: total // 2]
        send_ref[:, column : column + width] = part[total // 2 :]
        column += width


def forward(blocks, weight, place, chunk, chunks, by_column, tile, streamed, after):
    slots, (block, depth) = len(blocks), blocks[0].shape
    hidden = weight.shape[1 if by_column else 0] // chunks
    width = divisor(hidden, 512, 384, 256, 128)
    steps = hidden // width
    whole = pl.BlockSpec((block, depth), lambda i, place: (0, 0))
    if by_column:
        weight_spec = pl.BlockSpec((depth, width), lambda i, place: (0, chunk * steps + i))
    else:
        weight_spec = pl.BlockSpec((width, depth), lambda i, place: (chunk * steps + i, 0))
    half = block * slots // 2
    out = jax.ShapeDtypeStruct((half, hidden), jnp.float32)
    return pl.pallas_call(
        functools.partial(forward_kernel, slots, 0 if by_column else 1, tile, streamed),
        out_shape=(out, out),
        grid_spec=pltpu.PrefetchScalarGridSpec(
            num_scalar_prefetch=1,
            grid=(steps,),
            in_specs=[whole] * slots + [weight_spec] + [pl.BlockSpec(memory_space=pl.ANY)] * len(after),
            out_specs=[pl.BlockSpec((half, width), lambda i, place: (0, i))] * 2,
            scratch_shapes=[pltpu.VMEM((2 * block * slots, depth), jnp.bfloat16)],
        ),
        compiler_params=pltpu.CompilerParams(vmem_limit_bytes=VMEM_LIMIT),
        cost_estimate=pl.CostEstimate(
            flops=6 * block * slots * depth * hidden,
            bytes_accessed=4 * depth * hidden + 8 * half * hidden,
            transcendentals=0,
        ),
    )(place, *blocks, weight, *after)


def backward_kernel(slots, earlier, waits, tile, streamed, place_ref, *refs):
    act_refs, weight_ref = refs[:slots], refs[slots]
    earlier_refs = refs[slots + 1 : slots + 1 + earlier]
    out_refs = refs[slots + 1 + earlier + waits : -2]
    both, result = refs[-2:]
    block = act_refs[0].shape[0]
    total = block * slots

    @pl.when(pl.program_id(0) == 0)
    def _():
        for p in range(slots):
            high, low = split(act_refs[p][...])
            both[p * block : (p + 1) * block, :] = high
            both[total + p * block : total + (p + 1) * block, :] = low

    column = 0
    for part in three_pass(both, weight_ref, 1, tile, streamed):
        result[:, column : column + part.shape[1]] = part
        column += part.shape[1]
    for b in range(slots):
        row = pl.multiple_of(place_ref[b] * block, block)
        rows = result[pl.ds(row, block), :]
        out_refs[b][...] = rows + earlier_refs[b][...] if earlier else rows


def backward(acts, weight, place, earlier, chunk, part, parts, tile, streamed, after):
    slots, (block, hidden) = len(acts), acts[0].shape
    depth = weight.shape[0] // parts
    width = divisor(depth, 256, 128)
    steps = depth // width
    out = jax.ShapeDtypeStruct((block, depth), jnp.float32)
    return pl.pallas_call(
        functools.partial(backward_kernel, slots, len(earlier), len(after), tile, streamed),
        out_shape=[out] * slots,
        grid_spec=pltpu.PrefetchScalarGridSpec(
            num_scalar_prefetch=1,
            grid=(steps,),
            in_specs=[pl.BlockSpec((block, hidden), lambda i, place: (0, 0))] * slots
            + [pl.BlockSpec((width, hidden), lambda i, place: (part * steps + i, chunk))]
            + [pl.BlockSpec((block, width), lambda i, place: (0, part * steps + i))] * len(earlier)
            + [pl.BlockSpec(memory_space=pl.ANY)] * len(after),
            out_specs=[pl.BlockSpec((block, width), lambda i, place: (0, i))] * slots,
            scratch_shapes=[
                pltpu.VMEM((2 * block * slots, hidden), jnp.bfloat16),
                pltpu.VMEM((block * slots, width), jnp.float32),
            ],
        ),
        compiler_params=pltpu.CompilerParams(vmem_limit_bytes=VMEM_LIMIT),
        cost_estimate=pl.CostEstimate(
            flops=6 * block * slots * depth * hidden,
            bytes_accessed=4 * depth * hidden + 8 * block * slots * depth,
            transcendentals=0,
        ),
    )(place, *acts, weight, *earlier, *after)


def body(hid_size, emb_size, inputs, out_grad, in_weight, in_bias, out_weight, norm_gain):
    chips = emb_size // 2
    tokens, depth = inputs.shape
    model_width = depth * emb_size
    hidden = in_weight.shape[1]
    me = lax.axis_index("emb")
    chip, core = me // 2, me % 2

    def along_hid(values):
        return lax.ppermute(values, "hid", [(i, (i + 1) % hid_size) for i in range(hid_size)])

    def other_core(values):
        return lax.ppermute(values, "emb", [(i, i ^ 1) for i in range(emb_size)])

    def next_chip(values):
        return lax.ppermute(values, "emb", [(i, (i + 2) % emb_size) for i in range(emb_size)])

    owner = jnp.arange(emb_size, dtype=jnp.int32)
    place = ((owner % 2) ^ core) * chips + (owner // 2 - chip) % chips

    def gathered(values):
        blocks = [values]
        for _ in range(hid_size - 1):
            blocks.append(along_hid(blocks[-1]))
        return blocks

    grads = gathered(out_grad)

    local_mean = jnp.mean(inputs, axis=-1, keepdims=True)
    local_square = jnp.sum(jnp.square(inputs - local_mean), axis=-1)
    stats = lax.all_gather(jnp.stack([local_mean[:, 0], local_square]), "emb")
    row_mean = jnp.mean(stats[:, 0], axis=0)
    spread = jnp.sum(stats[:, 1] + depth * jnp.square(stats[:, 0] - row_mean), axis=0)
    inv_std = (1.0 / jnp.sqrt(spread / model_width + 1e-06))[:, None]
    normed = (inputs - row_mean[:, None]) * inv_std
    scaled = gathered(normed * norm_gain)

    def halved(partial):
        send, keep = partial
        return keep + other_core(send)

    def exchanged(summed):
        terms = [summed[d * tokens : (d + 1) * tokens] for d in range(chips)]
        arrival = next_chip(terms[chips - 1])
        for step in range(2, chips):
            arrival = next_chip(arrival + terms[chips - step])
        return arrival, terms[0]

    tall, wide = (256, depth), (depth, 256)
    back_0 = forward(grads, out_weight, place, 0, CHUNKS, False, tall, True, [scaled[hid_size // 2]])
    back_1 = forward(grads, out_weight, place, 1, CHUNKS, False, tall, False, [scaled[-1], back_0[1]])
    half_0 = halved(back_0)
    back_0 = exchanged(half_0)
    pre_0 = forward(scaled, in_weight, place, 0, CHUNKS, True, wide, False, [half_0])
    half_1 = halved(back_1)
    back_1 = exchanged(half_1)
    pre_1 = forward(scaled, in_weight, place, 1, CHUNKS, True, (256, 512), False, [half_1, back_0[0]])
    backs = [back_0, back_1]
    pres = [exchanged(halved(pre_0)), exchanged(halved(pre_1))]

    def spread_out(c):
        piece = hidden // CHUNKS
        act = sum(backs[c]) * gelu_slope(sum(pres[c]) + in_bias[c * piece : (c + 1) * piece])
        mine = [None] * chips
        mine[0] = act
        for step in range(1, chips):
            act = next_chip(act)
            mine[(chips - step) % chips] = act
        return mine + [other_core(block) for block in mine]

    def summed_along_hid(sums):
        running = sums[1 % hid_size]
        for step in range(1, hid_size):
            running = along_hid(running) + sums[(step + 1) % hid_size]
        return running

    acts_0, acts_1 = spread_out(0), spread_out(1)
    sums = backward(acts_0, in_weight, place, (), 0, 0, 1, (256, 768), True, [pre_1[1]])
    parts = 2 if depth % 512 == 0 else 1
    ends = []
    for part in range(parts):
        form = ((256, 768), (256, 1536))[part]
        ends.append(backward(acts_1, in_weight, place, sums, 1, part, parts, form, False, [ends[-1][0] if ends else sums[0]]))
    running = jnp.concatenate([summed_along_hid(end) for end in ends], axis=1)
    normed_grad = running * norm_gain
    totals = lax.psum(
        jnp.stack([jnp.sum(normed_grad, axis=-1), jnp.sum(normed_grad * normed, axis=-1)]), "emb"
    )
    first, second = (totals / model_width)[:, :, None]
    return inv_std * (normed_grad - first - normed * second)


def solution(mesh):
    hid_size, emb_size = mesh.shape["hid"], mesh.shape["emb"]
    assert hid_size == emb_size and emb_size % 2 == 0
    return jax.shard_map(
        functools.partial(body, hid_size, emb_size),
        mesh=mesh,
        in_specs=(
            P(("groups", "hid"), "emb"),
            P(("groups", "hid"), "emb"),
            P("emb", "hid"),
            P("hid"),
            P("hid", "emb"),
            P("emb"),
        ),
        out_specs=P(("groups", "hid"), "emb"),
        check_vma=False,
    )
```

```python
import functools
import math

import jax
import jax.numpy as jnp
from jax import lax
from jax.experimental import pallas as pl
from jax.experimental.pallas import tpu as pltpu
from jax.sharding import PartitionSpec as P

VMEM_LIMIT = 40 * 1024 * 1024
CHUNKS = 2


def gelu_slope(values):
    cdf = 0.5 * (1.0 + lax.erf(values * (1.0 / math.sqrt(2.0))))
    density = jnp.exp(-0.5 * values * values) * (1.0 / math.sqrt(2.0 * math.pi))
    return cdf + values * density


def split(values):
    high = values.astype(jnp.bfloat16)
    return high, (values - high.astype(jnp.float32)).astype(jnp.bfloat16)


def divisor(extent, *choices):
    return next(c for c in choices if extent % c == 0)


def three_pass(both, weight_refs, contract, width):
    rows = both.shape[0] // 2
    deep = weight_refs[0].shape[contract]
    extent = weight_refs[0].shape[1 - contract]
    width = min(width, extent)
    dot = functools.partial(
        lax.dot_general,
        dimension_numbers=(((1,), (contract,)), ((), ())),
        preferred_element_type=jnp.float32,
    )
    for column in range(0, extent, width):
        total = None
        for n, ref in enumerate(weight_refs):
            tile = ref[:, column : column + width] if contract == 0 else ref[column : column + width, :]
            high, low = split(tile)
            pair = both[:, n * deep : (n + 1) * deep]
            first = dot(pair, high)
            value = first[:rows] + first[rows:] + dot(pair[:rows], low)
            total = value if total is None else total + value
        yield column, total


def pieces_of(weight_block, index, contract, pieces):
    shape = list(weight_block)
    shape[contract] //= pieces

    def spec(n):
        def at(i, place):
            row, column = index(i)
            return (row * pieces + n, column) if contract == 0 else (row, column * pieces + n)

        return pl.BlockSpec(tuple(shape), at)

    return [spec(n) for n in range(pieces)]


def forward_kernel(slots, pieces, contract, place_ref, *refs):
    slot_refs, weight_refs, (send_ref, keep_ref, both) = refs[:slots], refs[slots : slots + pieces], refs[-3:]
    block = slot_refs[0].shape[0]
    total = block * slots

    @pl.when(pl.program_id(0) == 0)
    def _():
        for b in range(slots):
            high, low = split(slot_refs[b][...])
            row = pl.multiple_of(place_ref[b] * block, block)
            both[pl.ds(row, block), :] = high
            both[pl.ds(total + row, block), :] = low

    for column, part in three_pass(both, weight_refs, contract, 256):
        width = part.shape[1]
        keep_ref[:, column : column + width] = part[: total // 2]
        send_ref[:, column : column + width] = part[total // 2 :]


def forward(blocks, weight, place, chunk, chunks, by_column, pieces, after):
    slots, (block, depth) = len(blocks), blocks[0].shape
    hidden = weight.shape[1 if by_column else 0] // chunks
    width = divisor(hidden, 512, 384, 256, 128)
    steps = hidden // width
    whole = pl.BlockSpec((block, depth), lambda i, place: (0, 0))
    if by_column:
        weight_specs = pieces_of((depth, width), lambda i: (0, chunk * steps + i), 0, pieces)
    else:
        weight_specs = pieces_of((width, depth), lambda i: (chunk * steps + i, 0), 1, pieces)
    half = block * slots // 2
    out = jax.ShapeDtypeStruct((half, hidden), jnp.float32)
    return pl.pallas_call(
        functools.partial(forward_kernel, slots, pieces, 0 if by_column else 1),
        out_shape=(out, out),
        grid_spec=pltpu.PrefetchScalarGridSpec(
            num_scalar_prefetch=1,
            grid=(steps,),
            in_specs=[whole] * slots + weight_specs + [pl.BlockSpec(memory_space=pl.ANY)] * len(after),
            out_specs=[pl.BlockSpec((half, width), lambda i, place: (0, i))] * 2,
            scratch_shapes=[pltpu.VMEM((2 * block * slots, depth), jnp.bfloat16)],
        ),
        compiler_params=pltpu.CompilerParams(vmem_limit_bytes=VMEM_LIMIT),
        cost_estimate=pl.CostEstimate(
            flops=6 * block * slots * depth * hidden,
            bytes_accessed=4 * depth * hidden + 8 * half * hidden,
            transcendentals=0,
        ),
    )(place, *blocks, *[weight] * pieces, *after)


def backward_kernel(slots, pieces, earlier, place_ref, *refs):
    act_refs, weight_refs = refs[:slots], refs[slots : slots + pieces]
    earlier_refs = refs[slots + pieces : slots + pieces + earlier]
    out_refs = refs[-2 - slots : -2]
    both, result = refs[-2:]
    block = act_refs[0].shape[0]
    total = block * slots

    @pl.when(pl.program_id(0) == 0)
    def _():
        for p in range(slots):
            high, low = split(act_refs[p][...])
            both[p * block : (p + 1) * block, :] = high
            both[total + p * block : total + (p + 1) * block, :] = low

    for column, part in three_pass(both, weight_refs, 1, 256):
        result[:, column : column + part.shape[1]] = part
    for b in range(slots):
        row = pl.multiple_of(place_ref[b] * block, block)
        rows = result[pl.ds(row, block), :]
        out_refs[b][...] = rows + earlier_refs[b][...] if earlier else rows


def backward(acts, weight, place, earlier, chunk, part, parts, pieces, after):
    slots, (block, hidden) = len(acts), acts[0].shape
    depth = weight.shape[0] // parts
    width = divisor(depth, 256, 128)
    steps = depth // width
    out = jax.ShapeDtypeStruct((block, depth), jnp.float32)
    return pl.pallas_call(
        functools.partial(backward_kernel, slots, pieces, len(earlier)),
        out_shape=[out] * slots,
        grid_spec=pltpu.PrefetchScalarGridSpec(
            num_scalar_prefetch=1,
            grid=(steps,),
            in_specs=[pl.BlockSpec((block, hidden), lambda i, place: (0, 0))] * slots
            + pieces_of((width, hidden), lambda i: (part * steps + i, chunk), 1, pieces)
            + [pl.BlockSpec((block, width), lambda i, place: (0, part * steps + i))] * len(earlier)
            + [pl.BlockSpec(memory_space=pl.ANY)] * len(after),
            out_specs=[pl.BlockSpec((block, width), lambda i, place: (0, i))] * slots,
            scratch_shapes=[
                pltpu.VMEM((2 * block * slots, hidden), jnp.bfloat16),
                pltpu.VMEM((block * slots, width), jnp.float32),
            ],
        ),
        compiler_params=pltpu.CompilerParams(vmem_limit_bytes=VMEM_LIMIT),
        cost_estimate=pl.CostEstimate(
            flops=6 * block * slots * depth * hidden,
            bytes_accessed=4 * depth * hidden + 8 * block * slots * depth,
            transcendentals=0,
        ),
    )(place, *acts, *[weight] * pieces, *earlier, *after)


def body(hid_size, emb_size, inputs, out_grad, in_weight, in_bias, out_weight, norm_gain):
    chips = emb_size // 2
    tokens, depth = inputs.shape
    model_width = depth * emb_size
    hidden = in_weight.shape[1]
    me = lax.axis_index("emb")
    chip, core = me // 2, me % 2

    def along_hid(values, steps=1):
        return lax.ppermute(values, "hid", [(i, (i + steps) % hid_size) for i in range(hid_size)])

    def other_core(values):
        return lax.ppermute(values, "emb", [(i, i ^ 1) for i in range(emb_size)])

    def next_chip(values):
        return lax.ppermute(values, "emb", [(i, (i + 2) % emb_size) for i in range(emb_size)])

    owner = jnp.arange(emb_size, dtype=jnp.int32)
    place = ((owner % 2) ^ core) * chips + (owner // 2 - chip) % chips

    def gathered(values):
        blocks = [values]
        for _ in range(hid_size - 1):
            blocks.append(along_hid(blocks[-1]))
        return blocks

    grads = [out_grad] + [along_hid(out_grad, step) for step in range(1, hid_size)]

    local_mean = jnp.mean(inputs, axis=-1, keepdims=True)
    local_square = jnp.sum(jnp.square(inputs - local_mean), axis=-1)
    stats = lax.all_gather(jnp.stack([local_mean[:, 0], local_square]), "emb")
    row_mean = jnp.mean(stats[:, 0], axis=0)
    spread = jnp.sum(stats[:, 1] + depth * jnp.square(stats[:, 0] - row_mean), axis=0)
    inv_std = (1.0 / jnp.sqrt(spread / model_width + 1e-06))[:, None]
    normed = (inputs - row_mean[:, None]) * inv_std
    scaled = gathered(normed * norm_gain)

    def halved(partial):
        send, keep = partial
        return keep + other_core(send)

    def exchanged(summed):
        terms = [summed[d * tokens : (d + 1) * tokens] for d in range(chips)]
        arrival = next_chip(terms[chips - 1])
        for step in range(2, chips):
            arrival = next_chip(arrival + terms[chips - step])
        return arrival, terms[0]

    many = 6 if depth % 768 == 0 else 3
    back_0 = forward(grads, out_weight, place, 0, CHUNKS, False, 3, [scaled[1]])
    half_0 = halved(back_0)
    back_1 = forward(grads, out_weight, place, 1, CHUNKS, False, many, [half_0, scaled[hid_size // 2]])
    half_1 = halved(back_1)
    back_0, back_1 = exchanged(half_0), exchanged(half_1)
    pre_0 = forward(scaled, in_weight, place, 0, CHUNKS, True, 3, [half_1, back_0[0]])
    pre_1 = forward(scaled, in_weight, place, 1, CHUNKS, True, many, [pre_0[1], back_1[0]])
    backs = [back_0, back_1]
    pres = [exchanged(halved(pre_0)), exchanged(halved(pre_1))]

    def spread_out(c):
        piece = hidden // CHUNKS
        act = sum(backs[c]) * gelu_slope(sum(pres[c]) + in_bias[c * piece : (c + 1) * piece])
        mine = [None] * chips
        mine[0] = act
        for step in range(1, chips):
            act = next_chip(act)
            mine[(chips - step) % chips] = act
        return mine + [other_core(block) for block in mine]

    def summed_along_hid(sums):
        return sum([along_hid(sums[step], -step) for step in range(1, hid_size)], start=sums[0])

    acts_0, acts_1 = spread_out(0), spread_out(1)
    sums = backward(acts_0, in_weight, place, (), 0, 0, 1, 6, [pre_1[1]])
    parts = 2 if depth % 512 == 0 else 1
    ends = []
    for part in range(parts):
        ends.append(backward(acts_1, in_weight, place, sums, 1, part, parts, 6, [ends[-1][0] if ends else sums[0]]))
    running = jnp.concatenate([summed_along_hid(end) for end in ends], axis=1)
    normed_grad = running * norm_gain
    totals = lax.psum(
        jnp.stack([jnp.sum(normed_grad, axis=-1), jnp.sum(normed_grad * normed, axis=-1)]), "emb"
    )
    first, second = (totals / model_width)[:, :, None]
    return inv_std * (normed_grad - first - normed * second)


def solution(mesh):
    hid_size, emb_size = mesh.shape["hid"], mesh.shape["emb"]
    assert hid_size == emb_size and emb_size % 2 == 0
    return jax.shard_map(
        functools.partial(body, hid_size, emb_size),
        mesh=mesh,
        in_specs=(
            P(("groups", "hid"), "emb"),
            P(("groups", "hid"), "emb"),
            P("emb", "hid"),
            P("hid"),
            P("hid", "emb"),
            P("emb"),
        ),
        out_specs=P(("groups", "hid"), "emb"),
        check_vma=False,
    )
```

```python
import functools
import math

import jax
import jax.numpy as jnp
from jax import lax
from jax.experimental import pallas as pl
from jax.experimental.pallas import tpu as pltpu
from jax.sharding import PartitionSpec as P

VMEM_LIMIT = 6 * 1024 * 1024
CHUNKS = 2


def gelu_slope(values):
    cdf = 0.5 * (1.0 + lax.erf(values * (1.0 / math.sqrt(2.0))))
    density = jnp.exp(-0.5 * values * values) * (1.0 / math.sqrt(2.0 * math.pi))
    return cdf + values * density


def split(values):
    high = values.astype(jnp.bfloat16)
    return high, (values - high.astype(jnp.float32)).astype(jnp.bfloat16)


def divisor(extent, *choices):
    return next(c for c in choices if extent % c == 0)


def prepare_kernel(rows, columns, block, depth, weight_ref, *refs):
    high_ref, low_ref, landed, arrived = refs[-4:]
    steps = rows[1] // block

    def fetch(step):
        start = pl.multiple_of(rows[0] + step * block, block)
        slot = lax.rem(step, depth)
        return pltpu.make_async_copy(
            weight_ref.at[pl.ds(start, block), pl.ds(*columns)], landed.at[slot], arrived.at[slot]
        )

    for step in range(min(depth, steps)):
        fetch(step).start()

    @pl.loop(0, steps)
    def _(step):
        fetch(step).wait()
        high, low = split(landed[lax.rem(step, depth)])
        at = pl.ds(pl.multiple_of(step * block, block), block)
        high_ref[at, :] = high
        low_ref[at, :] = low

        @pl.when(step + depth < steps)
        def _():
            fetch(step + depth).start()


def prepare(weight, rows, columns, after):
    block = 128 * 1536 // columns[1]
    block = divisor(rows[1], *[b for b in (256, 128, 64, 32) if b <= max(block, 32)])
    depth = 4
    out = pltpu.VMEM((rows[1], columns[1]), jnp.bfloat16)
    return pl.pallas_call(
        functools.partial(prepare_kernel, rows, columns, block, depth),
        out_shape=(out, out),
        in_specs=[pl.BlockSpec(memory_space=pl.ANY)] * (1 + len(after)),
        out_specs=[pl.BlockSpec(memory_space=pltpu.VMEM)] * 2,
        scratch_shapes=[
            pltpu.VMEM((depth, block, columns[1]), jnp.float32),
            pltpu.SemaphoreType.DMA((depth,)),
        ],
        compiler_params=pltpu.CompilerParams(vmem_limit_bytes=VMEM_LIMIT),
        cost_estimate=pl.CostEstimate(
            flops=0, bytes_accessed=4 * rows[1] * columns[1], transcendentals=0
        ),
    )(weight, *after)


def three_pass(both, high, low, contract):
    rows = both.shape[0] // 2
    dot = functools.partial(
        lax.dot_general,
        dimension_numbers=(((1,), (contract,)), ((), ())),
        preferred_element_type=jnp.float32,
    )
    first = dot(both[...], high)
    return first[:rows] + first[rows:] + dot(both[:rows, :], low)


def forward_kernel(slots, contract, place_ref, *refs):
    slot_refs, (high_ref, low_ref) = refs[:slots], refs[slots : slots + 2]
    send_ref, keep_ref, both = refs[-3:]
    block = slot_refs[0].shape[0]
    total = block * slots
    for b in range(slots):
        high, low = split(slot_refs[b][...])
        row = pl.multiple_of(place_ref[b] * block, block)
        both[pl.ds(row, block), :] = high
        both[pl.ds(total + row, block), :] = low

    hidden = send_ref.shape[1]
    width = divisor(hidden, 256, 128)

    @pl.loop(0, hidden // width)
    def _(step):
        at = pl.ds(pl.multiple_of(step * width, width), width)
        tile = (slice(None), at) if contract == 0 else (at, slice(None))
        part = three_pass(both, high_ref[tile], low_ref[tile], contract)
        keep_ref[:, at] = part[: total // 2]
        send_ref[:, at] = part[total // 2 :]


def forward(blocks, weight, place, by_column, after):
    slots, (block, depth) = len(blocks), blocks[0].shape
    hidden = weight[0].shape[1 if by_column else 0]
    half = block * slots // 2
    out = jax.ShapeDtypeStruct((half, hidden), jnp.float32)
    inside = pl.BlockSpec(memory_space=pltpu.VMEM)
    return pl.pallas_call(
        functools.partial(forward_kernel, slots, 0 if by_column else 1),
        out_shape=(out, out),
        in_specs=[pl.BlockSpec(memory_space=pltpu.SMEM)]
        + [inside] * (slots + 2)
        + [pl.BlockSpec(memory_space=pl.ANY)] * len(after),
        out_specs=[inside] * 2,
        scratch_shapes=[pltpu.VMEM((2 * block * slots, depth), jnp.bfloat16)],
        compiler_params=pltpu.CompilerParams(vmem_limit_bytes=VMEM_LIMIT),
        cost_estimate=pl.CostEstimate(
            flops=6 * block * slots * depth * hidden, bytes_accessed=4 * depth * hidden, transcendentals=0
        ),
    )(place, *blocks, *[pltpu.with_memory_space_constraint(part, pltpu.VMEM) for part in weight], *after)


def backward_kernel(slots, earlier, first_column, place_ref, *refs):
    act_refs, (high_ref, low_ref) = refs[:slots], refs[slots : slots + 2]
    earlier_refs = refs[slots + 2 : slots + 2 + earlier]
    out_refs = refs[-2 - slots : -2]
    both, result = refs[-2:]
    block = act_refs[0].shape[0]
    total = block * slots
    for p in range(slots):
        high, low = split(act_refs[p][...])
        both[p * block : (p + 1) * block, :] = high
        both[total + p * block : total + (p + 1) * block, :] = low

    depth = out_refs[0].shape[1]
    width = result.shape[1]

    @pl.loop(0, depth // width)
    def _(step):
        start = pl.multiple_of(step * width, width)
        tile = (pl.ds(pl.multiple_of(first_column + start, width), width), slice(None))
        result[...] = three_pass(both, high_ref[tile], low_ref[tile], 1)
        for b in range(slots):
            row = pl.multiple_of(place_ref[b] * block, block)
            rows = result[pl.ds(row, block), :]
            if earlier:
                rows = rows + earlier_refs[b][:, pl.ds(pl.multiple_of(first_column + start, width), width)]
            out_refs[b][:, pl.ds(start, width)] = rows


def backward(acts, weight, place, earlier, part, parts, after):
    slots, (block, hidden) = len(acts), acts[0].shape
    depth = weight[0].shape[0] // parts
    width = divisor(depth, 256, 128)
    out = jax.ShapeDtypeStruct((block, depth), jnp.float32)
    inside = pl.BlockSpec(memory_space=pltpu.VMEM)
    return pl.pallas_call(
        functools.partial(backward_kernel, slots, len(earlier), part * depth),
        out_shape=[out] * slots,
        in_specs=[pl.BlockSpec(memory_space=pltpu.SMEM)]
        + [inside] * (slots + 2 + len(earlier))
        + [pl.BlockSpec(memory_space=pl.ANY)] * len(after),
        out_specs=[inside] * slots,
        scratch_shapes=[
            pltpu.VMEM((2 * block * slots, hidden), jnp.bfloat16),
            pltpu.VMEM((block * slots, width), jnp.float32),
        ],
        compiler_params=pltpu.CompilerParams(vmem_limit_bytes=VMEM_LIMIT),
        cost_estimate=pl.CostEstimate(
            flops=6 * block * slots * depth * hidden, bytes_accessed=4 * depth * hidden, transcendentals=0
        ),
    )(place, *acts, *[pltpu.with_memory_space_constraint(part, pltpu.VMEM) for part in weight], *earlier, *after)


def body(hid_size, emb_size, inputs, out_grad, in_weight, in_bias, out_weight, norm_gain):
    chips = emb_size // 2
    tokens, depth = inputs.shape
    model_width = depth * emb_size
    hidden = in_weight.shape[1]
    me = lax.axis_index("emb")
    chip, core = me // 2, me % 2

    def along_hid(values, steps=1):
        return lax.ppermute(values, "hid", [(i, (i + steps) % hid_size) for i in range(hid_size)])

    def other_core(values):
        return lax.ppermute(values, "emb", [(i, i ^ 1) for i in range(emb_size)])

    def next_chip(values):
        return lax.ppermute(values, "emb", [(i, (i + 2) % emb_size) for i in range(emb_size)])

    owner = jnp.arange(emb_size, dtype=jnp.int32)
    place = ((owner % 2) ^ core) * chips + (owner // 2 - chip) % chips

    def gathered(values):
        blocks = [values]
        for _ in range(hid_size - 1):
            blocks.append(along_hid(blocks[-1]))
        return blocks

    grads = [out_grad] + [along_hid(out_grad, step) for step in range(1, hid_size)]

    local_mean = jnp.mean(inputs, axis=-1, keepdims=True)
    local_square = jnp.sum(jnp.square(inputs - local_mean), axis=-1)
    stats = lax.all_gather(jnp.stack([local_mean[:, 0], local_square]), "emb")
    row_mean = jnp.mean(stats[:, 0], axis=0)
    spread = jnp.sum(stats[:, 1] + depth * jnp.square(stats[:, 0] - row_mean), axis=0)
    inv_std = (1.0 / jnp.sqrt(spread / model_width + 1e-06))[:, None]
    normed = (inputs - row_mean[:, None]) * inv_std
    scaled = gathered(normed * norm_gain)

    def halved(partial):
        send, keep = partial
        return keep + other_core(send)

    def exchanged(summed):
        terms = [summed[d * tokens : (d + 1) * tokens] for d in range(chips)]
        arrival = next_chip(terms[chips - 1])
        for step in range(2, chips):
            arrival = next_chip(arrival + terms[chips - step])
        return arrival, terms[0]

    piece = hidden // CHUNKS
    out_parts = [prepare(out_weight, (c * piece, piece), (0, depth), [scaled[0]]) for c in range(CHUNKS)]
    back_0 = forward(grads, out_parts[0], place, False, [scaled[1], out_parts[1][0]])
    half_0 = halved(back_0)
    back_1 = forward(grads, out_parts[1], place, False, [back_0[1]])
    half_1 = halved(back_1)
    back_0, back_1 = exchanged(half_0), exchanged(half_1)
    in_parts_0 = prepare(in_weight, (0, depth), (0, piece), [half_0, scaled[hid_size // 2]])
    pre_0 = forward(scaled, in_parts_0, place, True, [half_1])
    in_parts_1 = prepare(in_weight, (0, depth), (piece, piece), [pre_0[1], back_0[0]])
    pre_1 = forward(scaled, in_parts_1, place, True, [back_1[0]])
    backs = [back_0, back_1]
    pres = [exchanged(halved(pre_0)), exchanged(halved(pre_1))]

    def spread_out(c):
        act = sum(backs[c]) * gelu_slope(sum(pres[c]) + in_bias[c * piece : (c + 1) * piece])
        mine = [None] * chips
        mine[0] = act
        for step in range(1, chips):
            act = next_chip(act)
            mine[(chips - step) % chips] = act
        return mine + [other_core(block) for block in mine]

    def summed_along_hid(sums):
        return sum([along_hid(sums[step], -step) for step in range(1, hid_size)], start=sums[0])

    acts_0, acts_1 = spread_out(0), spread_out(1)
    sums = backward(acts_0, in_parts_0, place, (), 0, 1, [pre_1[1]])
    parts = 2 if depth % 512 == 0 else 1
    ends = []
    for part in range(parts):
        ends.append(backward(acts_1, in_parts_1, place, sums, part, parts, [ends[-1][0] if ends else sums[0]]))
    running = jnp.concatenate([summed_along_hid(end) for end in ends], axis=1)
    normed_grad = running * norm_gain
    totals = lax.psum(
        jnp.stack([jnp.sum(normed_grad, axis=-1), jnp.sum(normed_grad * normed, axis=-1)]), "emb"
    )
    first, second = (totals / model_width)[:, :, None]
    return inv_std * (normed_grad - first - normed * second)


def solution(mesh):
    hid_size, emb_size = mesh.shape["hid"], mesh.shape["emb"]
    assert hid_size == emb_size and emb_size % 2 == 0
    return jax.shard_map(
        functools.partial(body, hid_size, emb_size),
        mesh=mesh,
        in_specs=(
            P(("groups", "hid"), "emb"),
            P(("groups", "hid"), "emb"),
            P("emb", "hid"),
            P("hid"),
            P("hid", "emb"),
            P("emb"),
        ),
        out_specs=P(("groups", "hid"), "emb"),
        check_vma=False,
    )
```

```python
import functools
import math

import jax
import jax.numpy as jnp
from jax import lax
from jax.experimental import pallas as pl
from jax.experimental.pallas import tpu as pltpu
from jax.sharding import PartitionSpec as P

VMEM_LIMIT = 5 * 1024 * 1024
CHUNKS = 2
SHORT = pl.CostEstimate(flops=1 << 20, bytes_accessed=1 << 18, transcendentals=0)


def gelu_slope(values):
    cdf = 0.5 * (1.0 + lax.erf(values * (1.0 / math.sqrt(2.0))))
    density = jnp.exp(-0.5 * values * values) * (1.0 / math.sqrt(2.0 * math.pi))
    return cdf + values * density


def split(values):
    high = values.astype(jnp.bfloat16)
    return high, (values - high.astype(jnp.float32)).astype(jnp.bfloat16)


def divisor(extent, *choices):
    return next(c for c in choices if extent % c == 0)


def call(kernel, out_shape, operands, after):
    outs = out_shape if isinstance(out_shape, tuple) else (out_shape,)

    def run(*refs):
        kernel(*refs[: len(operands)], *refs[len(operands) + len(after) :])

    inside = pl.BlockSpec(memory_space=pltpu.VMEM)
    result = pl.pallas_call(
        run,
        out_shape=tuple(jax.ShapeDtypeStruct(o.shape, o.dtype) for o in outs),
        in_specs=[inside] * len(operands) + [pl.BlockSpec(memory_space=pl.ANY)] * len(after),
        out_specs=[inside] * len(outs),
        compiler_params=pltpu.CompilerParams(vmem_limit_bytes=VMEM_LIMIT),
        cost_estimate=SHORT,
    )(*operands, *after)
    return result if isinstance(out_shape, tuple) else result[0]


def moments_kernel(inputs_ref, out_ref):
    rows, depth = inputs_ref.shape
    mean = jnp.sum(inputs_ref[...], axis=1, keepdims=True) * (1.0 / depth)
    square = jnp.sum(jnp.square(inputs_ref[...] - mean), axis=1, keepdims=True)
    out_ref[:rows] = jnp.broadcast_to(mean, (rows, 128))
    out_ref[rows:] = jnp.broadcast_to(square, (rows, 128))


def merge(moments, count):
    rows = moments[0].shape[0] // 2
    mean = sum(part[:rows] for part in moments) * (1.0 / len(moments))
    square = sum(part[rows:] + count * jnp.square(part[:rows] - mean) for part in moments)
    return mean, square


def merge_kernel(count, first_ref, second_ref, out_ref):
    rows = out_ref.shape[0] // 2
    out_ref[:rows], out_ref[rows:] = merge((first_ref[...], second_ref[...]), count)


def normalise_kernel(count, inputs_ref, gain_ref, *refs):
    *moment_refs, normed_ref, scaled_ref, inv_std_ref = refs
    mean, square = merge([ref[...] for ref in moment_refs], count)
    inv_std = 1.0 / jnp.sqrt(square * (1.0 / (count * len(moment_refs))) + 1e-06)
    normed = (inputs_ref[...] - mean[:, :1]) * inv_std[:, :1]
    normed_ref[...] = normed
    scaled_ref[...] = normed * gain_ref[...]
    inv_std_ref[...] = inv_std


def prepare_kernel(rows, columns, block, depth, weight_ref, *refs):
    high_ref, low_ref, landed, arrived = refs[-4:]
    steps = rows[1] // block

    def fetch(step):
        start = pl.multiple_of(rows[0] + step * block, block)
        slot = lax.rem(step, depth)
        return pltpu.make_async_copy(
            weight_ref.at[pl.ds(start, block), pl.ds(*columns)], landed.at[slot], arrived.at[slot]
        )

    for step in range(min(depth, steps)):
        fetch(step).start()

    @pl.loop(0, steps)
    def _(step):
        fetch(step).wait()
        high, low = split(landed[lax.rem(step, depth)])
        at = pl.ds(pl.multiple_of(step * block, block), block)
        high_ref[at, :] = high
        low_ref[at, :] = low

        @pl.when(step + depth < steps)
        def _():
            fetch(step + depth).start()


def prepare(weight, rows, columns, after):
    block = 128 * 1536 // columns[1]
    block = divisor(rows[1], *[b for b in (256, 128, 64, 32) if b <= max(block, 32)])
    depth = 4
    out = pltpu.VMEM((rows[1], columns[1]), jnp.bfloat16)
    return pl.pallas_call(
        functools.partial(prepare_kernel, rows, columns, block, depth),
        out_shape=(out, out),
        in_specs=[pl.BlockSpec(memory_space=pl.ANY)] * (1 + len(after)),
        out_specs=[pl.BlockSpec(memory_space=pltpu.VMEM)] * 2,
        scratch_shapes=[
            pltpu.VMEM((depth, block, columns[1]), jnp.float32),
            pltpu.SemaphoreType.DMA((depth,)),
        ],
        compiler_params=pltpu.CompilerParams(vmem_limit_bytes=VMEM_LIMIT),
        cost_estimate=SHORT,
    )(pltpu.with_memory_space_constraint(weight, pltpu.HBM), *after)


def three_pass(both, high, low, contract, streamed):
    rows = both.shape[0] // 2
    dims = ((contract,), (1,)) if streamed else ((1,), (contract,))

    def dot(left, weight):
        pair = (weight, left) if streamed else (left, weight)
        return lax.dot_general(*pair, (dims, ((), ())), preferred_element_type=jnp.float32)

    first, second = dot(both[...], high), dot(both[:rows, :], low)
    if streamed:
        return (first[:, :rows] + first[:, rows:] + second).T
    return first[:rows] + first[rows:] + second


def forward_kernel(slots, contract, streamed, span, earlier, place_ref, *refs):
    slot_refs, (high_ref, low_ref) = refs[:slots], refs[slots : slots + 2]
    send_ref, keep_ref, both = refs[-3:]
    for part_ref, whole_ref in zip(refs[slots + 2 : slots + 2 + earlier], (send_ref, keep_ref)):
        whole_ref[:, : span[0]] = part_ref[...]
    block = slot_refs[0].shape[0]
    total = block * slots
    for b in range(slots):
        high, low = split(slot_refs[b][...])
        row = pl.multiple_of(place_ref[b] * block, block)
        both[pl.ds(row, block), :] = high
        both[pl.ds(total + row, block), :] = low

    width = divisor(span[1], *((512,) if streamed else ()), 256, 128)

    @pl.loop(0, span[1] // width, unroll=1 if streamed else 2)
    def _(step):
        at = pl.ds(pl.multiple_of(span[0] + step * width, width), width)
        tile = pl.ds(pl.multiple_of(step * width, width), width)
        tile = (slice(None), tile) if contract == 0 else (tile, slice(None))
        part = three_pass(both, high_ref[tile], low_ref[tile], contract, streamed)
        keep_ref[:, at] = part[: total // 2]
        send_ref[:, at] = part[total // 2 :]


def forward(blocks, weight, place, by_column, streamed, span, earlier, after):
    slots, (block, depth) = len(blocks), blocks[0].shape
    half = block * slots // 2
    out = jax.ShapeDtypeStruct((half, sum(span)), jnp.float32)
    inside = pl.BlockSpec(memory_space=pltpu.VMEM)
    return pl.pallas_call(
        functools.partial(forward_kernel, slots, 0 if by_column else 1, streamed, span, len(earlier)),
        out_shape=(out, out),
        in_specs=[pl.BlockSpec(memory_space=pltpu.SMEM)]
        + [inside] * (slots + 2 + len(earlier))
        + [pl.BlockSpec(memory_space=pl.ANY)] * len(after),
        out_specs=[inside] * 2,
        scratch_shapes=[pltpu.VMEM((2 * block * slots, depth), jnp.bfloat16)],
        compiler_params=pltpu.CompilerParams(vmem_limit_bytes=VMEM_LIMIT),
        cost_estimate=SHORT,
    )(place, *blocks, *[pltpu.with_memory_space_constraint(part, pltpu.VMEM) for part in weight], *earlier, *after)


def stream_kernel(slots, first_column, depth, place_ref, *refs):
    slot_refs, weight_ref = refs[:slots], refs[slots]
    send_ref, keep_ref, high_ref, low_ref, both, landed, arrived = refs[-7:]
    block = slot_refs[0].shape[0]
    total = block * slots
    width = landed.shape[2]
    steps = send_ref.shape[1] // width

    def fetch(step):
        start = pl.multiple_of(first_column + step * width, width)
        slot = lax.rem(step, depth)
        return pltpu.make_async_copy(weight_ref.at[:, pl.ds(start, width)], landed.at[slot], arrived.at[slot])

    for step in range(min(depth, steps)):
        fetch(step).start()
    for b in range(slots):
        high, low = split(slot_refs[b][...])
        row = pl.multiple_of(place_ref[b] * block, block)
        both[pl.ds(row, block), :] = high
        both[pl.ds(total + row, block), :] = low

    @pl.loop(0, steps)
    def _(step):
        fetch(step).wait()
        high, low = split(landed[lax.rem(step, depth)])
        at = pl.ds(pl.multiple_of(step * width, width), width)
        high_ref[:, at] = high
        low_ref[:, at] = low
        part = three_pass(both, high, low, 0, False)
        keep_ref[:, at] = part[: total // 2]
        send_ref[:, at] = part[total // 2 :]

        @pl.when(step + depth < steps)
        def _():
            fetch(step + depth).start()


def stream(blocks, weight, place, columns, after):
    slots, (block, rows) = len(blocks), blocks[0].shape
    half, hidden = block * slots // 2, columns[1]
    width = divisor(hidden, 256, 128)
    depth = 3
    out = jax.ShapeDtypeStruct((half, hidden), jnp.float32)
    kept = pltpu.VMEM((rows, hidden), jnp.bfloat16)
    inside = pl.BlockSpec(memory_space=pltpu.VMEM)
    result = pl.pallas_call(
        functools.partial(stream_kernel, slots, columns[0], depth),
        out_shape=(out, out, kept, kept),
        in_specs=[pl.BlockSpec(memory_space=pltpu.SMEM)]
        + [inside] * slots
        + [pl.BlockSpec(memory_space=pl.ANY)] * (1 + len(after)),
        out_specs=[inside] * 4,
        scratch_shapes=[
            pltpu.VMEM((2 * block * slots, rows), jnp.bfloat16),
            pltpu.VMEM((depth, rows, width), jnp.float32),
            pltpu.SemaphoreType.DMA((depth,)),
        ],
        compiler_params=pltpu.CompilerParams(vmem_limit_bytes=2 * VMEM_LIMIT),
        cost_estimate=SHORT,
    )(place, *blocks, pltpu.with_memory_space_constraint(weight, pltpu.HBM), *after)
    return result[:2], result[2:]


def backward_kernel(slots, earlier, first_column, streamed, place_ref, *refs):
    act_refs, (high_ref, low_ref) = refs[:slots], refs[slots : slots + 2]
    earlier_refs = refs[slots + 2 : slots + 2 + earlier]
    out_refs = refs[-2 - slots : -2]
    both, result = refs[-2:]
    block = act_refs[0].shape[0]
    total = block * slots
    for p in range(slots):
        high, low = split(act_refs[p][...])
        both[p * block : (p + 1) * block, :] = high
        both[total + p * block : total + (p + 1) * block, :] = low

    depth = out_refs[0].shape[1]
    width = result.shape[1]

    @pl.loop(0, depth // width)
    def _(step):
        start = pl.multiple_of(step * width, width)
        tile = (pl.ds(pl.multiple_of(first_column + start, width), width), slice(None))
        result[...] = three_pass(both, high_ref[tile], low_ref[tile], 1, streamed)
        for b in range(slots):
            row = pl.multiple_of(place_ref[b] * block, block)
            rows = result[pl.ds(row, block), :]
            if earlier:
                rows = rows + earlier_refs[b][:, pl.ds(pl.multiple_of(first_column + start, width), width)]
            out_refs[b][:, pl.ds(start, width)] = rows


def backward(acts, weight, place, earlier, part, parts, streamed, after):
    slots, (block, hidden) = len(acts), acts[0].shape
    depth = weight[0].shape[0] // parts
    width = divisor(depth, 256, 128)
    out = jax.ShapeDtypeStruct((block, depth), jnp.float32)
    inside = pl.BlockSpec(memory_space=pltpu.VMEM)
    return pl.pallas_call(
        functools.partial(backward_kernel, slots, len(earlier), part * depth, streamed),
        out_shape=[out] * slots,
        in_specs=[pl.BlockSpec(memory_space=pltpu.SMEM)]
        + [inside] * (slots + 2 + len(earlier))
        + [pl.BlockSpec(memory_space=pl.ANY)] * len(after),
        out_specs=[inside] * slots,
        scratch_shapes=[
            pltpu.VMEM((2 * block * slots, hidden), jnp.bfloat16),
            pltpu.VMEM((block * slots, width), jnp.float32),
        ],
        compiler_params=pltpu.CompilerParams(vmem_limit_bytes=VMEM_LIMIT),
        cost_estimate=SHORT,
    )(place, *acts, *[pltpu.with_memory_space_constraint(part, pltpu.VMEM) for part in weight], *earlier, *after)


def body(hid_size, emb_size, inputs, out_grad, in_weight, in_bias, out_weight, norm_gain):
    chips = emb_size // 2
    tokens, depth = inputs.shape
    model_width = depth * emb_size
    hidden = in_weight.shape[1]
    me = lax.axis_index("emb")
    chip, core = me // 2, me % 2

    def along_hid(values, steps=1):
        return lax.ppermute(values, "hid", [(i, (i + steps) % hid_size) for i in range(hid_size)])

    def other_core(values):
        return lax.ppermute(values, "emb", [(i, i ^ 1) for i in range(emb_size)])

    def next_chip(values):
        return lax.ppermute(values, "emb", [(i, (i + 2) % emb_size) for i in range(emb_size)])

    owner = jnp.arange(emb_size, dtype=jnp.int32)
    place = ((owner % 2) ^ core) * chips + (owner // 2 - chip) % chips

    def gathered(values):
        return [values] + [along_hid(values, step) for step in range(1, hid_size)]

    grads = gathered(out_grad)
    piece = hidden // CHUNKS

    moments = call(moments_kernel, jax.ShapeDtypeStruct((2 * tokens, 128), jnp.float32), (inputs,), ())
    quarter = piece // 2
    out_parts = [prepare(out_weight, (0, quarter), (0, depth), [place, moments])]
    moments = call(
        functools.partial(merge_kernel, depth), moments, (moments, other_core(moments)), (out_parts[0][0],)
    )
    for c in range(1, 4):
        out_parts.append(prepare(out_weight, (c * quarter, quarter), (0, depth), [moments, out_parts[-1][0]]))
    parts = [moments]
    for _ in range(1, chips):
        parts.append(next_chip(parts[-1]))
    normed, scaled, inv_std = call(
        functools.partial(normalise_kernel, 2 * depth),
        (inputs, inputs, jax.ShapeDtypeStruct((tokens, 128), jnp.float32)),
        (inputs, norm_gain[None, :], *parts),
        (out_parts[-1][0],),
    )
    inv_std = inv_std[:, :1]
    scaled = gathered(scaled)

    def halved(partial):
        send, keep = partial
        return keep + other_core(send)

    def exchanged(summed):
        terms = [summed[d * tokens : (d + 1) * tokens] for d in range(chips)]
        arrival = next_chip(terms[chips - 1])
        for step in range(2, chips):
            arrival = next_chip(arrival + terms[chips - step])
        return arrival, terms[0]

    def back(c, streamed, earlier, after):
        span = (c % 2 * quarter, quarter)
        return forward(grads, out_parts[c], place, False, streamed, span, earlier, after)

    near, far = [scaled[1], scaled[-1]], scaled[2 : hid_size - 1]
    back_0 = back(0, True, (), [scaled[0]])
    back_0 = back(1, False, back_0, [])
    half_0 = halved(back_0)
    back_1 = back(2, True, (), [back_0[1], *near])
    back_1 = back(3, False, back_1, far)
    half_1 = halved(back_1)
    back_0, back_1 = exchanged(half_0), exchanged(half_1)
    pre_0, in_parts_0 = stream(scaled, in_weight, place, (0, piece), [half_0, half_1])
    pre_1, in_parts_1 = stream(scaled, in_weight, place, (piece, piece), [pre_0[1], back_0[0]])
    backs = [back_0, back_1]
    pres = [exchanged(halved(pre_0)), exchanged(halved(pre_1))]

    def spread_out(c):
        act = sum(backs[c]) * gelu_slope(sum(pres[c]) + in_bias[c * piece : (c + 1) * piece])
        mine = [None] * chips
        mine[0] = act
        for step in range(1, chips):
            act = next_chip(act)
            mine[(chips - step) % chips] = act
        return mine + [other_core(block) for block in mine]

    def summed_along_hid(sums):
        return sum([along_hid(sums[step], -step) for step in range(1, hid_size)], start=sums[0])

    acts_0, acts_1 = spread_out(0), spread_out(1)
    sums = backward(acts_0, in_parts_0, place, (), 0, 1, True, [pre_1[1]])
    parts = 2 if depth % 512 == 0 else 1
    ends = []
    for part in range(parts):
        ends.append(backward(acts_1, in_parts_1, place, sums, part, parts, False, [ends[-1][0] if ends else sums[0]]))
    running = jnp.concatenate([summed_along_hid(end) for end in ends], axis=1)
    normed_grad = running * norm_gain
    totals = lax.psum(
        jnp.stack([jnp.sum(normed_grad, axis=-1), jnp.sum(normed_grad * normed, axis=-1)]), "emb"
    )
    first, second = (totals / model_width)[:, :, None]
    return inv_std * (normed_grad - first - normed * second)


def solution(mesh):
    hid_size, emb_size = mesh.shape["hid"], mesh.shape["emb"]
    assert hid_size == emb_size and emb_size % 2 == 0
    return jax.shard_map(
        functools.partial(body, hid_size, emb_size),
        mesh=mesh,
        in_specs=(
            P(("groups", "hid"), "emb"),
            P(("groups", "hid"), "emb"),
            P("emb", "hid"),
            P("hid"),
            P("hid", "emb"),
            P("emb"),
        ),
        out_specs=P(("groups", "hid"), "emb"),
        check_vma=False,
    )
```

```python
import functools
import math

import jax
import jax.numpy as jnp
from jax import lax
from jax.experimental import pallas as pl
from jax.experimental.pallas import tpu as pltpu
from jax.sharding import PartitionSpec as P

VMEM_LIMIT = 5 * 1024 * 1024
CHUNKS = 2
SHORT = pl.CostEstimate(flops=1 << 20, bytes_accessed=1 << 18, transcendentals=0)


def gelu_slope(values):
    cdf = 0.5 * (1.0 + lax.erf(values * (1.0 / math.sqrt(2.0))))
    density = jnp.exp(-0.5 * values * values) * (1.0 / math.sqrt(2.0 * math.pi))
    return cdf + values * density


def split(values):
    high = values.astype(jnp.bfloat16)
    return high, (values - high.astype(jnp.float32)).astype(jnp.bfloat16)


def divisor(extent, *choices):
    return next(c for c in choices if extent % c == 0)


def call(kernel, out_shape, operands, after):
    outs = out_shape if isinstance(out_shape, tuple) else (out_shape,)

    def run(*refs):
        kernel(*refs[: len(operands)], *refs[len(operands) + len(after) :])

    inside = pl.BlockSpec(memory_space=pltpu.VMEM)
    result = pl.pallas_call(
        run,
        out_shape=tuple(jax.ShapeDtypeStruct(o.shape, o.dtype) for o in outs),
        in_specs=[inside] * len(operands) + [pl.BlockSpec(memory_space=pl.ANY)] * len(after),
        out_specs=[inside] * len(outs),
        compiler_params=pltpu.CompilerParams(vmem_limit_bytes=VMEM_LIMIT),
        cost_estimate=SHORT,
    )(*operands, *after)
    return result if isinstance(out_shape, tuple) else result[0]


def moments_kernel(inputs_ref, out_ref):
    rows, depth = inputs_ref.shape
    mean = jnp.sum(inputs_ref[...], axis=1, keepdims=True) * (1.0 / depth)
    square = jnp.sum(jnp.square(inputs_ref[...] - mean), axis=1, keepdims=True)
    out_ref[:rows] = jnp.broadcast_to(mean, (rows, 128))
    out_ref[rows:] = jnp.broadcast_to(square, (rows, 128))


def merge(moments, count):
    rows = moments[0].shape[0] // 2
    mean = sum(part[:rows] for part in moments) * (1.0 / len(moments))
    square = sum(part[rows:] + count * jnp.square(part[:rows] - mean) for part in moments)
    return mean, square


def merge_kernel(count, first_ref, second_ref, out_ref):
    rows = out_ref.shape[0] // 2
    out_ref[:rows], out_ref[rows:] = merge((first_ref[...], second_ref[...]), count)


def normalise_kernel(count, inputs_ref, gain_ref, *refs):
    *moment_refs, normed_ref, scaled_ref, inv_std_ref = refs
    mean, square = merge([ref[...] for ref in moment_refs], count)
    inv_std = 1.0 / jnp.sqrt(square * (1.0 / (count * len(moment_refs))) + 1e-06)
    normed = (inputs_ref[...] - mean[:, :1]) * inv_std[:, :1]
    normed_ref[...] = normed
    scaled_ref[...] = normed * gain_ref[...]
    inv_std_ref[...] = inv_std


def prepare_kernel(rows, columns, block, depth, weight_ref, *refs):
    high_ref, low_ref, landed, arrived = refs[-4:]
    steps = rows[1] // block

    def fetch(step):
        start = pl.multiple_of(rows[0] + step * block, block)
        slot = lax.rem(step, depth)
        return pltpu.make_async_copy(
            weight_ref.at[pl.ds(start, block), pl.ds(*columns)], landed.at[slot], arrived.at[slot]
        )

    for step in range(min(depth, steps)):
        fetch(step).start()

    @pl.loop(0, steps)
    def _(step):
        fetch(step).wait()
        high, low = split(landed[lax.rem(step, depth)])
        at = pl.ds(pl.multiple_of(step * block, block), block)
        high_ref[at, :] = high
        low_ref[at, :] = low

        @pl.when(step + depth < steps)
        def _():
            fetch(step + depth).start()


def prepare(weight, rows, columns, after):
    block = 128 * 1536 // columns[1]
    block = divisor(rows[1], *[b for b in (256, 128, 64, 32) if b <= max(block, 32)])
    depth = 4
    out = pltpu.VMEM((rows[1], columns[1]), jnp.bfloat16)
    return pl.pallas_call(
        functools.partial(prepare_kernel, rows, columns, block, depth),
        out_shape=(out, out),
        in_specs=[pl.BlockSpec(memory_space=pl.ANY)] * (1 + len(after)),
        out_specs=[pl.BlockSpec(memory_space=pltpu.VMEM)] * 2,
        scratch_shapes=[
            pltpu.VMEM((depth, block, columns[1]), jnp.float32),
            pltpu.SemaphoreType.DMA((depth,)),
        ],
        compiler_params=pltpu.CompilerParams(vmem_limit_bytes=VMEM_LIMIT),
        cost_estimate=SHORT,
    )(pltpu.with_memory_space_constraint(weight, pltpu.HBM), *after)


def three_pass(both, high, low, contract, streamed):
    rows = both.shape[0] // 2
    dims = ((contract,), (1,)) if streamed else ((1,), (contract,))

    def dot(left, weight):
        pair = (weight, left) if streamed else (left, weight)
        return lax.dot_general(*pair, (dims, ((), ())), preferred_element_type=jnp.float32)

    first, second = dot(both[...], high), dot(both[:rows, :], low)
    if streamed:
        return (first[:, :rows] + first[:, rows:] + second).T
    return first[:rows] + first[rows:] + second


def forward_kernel(slots, contract, streamed, span, earlier, place_ref, *refs):
    slot_refs, (high_ref, low_ref) = refs[:slots], refs[slots : slots + 2]
    send_ref, keep_ref, both = refs[-3:]
    for part_ref, whole_ref in zip(refs[slots + 2 : slots + 2 + earlier], (send_ref, keep_ref)):
        whole_ref[:, : span[0]] = part_ref[...]
    block = slot_refs[0].shape[0]
    total = block * slots
    for b in range(slots):
        high, low = split(slot_refs[b][...])
        row = pl.multiple_of(place_ref[b] * block, block)
        both[pl.ds(row, block), :] = high
        both[pl.ds(total + row, block), :] = low

    width = divisor(span[1], *((512,) if streamed else ()), 256, 128)

    @pl.loop(0, span[1] // width, unroll=1 if streamed else 2)
    def _(step):
        at = pl.ds(pl.multiple_of(span[0] + step * width, width), width)
        tile = pl.ds(pl.multiple_of(step * width, width), width)
        tile = (slice(None), tile) if contract == 0 else (tile, slice(None))
        part = three_pass(both, high_ref[tile], low_ref[tile], contract, streamed)
        keep_ref[:, at] = part[: total // 2]
        send_ref[:, at] = part[total // 2 :]


def forward(blocks, weight, place, by_column, streamed, span, earlier, after):
    slots, (block, depth) = len(blocks), blocks[0].shape
    half = block * slots // 2
    out = jax.ShapeDtypeStruct((half, sum(span)), jnp.float32)
    inside = pl.BlockSpec(memory_space=pltpu.VMEM)
    return pl.pallas_call(
        functools.partial(forward_kernel, slots, 0 if by_column else 1, streamed, span, len(earlier)),
        out_shape=(out, out),
        in_specs=[pl.BlockSpec(memory_space=pltpu.SMEM)]
        + [inside] * (slots + 2 + len(earlier))
        + [pl.BlockSpec(memory_space=pl.ANY)] * len(after),
        out_specs=[inside] * 2,
        scratch_shapes=[pltpu.VMEM((2 * block * slots, depth), jnp.bfloat16)],
        compiler_params=pltpu.CompilerParams(vmem_limit_bytes=VMEM_LIMIT),
        cost_estimate=SHORT,
    )(place, *blocks, *[pltpu.with_memory_space_constraint(part, pltpu.VMEM) for part in weight], *earlier, *after)


def stream_kernel(slots, first_column, span, earlier, depth, place_ref, *refs):
    slot_refs, weight_ref = refs[:slots], refs[slots]
    send_ref, keep_ref, high_ref, low_ref, both, landed, arrived = refs[-7:]
    for part_ref, whole_ref in zip(refs[slots + 1 : slots + 1 + earlier], (send_ref, keep_ref)):
        whole_ref[:, : span[0]] = part_ref[...]
    block = slot_refs[0].shape[0]
    total = block * slots
    width = landed.shape[2]
    steps = span[1] // width

    def fetch(step):
        start = pl.multiple_of(first_column + step * width, width)
        slot = lax.rem(step, depth)
        return pltpu.make_async_copy(weight_ref.at[:, pl.ds(start, width)], landed.at[slot], arrived.at[slot])

    for step in range(min(depth, steps)):
        fetch(step).start()
    for b in range(slots):
        high, low = split(slot_refs[b][...])
        row = pl.multiple_of(place_ref[b] * block, block)
        both[pl.ds(row, block), :] = high
        both[pl.ds(total + row, block), :] = low

    @pl.loop(0, steps)
    def _(step):
        fetch(step).wait()
        high, low = split(landed[lax.rem(step, depth)])
        at = pl.ds(pl.multiple_of(step * width, width), width)
        high_ref[:, at] = high
        low_ref[:, at] = low
        part = three_pass(both, high, low, 0, False)
        at = pl.ds(pl.multiple_of(span[0] + step * width, width), width)
        keep_ref[:, at] = part[: total // 2]
        send_ref[:, at] = part[total // 2 :]

        @pl.when(step + depth < steps)
        def _():
            fetch(step + depth).start()


def stream(blocks, weight, place, first_column, span, earlier, after):
    slots, (block, rows) = len(blocks), blocks[0].shape
    half, hidden = block * slots // 2, sum(span)
    width = divisor(span[1], 256, 128)
    depth = 3
    out = jax.ShapeDtypeStruct((half, hidden), jnp.float32)
    kept = pltpu.VMEM((rows, span[1]), jnp.bfloat16)
    inside = pl.BlockSpec(memory_space=pltpu.VMEM)
    result = pl.pallas_call(
        functools.partial(stream_kernel, slots, first_column, span, len(earlier), depth),
        out_shape=(out, out, kept, kept),
        in_specs=[pl.BlockSpec(memory_space=pltpu.SMEM)]
        + [inside] * slots
        + [pl.BlockSpec(memory_space=pl.ANY)]
        + [inside] * len(earlier)
        + [pl.BlockSpec(memory_space=pl.ANY)] * len(after),
        out_specs=[inside] * 4,
        scratch_shapes=[
            pltpu.VMEM((2 * block * slots, rows), jnp.bfloat16),
            pltpu.VMEM((depth, rows, width), jnp.float32),
            pltpu.SemaphoreType.DMA((depth,)),
        ],
        compiler_params=pltpu.CompilerParams(vmem_limit_bytes=2 * VMEM_LIMIT),
        cost_estimate=SHORT,
    )(place, *blocks, pltpu.with_memory_space_constraint(weight, pltpu.HBM), *earlier, *after)
    return result[:2], result[2:]


def backward_kernel(slots, pieces, earlier, first_column, place_ref, *refs):
    act_refs, weight_refs = refs[:slots], refs[slots : slots + 2 * pieces]
    earlier_refs = refs[slots + 2 * pieces : slots + 2 * pieces + earlier]
    out_refs = refs[-2 - slots : -2]
    both, result = refs[-2:]
    block = act_refs[0].shape[0]
    total = block * slots
    for p in range(slots):
        high, low = split(act_refs[p][...])
        both[p * block : (p + 1) * block, :] = high
        both[total + p * block : total + (p + 1) * block, :] = low

    depth = out_refs[0].shape[1]
    width = result.shape[1]

    @pl.loop(0, depth // width)
    def _(step):
        start = pl.multiple_of(step * width, width)
        tile = (pl.ds(pl.multiple_of(first_column + start, width), width), slice(None))
        total_sum, column = 0.0, 0
        for high_ref, low_ref in zip(weight_refs[::2], weight_refs[1::2]):
            columns = slice(column, column + high_ref.shape[1])
            total_sum += three_pass(both[:, columns], high_ref[tile], low_ref[tile], 1, False)
            column = columns.stop
        result[...] = total_sum
        for b in range(slots):
            row = pl.multiple_of(place_ref[b] * block, block)
            rows = result[pl.ds(row, block), :]
            if earlier:
                rows = rows + earlier_refs[b][:, pl.ds(pl.multiple_of(first_column + start, width), width)]
            out_refs[b][:, pl.ds(start, width)] = rows


def backward(acts, weights, place, earlier, part, parts, after):
    slots, (block, hidden) = len(acts), acts[0].shape
    depth = weights[0].shape[0] // parts
    width = divisor(depth, 256, 128)
    out = jax.ShapeDtypeStruct((block, depth), jnp.float32)
    inside = pl.BlockSpec(memory_space=pltpu.VMEM)
    return pl.pallas_call(
        functools.partial(backward_kernel, slots, len(weights) // 2, len(earlier), part * depth),
        out_shape=[out] * slots,
        in_specs=[pl.BlockSpec(memory_space=pltpu.SMEM)]
        + [inside] * (slots + len(weights) + len(earlier))
        + [pl.BlockSpec(memory_space=pl.ANY)] * len(after),
        out_specs=[inside] * slots,
        scratch_shapes=[
            pltpu.VMEM((2 * block * slots, hidden), jnp.bfloat16),
            pltpu.VMEM((block * slots, width), jnp.float32),
        ],
        compiler_params=pltpu.CompilerParams(vmem_limit_bytes=VMEM_LIMIT),
        cost_estimate=SHORT,
    )(place, *acts, *[pltpu.with_memory_space_constraint(part, pltpu.VMEM) for part in weights], *earlier, *after)


def body(hid_size, emb_size, inputs, out_grad, in_weight, in_bias, out_weight, norm_gain):
    chips = emb_size // 2
    tokens, depth = inputs.shape
    model_width = depth * emb_size
    hidden = in_weight.shape[1]
    me = lax.axis_index("emb")
    chip, core = me // 2, me % 2

    def along_hid(values, steps=1):
        return lax.ppermute(values, "hid", [(i, (i + steps) % hid_size) for i in range(hid_size)])

    def other_core(values):
        return lax.ppermute(values, "emb", [(i, i ^ 1) for i in range(emb_size)])

    def next_chip(values):
        return lax.ppermute(values, "emb", [(i, (i + 2) % emb_size) for i in range(emb_size)])

    owner = jnp.arange(emb_size, dtype=jnp.int32)
    place = ((owner % 2) ^ core) * chips + (owner // 2 - chip) % chips

    def gathered(values):
        return [values] + [along_hid(values, step) for step in range(1, hid_size)]

    grads = gathered(out_grad)
    piece = hidden // CHUNKS

    def tied(values, others):
        return lax.optimization_barrier((values, others))

    def halved(partial, behind=()):
        send, keep = partial
        return keep + tied(other_core(send), behind)[0]

    def exchanged(summed):
        terms = [summed[d * tokens : (d + 1) * tokens] for d in range(chips)]
        arrival = next_chip(terms[chips - 1])
        for step in range(2, chips):
            arrival = next_chip(arrival + terms[chips - step])
        return arrival, terms[0]

    def prepared(c, after):
        return prepare(out_weight, (c * quarter, quarter), (0, depth), after)

    def back(c, earlier, after):
        return forward(grads, out_parts[c], place, False, False, (c % 2 * quarter, quarter), earlier, after)

    quarter = piece // 2
    moments = call(moments_kernel, jax.ShapeDtypeStruct((2 * tokens, 128), jnp.float32), (inputs,), ())
    out_parts = [prepared(0, [place, moments])]
    out_parts.append(prepared(1, [out_parts[0][0]]))
    out_parts.append(prepared(2, [out_parts[1][0]]))
    back_0 = back(0, (), [out_parts[2][0]])
    moments = call(functools.partial(merge_kernel, depth), moments, (moments, other_core(moments)), (back_0[0],))
    back_0 = back(1, back_0, [moments])
    parts = [moments]
    for _ in range(1, chips):
        parts.append(next_chip(parts[-1]))
    normed, scaled, inv_std = call(
        functools.partial(normalise_kernel, 2 * depth),
        (inputs, inputs, jax.ShapeDtypeStruct((tokens, 128), jnp.float32)),
        (inputs, norm_gain[None, :], *parts),
        (back_0[1],),
    )
    inv_std = inv_std[:, :1]
    scaled = gathered(scaled)
    back_0, _ = tied(back_0, parts)
    out_parts.append(prepared(3, [scaled[0]]))
    half_0 = halved(back_0, (out_parts[3], scaled[1], scaled[-1]))
    back_1 = back(2, (), [out_parts[3][0], half_0])
    back_1 = back(3, back_1, [scaled[1], scaled[-1]])
    back_0 = exchanged(half_0)
    back_1, (back_0, scaled[2:-1]) = tied(back_1, (back_0, scaled[2:-1]))

    def pre(c, earlier, after):
        span = (c % 2 * quarter, quarter)
        return stream(scaled, in_weight, place, c * quarter, span, earlier, after)

    pre_0, in_parts_0 = pre(0, (), [back_1[1]])
    half_1 = halved(back_1, pre_0)
    back_1 = exchanged(half_1)
    pre_0, in_parts_1 = pre(1, pre_0, [half_1])
    pre_1, in_parts_2 = pre(2, (), [pre_0[1]])
    half_0 = halved(pre_0, pre_1)
    pre_1, in_parts_3 = pre(3, pre_1, [half_0])
    pre_1, back_1 = tied(pre_1, back_1)
    backs = [back_0, back_1]
    pres = [exchanged(half_0), exchanged(halved(pre_1))]

    def spread_out(c):
        act = sum(backs[c]) * gelu_slope(sum(pres[c]) + in_bias[c * piece : (c + 1) * piece])
        mine = [None] * chips
        mine[0] = act
        for step in range(1, chips):
            act = next_chip(act)
            mine[(chips - step) % chips] = act
        return mine

    def both_cores(mine):
        return mine + [other_core(block) for block in mine]

    def summed_along_hid(sums):
        return sum([along_hid(sums[step], -step) for step in range(1, hid_size)], start=sums[0])

    acts_0, acts_1 = spread_out(0), spread_out(1)
    sums = backward(both_cores(acts_0), in_parts_0 + in_parts_1, place, (), 0, 1, [pre_1[1]])
    acts_1[1:], sums = tied(acts_1[1:], sums)
    acts_1, in_parts_1 = both_cores(acts_1), in_parts_2 + in_parts_3
    parts = 2 if depth % 512 == 0 else 1
    ends = []
    for part in range(parts):
        ends.append(backward(acts_1, in_parts_1, place, sums, part, parts, [ends[-1][0] if ends else sums[0]]))
    running = jnp.concatenate([summed_along_hid(end) for end in ends], axis=1)
    normed_grad = running * norm_gain
    totals = lax.psum(
        jnp.stack([jnp.sum(normed_grad, axis=-1), jnp.sum(normed_grad * normed, axis=-1)]), "emb"
    )
    first, second = (totals / model_width)[:, :, None]
    return inv_std * (normed_grad - first - normed * second)


def solution(mesh):
    hid_size, emb_size = mesh.shape["hid"], mesh.shape["emb"]
    assert hid_size == emb_size and emb_size % 2 == 0
    return jax.shard_map(
        functools.partial(body, hid_size, emb_size),
        mesh=mesh,
        in_specs=(
            P(("groups", "hid"), "emb"),
            P(("groups", "hid"), "emb"),
            P("emb", "hid"),
            P("hid"),
            P("hid", "emb"),
            P("emb"),
        ),
        out_specs=P(("groups", "hid"), "emb"),
        check_vma=False,
    )
```

```python
import functools
import math

import jax
import jax.numpy as jnp
from jax import lax
from jax.experimental import pallas as pl
from jax.experimental.pallas import tpu as pltpu
from jax.sharding import PartitionSpec as P

VMEM_LIMIT = 5 * 1024 * 1024
CHUNKS = 2
SHORT = pl.CostEstimate(flops=1 << 20, bytes_accessed=1 << 18, transcendentals=0)


def gelu_slope(values):
    cdf = 0.5 * (1.0 + lax.erf(values * (1.0 / math.sqrt(2.0))))
    density = jnp.exp(-0.5 * values * values) * (1.0 / math.sqrt(2.0 * math.pi))
    return cdf + values * density


def split(values):
    high = values.astype(jnp.bfloat16)
    return high, (values - high.astype(jnp.float32)).astype(jnp.bfloat16)


def divisor(extent, *choices):
    return next(c for c in choices if extent % c == 0)


def call(kernel, out_shape, operands, after):
    outs = out_shape if isinstance(out_shape, tuple) else (out_shape,)

    def run(*refs):
        kernel(*refs[: len(operands)], *refs[len(operands) + len(after) :])

    inside = pl.BlockSpec(memory_space=pltpu.VMEM)
    result = pl.pallas_call(
        run,
        out_shape=tuple(jax.ShapeDtypeStruct(o.shape, o.dtype) for o in outs),
        in_specs=[inside] * len(operands) + [pl.BlockSpec(memory_space=pl.ANY)] * len(after),
        out_specs=[inside] * len(outs),
        compiler_params=pltpu.CompilerParams(vmem_limit_bytes=VMEM_LIMIT),
        cost_estimate=SHORT,
    )(*operands, *after)
    return result if isinstance(out_shape, tuple) else result[0]


def moments_kernel(inputs_ref, out_ref):
    rows, depth = inputs_ref.shape
    mean = jnp.sum(inputs_ref[...], axis=1, keepdims=True) * (1.0 / depth)
    square = jnp.sum(jnp.square(inputs_ref[...] - mean), axis=1, keepdims=True)
    out_ref[:rows] = jnp.broadcast_to(mean, (rows, 128))
    out_ref[rows:] = jnp.broadcast_to(square, (rows, 128))


def merge(moments, count):
    rows = moments[0].shape[0] // 2
    mean = sum(part[:rows] for part in moments) * (1.0 / len(moments))
    square = sum(part[rows:] + count * jnp.square(part[:rows] - mean) for part in moments)
    return mean, square


def merge_kernel(count, first_ref, second_ref, out_ref):
    rows = out_ref.shape[0] // 2
    out_ref[:rows], out_ref[rows:] = merge((first_ref[...], second_ref[...]), count)


def normalise_kernel(count, inputs_ref, gain_ref, *refs):
    *moment_refs, normed_ref, scaled_ref, inv_std_ref = refs
    mean, square = merge([ref[...] for ref in moment_refs], count)
    inv_std = 1.0 / jnp.sqrt(square * (1.0 / (count * len(moment_refs))) + 1e-06)
    normed = (inputs_ref[...] - mean[:, :1]) * inv_std[:, :1]
    normed_ref[...] = normed
    scaled_ref[...] = normed * gain_ref[...]
    inv_std_ref[...] = inv_std


def prepare_kernel(rows, columns, block, depth, weight_ref, *refs):
    high_ref, low_ref, landed, arrived = refs[-4:]
    steps = rows[1] // block

    def fetch(step):
        start = pl.multiple_of(rows[0] + step * block, block)
        slot = lax.rem(step, depth)
        return pltpu.make_async_copy(
            weight_ref.at[pl.ds(start, block), pl.ds(*columns)], landed.at[slot], arrived.at[slot]
        )

    for step in range(min(depth, steps)):
        fetch(step).start()

    @pl.loop(0, steps)
    def _(step):
        fetch(step).wait()
        high, low = split(landed[lax.rem(step, depth)])
        at = pl.ds(pl.multiple_of(step * block, block), block)
        high_ref[at, :] = high
        low_ref[at, :] = low

        @pl.when(step + depth < steps)
        def _():
            fetch(step + depth).start()


def prepare(weight, rows, columns, after):
    block = 128 * 1536 // columns[1]
    block = divisor(rows[1], *[b for b in (256, 128, 64, 32) if b <= max(block, 32)])
    depth = 4
    out = pltpu.VMEM((rows[1], columns[1]), jnp.bfloat16)
    return pl.pallas_call(
        functools.partial(prepare_kernel, rows, columns, block, depth),
        out_shape=(out, out),
        in_specs=[pl.BlockSpec(memory_space=pl.ANY)] * (1 + len(after)),
        out_specs=[pl.BlockSpec(memory_space=pltpu.VMEM)] * 2,
        scratch_shapes=[
            pltpu.VMEM((depth, block, columns[1]), jnp.float32),
            pltpu.SemaphoreType.DMA((depth,)),
        ],
        compiler_params=pltpu.CompilerParams(vmem_limit_bytes=VMEM_LIMIT),
        cost_estimate=SHORT,
    )(pltpu.with_memory_space_constraint(weight, pltpu.HBM), *after)


def three_pass(both, high, low, contract):
    rows = both.shape[0] // 2
    dot = functools.partial(
        lax.dot_general,
        dimension_numbers=(((1,), (contract,)), ((), ())),
        preferred_element_type=jnp.float32,
    )
    first = dot(both[...], high)
    return first[:rows] + first[rows:] + dot(both[:rows, :], low)


def fill(both, block_refs, place_ref):
    total = both.shape[0] // 2
    block = total // place_ref.shape[0]
    index = 0
    for ref in block_refs:
        for start in range(0, ref.shape[0], block):
            high, low = split(ref[start : start + block, :])
            row = pl.multiple_of(place_ref[index] * block, block)
            both[pl.ds(row, block), :] = high
            both[pl.ds(total + row, block), :] = low
            index += 1


def follow(earlier_refs, out_refs):
    for earlier_ref, out_ref in zip(earlier_refs, out_refs):
        out_ref[:, : earlier_ref.shape[1]] = earlier_ref[...]
    return earlier_refs[0].shape[1] if earlier_refs else 0


def forward_kernel(place_ref, slot_refs, weight_refs, earlier_refs, send_ref, keep_ref, both):
    fill(both, slot_refs, place_ref)
    half, column = send_ref.shape[0], follow(earlier_refs, (send_ref, keep_ref))
    for high_ref, low_ref in zip(weight_refs[::2], weight_refs[1::2]):
        width = divisor(high_ref.shape[1], 256, 128)

        @pl.loop(0, high_ref.shape[1] // width, unroll=2)
        def _(step):
            at = pl.ds(pl.multiple_of(step * width, width), width)
            part = three_pass(both, high_ref[:, at], low_ref[:, at], 0)
            at = pl.ds(pl.multiple_of(column + step * width, width), width)
            keep_ref[:, at] = part[:half]
            send_ref[:, at] = part[half:]

        column += high_ref.shape[1]


def forward(slots, weights, place, earlier, after):
    tokens, depth = slots[0].shape[0] * len(slots), slots[0].shape[1]
    hidden = sum(w.shape[1] for w in weights[::2]) + (earlier[0].shape[1] if earlier else 0)
    out = jax.ShapeDtypeStruct((tokens // 2, hidden), jnp.float32)
    inside, anywhere = pl.BlockSpec(memory_space=pltpu.VMEM), pl.BlockSpec(memory_space=pl.ANY)
    ends = [1 + len(slots), 1 + len(slots) + len(weights), 1 + len(slots) + len(weights) + len(earlier)]
    return pl.pallas_call(
        lambda *refs: forward_kernel(
            refs[0], refs[1 : ends[0]], refs[ends[0] : ends[1]], refs[ends[1] : ends[2]], *refs[-3:]
        ),
        out_shape=(out, out),
        in_specs=[pl.BlockSpec(memory_space=pltpu.SMEM)] + [inside] * (ends[2] - 1) + [anywhere] * len(after),
        out_specs=[inside] * 2,
        scratch_shapes=[pltpu.VMEM((2 * tokens, depth), jnp.bfloat16)],
        compiler_params=pltpu.CompilerParams(vmem_limit_bytes=VMEM_LIMIT),
        cost_estimate=SHORT,
    )(place, *slots, *[pltpu.with_memory_space_constraint(w, pltpu.VMEM) for w in weights], *earlier, *after)


def stream_kernel(first, depth, place_ref, slot_refs, weight_ref, earlier_refs, send_ref, keep_ref, both, landed, arrived):
    half = send_ref.shape[0]
    width = landed.shape[1]
    column = follow(earlier_refs, (send_ref, keep_ref))
    steps = (send_ref.shape[1] - column) // width

    def fetch(step):
        start = pl.multiple_of(first + step * width, width)
        slot = lax.rem(step, depth)
        return pltpu.make_async_copy(weight_ref.at[pl.ds(start, width), :], landed.at[slot], arrived.at[slot])

    for step in range(min(depth, steps)):
        fetch(step).start()
    fill(both, slot_refs, place_ref)

    @pl.loop(0, steps)
    def _(step):
        fetch(step).wait()
        high, low = split(landed[lax.rem(step, depth)])
        part = three_pass(both, high, low, 1)
        at = pl.ds(pl.multiple_of(column + step * width, width), width)
        keep_ref[:, at] = part[:half]
        send_ref[:, at] = part[half:]

        @pl.when(step + depth < steps)
        def _():
            fetch(step + depth).start()


def stream(slots, weight, place, first, hidden, earlier, after):
    tokens, columns = slots[0].shape[0] * len(slots), slots[0].shape[1]
    width, depth = divisor(hidden, 256, 128), 2
    out = jax.ShapeDtypeStruct((tokens // 2, hidden + (earlier[0].shape[1] if earlier else 0)), jnp.float32)
    inside, anywhere = pl.BlockSpec(memory_space=pltpu.VMEM), pl.BlockSpec(memory_space=pl.ANY)
    last = 1 + len(slots)
    return pl.pallas_call(
        lambda *refs: stream_kernel(
            first, depth, refs[0], refs[1:last], refs[last], refs[last + 1 : last + 1 + len(earlier)], *refs[-5:]
        ),
        out_shape=(out, out),
        in_specs=[pl.BlockSpec(memory_space=pltpu.SMEM)]
        + [inside] * len(slots)
        + [anywhere]
        + [inside] * len(earlier)
        + [anywhere] * len(after),
        out_specs=[inside] * 2,
        scratch_shapes=[
            pltpu.VMEM((2 * tokens, columns), jnp.bfloat16),
            pltpu.VMEM((depth, width, columns), jnp.float32),
            pltpu.SemaphoreType.DMA((depth,)),
        ],
        compiler_params=pltpu.CompilerParams(vmem_limit_bytes=VMEM_LIMIT),
        cost_estimate=SHORT,
    )(place, *slots, pltpu.with_memory_space_constraint(weight, pltpu.HBM), *earlier, *after)


def backward_kernel(slots, pieces, earlier, first_column, place_ref, *refs):
    act_refs, weight_refs = refs[:slots], refs[slots : slots + 2 * pieces]
    earlier_refs = refs[slots + 2 * pieces : slots + 2 * pieces + earlier]
    out_refs = refs[-2 - slots : -2]
    both, result = refs[-2:]
    block = act_refs[0].shape[0]
    total = block * slots
    for p in range(slots):
        high, low = split(act_refs[p][...])
        both[p * block : (p + 1) * block, :] = high
        both[total + p * block : total + (p + 1) * block, :] = low

    depth = out_refs[0].shape[1]
    width = result.shape[1]

    @pl.loop(0, depth // width)
    def _(step):
        start = pl.multiple_of(step * width, width)
        tile = (pl.ds(pl.multiple_of(first_column + start, width), width), slice(None))
        total_sum, column = 0.0, 0
        for high_ref, low_ref in zip(weight_refs[::2], weight_refs[1::2]):
            columns = slice(column, column + high_ref.shape[1])
            total_sum += three_pass(both[:, columns], high_ref[tile], low_ref[tile], 1)
            column = columns.stop
        result[...] = total_sum
        for b in range(slots):
            row = pl.multiple_of(place_ref[b] * block, block)
            rows = result[pl.ds(row, block), :]
            if earlier:
                rows = rows + earlier_refs[b][:, pl.ds(pl.multiple_of(first_column + start, width), width)]
            out_refs[b][:, pl.ds(start, width)] = rows


def backward(acts, weights, place, earlier, part, parts, after):
    slots, (block, hidden) = len(acts), acts[0].shape
    depth = weights[0].shape[0] // parts
    width = divisor(depth, 256, 128)
    out = jax.ShapeDtypeStruct((block, depth), jnp.float32)
    inside = pl.BlockSpec(memory_space=pltpu.VMEM)
    return pl.pallas_call(
        functools.partial(backward_kernel, slots, len(weights) // 2, len(earlier), part * depth),
        out_shape=[out] * slots,
        in_specs=[pl.BlockSpec(memory_space=pltpu.SMEM)]
        + [inside] * (slots + len(weights) + len(earlier))
        + [pl.BlockSpec(memory_space=pl.ANY)] * len(after),
        out_specs=[inside] * slots,
        scratch_shapes=[
            pltpu.VMEM((2 * block * slots, hidden), jnp.bfloat16),
            pltpu.VMEM((block * slots, width), jnp.float32),
        ],
        compiler_params=pltpu.CompilerParams(vmem_limit_bytes=VMEM_LIMIT),
        cost_estimate=SHORT,
    )(place, *acts, *[pltpu.with_memory_space_constraint(part, pltpu.VMEM) for part in weights], *earlier, *after)


def body(hid_size, emb_size, inputs, out_grad, in_weight, in_bias, out_weight, norm_gain):
    chips = emb_size // 2
    tokens, depth = inputs.shape
    model_width = depth * emb_size
    hidden = in_weight.shape[1]
    me = lax.axis_index("emb")
    chip, core = me // 2, me % 2

    def along_hid(values, steps=1):
        return lax.ppermute(values, "hid", [(i, (i + steps) % hid_size) for i in range(hid_size)])

    def other_core(values):
        return lax.ppermute(values, "emb", [(i, i ^ 1) for i in range(emb_size)])

    def next_chip(values):
        return lax.ppermute(values, "emb", [(i, (i + 2) % emb_size) for i in range(emb_size)])

    owner = jnp.arange(emb_size, dtype=jnp.int32)
    place = ((owner % 2) ^ core) * chips + (owner // 2 - chip) % chips

    def gathered(values):
        return [values] + [along_hid(values, step) for step in range(1, hid_size)]

    grads = gathered(out_grad)
    piece = hidden // CHUNKS
    quarter = piece // 2

    def tied(values, others):
        return lax.optimization_barrier((values, others))

    def halved(partial, behind=()):
        send, keep = partial
        return keep + tied(other_core(send), behind)[0]

    def exchanged(summed):
        terms = [summed[d * tokens : (d + 1) * tokens] for d in range(chips)]
        arrival = next_chip(terms[chips - 1])
        for step in range(2, chips):
            arrival = next_chip(arrival + terms[chips - step])
        return arrival, terms[0]

    def prepared(c, after):
        return prepare(in_weight, (0, depth), (c * quarter, quarter), after)

    moments = call(moments_kernel, jax.ShapeDtypeStruct((2 * tokens, 128), jnp.float32), (inputs,), ())
    in_parts = prepared(0, [place, moments])
    in_parts += prepared(1, [in_parts[0]])
    in_parts += prepared(2, [in_parts[2]])
    moments = call(
        functools.partial(merge_kernel, depth), moments, (moments, other_core(moments)), (in_parts[4], *grads[1:])
    )
    back_0 = stream(grads, out_weight, place, 0, piece, (), [moments])
    parts = [moments]
    for _ in range(1, chips):
        parts.append(next_chip(parts[-1]))
    normed, scaled, inv_std = call(
        functools.partial(normalise_kernel, 2 * depth),
        (inputs, inputs, jax.ShapeDtypeStruct((tokens, 128), jnp.float32)),
        (inputs, norm_gain[None, :], *parts),
        (back_0[1],),
    )
    inv_std = inv_std[:, :1]
    scaled = gathered(scaled)
    back_0, _ = tied(back_0, parts)
    half_0 = halved(back_0, scaled[0])
    in_parts += prepared(3, [scaled[0], half_0])
    back_1 = stream(grads, out_weight, place, piece, piece, (), [in_parts[6]])
    back_0 = exchanged(half_0)
    back_1, (back_0, scaled) = tied(back_1, (back_0, scaled))
    pre_0 = forward(scaled, in_parts[:2], place, (), [back_1[1]])
    half_1 = halved(back_1, pre_0)
    back_1 = exchanged(half_1)
    pre_0 = forward(scaled, in_parts[2:4], place, pre_0, [half_1])
    pre_1 = forward(scaled, in_parts[4:6], place, (), [pre_0[1]])
    half_0 = halved(pre_0, pre_1)
    pre_1 = forward(scaled, in_parts[6:], place, pre_1, [half_0])
    pre_1, back_1 = tied(pre_1, back_1)
    backs = [back_0, back_1]
    pres = [exchanged(half_0), exchanged(halved(pre_1))]

    def spread_out(c):
        act = sum(backs[c]) * gelu_slope(sum(pres[c]) + in_bias[c * piece : (c + 1) * piece])
        mine = [None] * chips
        mine[0] = act
        for step in range(1, chips):
            act = next_chip(act)
            mine[(chips - step) % chips] = act
        return mine

    def both_cores(mine):
        return mine + [other_core(block) for block in mine]

    def summed_along_hid(sums):
        return sum([along_hid(sums[step], -step) for step in range(1, hid_size)], start=sums[0])

    acts_0, acts_1 = spread_out(0), spread_out(1)
    sums = backward(both_cores(acts_0), in_parts[:4], place, (), 0, 1, [pre_1[1]])
    acts_1[1:], sums = tied(acts_1[1:], sums)
    acts_1 = both_cores(acts_1)
    parts = 2 if depth % 512 == 0 else 1
    ends = []
    for part in range(parts):
        ends.append(backward(acts_1, in_parts[4:], place, sums, part, parts, [ends[-1][0] if ends else sums[0]]))
    running = jnp.concatenate([summed_along_hid(end) for end in ends], axis=1)
    normed_grad = running * norm_gain
    totals = lax.psum(
        jnp.stack([jnp.sum(normed_grad, axis=-1), jnp.sum(normed_grad * normed, axis=-1)]), "emb"
    )
    first, second = (totals / model_width)[:, :, None]
    return inv_std * (normed_grad - first - normed * second)


def solution(mesh):
    hid_size, emb_size = mesh.shape["hid"], mesh.shape["emb"]
    assert hid_size == emb_size and emb_size % 2 == 0
    return jax.shard_map(
        functools.partial(body, hid_size, emb_size),
        mesh=mesh,
        in_specs=(
            P(("groups", "hid"), "emb"),
            P(("groups", "hid"), "emb"),
            P("emb", "hid"),
            P("hid"),
            P("hid", "emb"),
            P("emb"),
        ),
        out_specs=P(("groups", "hid"), "emb"),
        check_vma=False,
    )
```

```python
import functools
import math

import jax
import jax.numpy as jnp
from jax import lax
from jax.experimental import pallas as pl
from jax.experimental.pallas import tpu as pltpu
from jax.sharding import PartitionSpec as P

VMEM_LIMIT = 5 * 1024 * 1024
CHUNKS = 2
SHORT = pl.CostEstimate(flops=1 << 20, bytes_accessed=1 << 18, transcendentals=0)


def gelu_slope(values):
    cdf = 0.5 * (1.0 + lax.erf(values * (1.0 / math.sqrt(2.0))))
    density = jnp.exp(-0.5 * values * values) * (1.0 / math.sqrt(2.0 * math.pi))
    return cdf + values * density


def split(values):
    high = values.astype(jnp.bfloat16)
    return high, (values - high.astype(jnp.float32)).astype(jnp.bfloat16)


def divisor(extent, *choices):
    return next(c for c in choices if extent % c == 0)


def call(kernel, out_shape, operands, after):
    outs = out_shape if isinstance(out_shape, tuple) else (out_shape,)

    def run(*refs):
        kernel(*refs[: len(operands)], *refs[len(operands) + len(after) :])

    inside = pl.BlockSpec(memory_space=pltpu.VMEM)
    result = pl.pallas_call(
        run,
        out_shape=tuple(jax.ShapeDtypeStruct(o.shape, o.dtype) for o in outs),
        in_specs=[inside] * len(operands) + [pl.BlockSpec(memory_space=pl.ANY)] * len(after),
        out_specs=[inside] * len(outs),
        compiler_params=pltpu.CompilerParams(vmem_limit_bytes=VMEM_LIMIT),
        cost_estimate=SHORT,
    )(*operands, *after)
    return result if isinstance(out_shape, tuple) else result[0]


def moments_kernel(inputs_ref, out_ref):
    rows, depth = inputs_ref.shape
    mean = jnp.sum(inputs_ref[...], axis=1, keepdims=True) * (1.0 / depth)
    square = jnp.sum(jnp.square(inputs_ref[...] - mean), axis=1, keepdims=True)
    out_ref[:rows] = jnp.broadcast_to(mean, (rows, 128))
    out_ref[rows:] = jnp.broadcast_to(square, (rows, 128))


def merge(moments, count):
    rows = moments[0].shape[0] // 2
    mean = sum(part[:rows] for part in moments) * (1.0 / len(moments))
    square = sum(part[rows:] + count * jnp.square(part[:rows] - mean) for part in moments)
    return mean, square


def merge_kernel(count, first_ref, second_ref, out_ref):
    rows = out_ref.shape[0] // 2
    out_ref[:rows], out_ref[rows:] = merge((first_ref[...], second_ref[...]), count)


def normalise_kernel(count, inputs_ref, gain_ref, *refs):
    *moment_refs, normed_ref, scaled_ref, inv_std_ref = refs
    mean, square = merge([ref[...] for ref in moment_refs], count)
    inv_std = 1.0 / jnp.sqrt(square * (1.0 / (count * len(moment_refs))) + 1e-06)
    normed = (inputs_ref[...] - mean[:, :1]) * inv_std[:, :1]
    normed_ref[...] = normed
    scaled_ref[...] = normed * gain_ref[...]
    inv_std_ref[...] = inv_std


def prepare_kernel(rows, columns, block, depth, weight_ref, *refs):
    high_ref, low_ref, landed, arrived = refs[-4:]
    steps = rows[1] // block

    def fetch(step):
        start = pl.multiple_of(rows[0] + step * block, block)
        slot = lax.rem(step, depth)
        return pltpu.make_async_copy(
            weight_ref.at[pl.ds(start, block), pl.ds(*columns)], landed.at[slot], arrived.at[slot]
        )

    for step in range(min(depth, steps)):
        fetch(step).start()

    @pl.loop(0, steps)
    def _(step):
        fetch(step).wait()
        high, low = split(landed[lax.rem(step, depth)])
        at = pl.ds(pl.multiple_of(step * block, block), block)
        high_ref[at, :] = high
        low_ref[at, :] = low

        @pl.when(step + depth < steps)
        def _():
            fetch(step + depth).start()


def prepare(weight, rows, columns, after):
    block = 256 * 1536 // columns[1]
    block = divisor(rows[1], *[b for b in (256, 128, 64, 32) if b <= max(block, 32)])
    depth = 4
    out = pltpu.VMEM((rows[1], columns[1]), jnp.bfloat16)
    return pl.pallas_call(
        functools.partial(prepare_kernel, rows, columns, block, depth),
        out_shape=(out, out),
        in_specs=[pl.BlockSpec(memory_space=pl.ANY)] * (1 + len(after)),
        out_specs=[pl.BlockSpec(memory_space=pltpu.VMEM)] * 2,
        scratch_shapes=[
            pltpu.VMEM((depth, block, columns[1]), jnp.float32),
            pltpu.SemaphoreType.DMA((depth,)),
        ],
        compiler_params=pltpu.CompilerParams(vmem_limit_bytes=2 * VMEM_LIMIT),
        cost_estimate=SHORT,
    )(pltpu.with_memory_space_constraint(weight, pltpu.HBM), *after)


def three_pass(both, high, low, contract):
    rows = both.shape[0] // 2
    dot = functools.partial(
        lax.dot_general,
        dimension_numbers=(((1,), (contract,)), ((), ())),
        preferred_element_type=jnp.float32,
    )
    first = dot(both[...], high)
    return first[:rows] + first[rows:] + dot(both[:rows, :], low)


def fill(both, block_refs, place_ref):
    total = both.shape[0] // 2
    block = total // place_ref.shape[0]
    index = 0
    for ref in block_refs:
        for start in range(0, ref.shape[0], block):
            high, low = split(ref[start : start + block, :])
            row = pl.multiple_of(place_ref[index] * block, block)
            both[pl.ds(row, block), :] = high
            both[pl.ds(total + row, block), :] = low
            index += 1


def follow(earlier_refs, out_refs):
    for earlier_ref, out_ref in zip(earlier_refs, out_refs):
        out_ref[:, : earlier_ref.shape[1]] = earlier_ref[...]
    return earlier_refs[0].shape[1] if earlier_refs else 0


def forward_kernel(place_ref, slot_refs, weight_refs, earlier_refs, send_ref, keep_ref, both):
    fill(both, slot_refs, place_ref)
    half, column = send_ref.shape[0], follow(earlier_refs, (send_ref, keep_ref))
    for high_ref, low_ref in zip(weight_refs[::2], weight_refs[1::2]):
        width = divisor(high_ref.shape[1], 256, 128)

        @pl.loop(0, high_ref.shape[1] // width, unroll=2)
        def _(step):
            at = pl.ds(pl.multiple_of(step * width, width), width)
            part = three_pass(both, high_ref[:, at], low_ref[:, at], 0)
            at = pl.ds(pl.multiple_of(column + step * width, width), width)
            keep_ref[:, at] = part[:half]
            send_ref[:, at] = part[half:]

        column += high_ref.shape[1]


def forward(slots, weights, place, earlier, after):
    tokens, depth = slots[0].shape[0] * len(slots), slots[0].shape[1]
    hidden = sum(w.shape[1] for w in weights[::2]) + (earlier[0].shape[1] if earlier else 0)
    out = jax.ShapeDtypeStruct((tokens // 2, hidden), jnp.float32)
    inside, anywhere = pl.BlockSpec(memory_space=pltpu.VMEM), pl.BlockSpec(memory_space=pl.ANY)
    ends = [1 + len(slots), 1 + len(slots) + len(weights), 1 + len(slots) + len(weights) + len(earlier)]
    return pl.pallas_call(
        lambda *refs: forward_kernel(
            refs[0], refs[1 : ends[0]], refs[ends[0] : ends[1]], refs[ends[1] : ends[2]], *refs[-3:]
        ),
        out_shape=(out, out),
        in_specs=[pl.BlockSpec(memory_space=pltpu.SMEM)] + [inside] * (ends[2] - 1) + [anywhere] * len(after),
        out_specs=[inside] * 2,
        scratch_shapes=[pltpu.VMEM((2 * tokens, depth), jnp.bfloat16)],
        compiler_params=pltpu.CompilerParams(vmem_limit_bytes=VMEM_LIMIT),
        cost_estimate=SHORT,
    )(place, *slots, *[pltpu.with_memory_space_constraint(w, pltpu.VMEM) for w in weights], *earlier, *after)


def stream_kernel(first, depth, place_ref, slot_refs, weight_ref, earlier_refs, send_ref, keep_ref, both, landed, arrived):
    half = send_ref.shape[0]
    width = landed.shape[1]
    column = follow(earlier_refs, (send_ref, keep_ref))
    steps = (send_ref.shape[1] - column) // width

    def fetch(step):
        start = pl.multiple_of(first + step * width, width)
        slot = lax.rem(step, depth)
        return pltpu.make_async_copy(weight_ref.at[pl.ds(start, width), :], landed.at[slot], arrived.at[slot])

    for step in range(min(depth, steps)):
        fetch(step).start()
    fill(both, slot_refs, place_ref)

    @pl.loop(0, steps)
    def _(step):
        fetch(step).wait()
        high, low = split(landed[lax.rem(step, depth)])
        part = three_pass(both, high, low, 1)
        at = pl.ds(pl.multiple_of(column + step * width, width), width)
        keep_ref[:, at] = part[:half]
        send_ref[:, at] = part[half:]

        @pl.when(step + depth < steps)
        def _():
            fetch(step + depth).start()


def stream(slots, weight, place, first, hidden, earlier, after):
    tokens, columns = slots[0].shape[0] * len(slots), slots[0].shape[1]
    width, depth = divisor(hidden, 256, 128), 4
    out = jax.ShapeDtypeStruct((tokens // 2, hidden + (earlier[0].shape[1] if earlier else 0)), jnp.float32)
    inside, anywhere = pl.BlockSpec(memory_space=pltpu.VMEM), pl.BlockSpec(memory_space=pl.ANY)
    last = 1 + len(slots)
    return pl.pallas_call(
        lambda *refs: stream_kernel(
            first, depth, refs[0], refs[1:last], refs[last], refs[last + 1 : last + 1 + len(earlier)], *refs[-5:]
        ),
        out_shape=(out, out),
        in_specs=[pl.BlockSpec(memory_space=pltpu.SMEM)]
        + [inside] * len(slots)
        + [anywhere]
        + [inside] * len(earlier)
        + [anywhere] * len(after),
        out_specs=[inside] * 2,
        scratch_shapes=[
            pltpu.VMEM((2 * tokens, columns), jnp.bfloat16),
            pltpu.VMEM((depth, width, columns), jnp.float32),
            pltpu.SemaphoreType.DMA((depth,)),
        ],
        compiler_params=pltpu.CompilerParams(vmem_limit_bytes=2 * VMEM_LIMIT),
        cost_estimate=SHORT,
    )(place, *slots, pltpu.with_memory_space_constraint(weight, pltpu.HBM), *earlier, *after)


def backward_kernel(slots, pieces, earlier, first_column, place_ref, *refs):
    act_refs, weight_refs = refs[:slots], refs[slots : slots + 2 * pieces]
    earlier_refs = refs[slots + 2 * pieces : slots + 2 * pieces + earlier]
    out_refs = refs[-2 - slots : -2]
    both, result = refs[-2:]
    block = act_refs[0].shape[0]
    total = block * slots
    for p in range(slots):
        high, low = split(act_refs[p][...])
        both[p * block : (p + 1) * block, :] = high
        both[total + p * block : total + (p + 1) * block, :] = low

    depth = out_refs[0].shape[1]
    width = result.shape[1]

    @pl.loop(0, depth // width)
    def _(step):
        start = pl.multiple_of(step * width, width)
        tile = (pl.ds(pl.multiple_of(first_column + start, width), width), slice(None))
        total_sum, column = 0.0, 0
        for high_ref, low_ref in zip(weight_refs[::2], weight_refs[1::2]):
            columns = slice(column, column + high_ref.shape[1])
            total_sum += three_pass(both[:, columns], high_ref[tile], low_ref[tile], 1)
            column = columns.stop
        result[...] = total_sum
        for b in range(slots):
            row = pl.multiple_of(place_ref[b] * block, block)
            rows = result[pl.ds(row, block), :]
            if earlier:
                rows = rows + earlier_refs[b][:, pl.ds(pl.multiple_of(first_column + start, width), width)]
            out_refs[b][:, pl.ds(start, width)] = rows


def backward(acts, weights, place, earlier, part, parts, after):
    slots, (block, hidden) = len(acts), acts[0].shape
    depth = weights[0].shape[0] // parts
    width = divisor(depth, 256, 128)
    out = jax.ShapeDtypeStruct((block, depth), jnp.float32)
    inside = pl.BlockSpec(memory_space=pltpu.VMEM)
    return pl.pallas_call(
        functools.partial(backward_kernel, slots, len(weights) // 2, len(earlier), part * depth),
        out_shape=[out] * slots,
        in_specs=[pl.BlockSpec(memory_space=pltpu.SMEM)]
        + [inside] * (slots + len(weights) + len(earlier))
        + [pl.BlockSpec(memory_space=pl.ANY)] * len(after),
        out_specs=[inside] * slots,
        scratch_shapes=[
            pltpu.VMEM((2 * block * slots, hidden), jnp.bfloat16),
            pltpu.VMEM((block * slots, width), jnp.float32),
        ],
        compiler_params=pltpu.CompilerParams(vmem_limit_bytes=VMEM_LIMIT),
        cost_estimate=SHORT,
    )(place, *acts, *[pltpu.with_memory_space_constraint(part, pltpu.VMEM) for part in weights], *earlier, *after)


def body(hid_size, emb_size, inputs, out_grad, in_weight, in_bias, out_weight, norm_gain):
    chips = emb_size // 2
    tokens, depth = inputs.shape
    model_width = depth * emb_size
    hidden = in_weight.shape[1]
    me = lax.axis_index("emb")
    chip, core = me // 2, me % 2

    def along_hid(values, steps=1):
        return lax.ppermute(values, "hid", [(i, (i + steps) % hid_size) for i in range(hid_size)])

    def other_core(values):
        return lax.ppermute(values, "emb", [(i, i ^ 1) for i in range(emb_size)])

    def next_chip(values):
        return lax.ppermute(values, "emb", [(i, (i + 2) % emb_size) for i in range(emb_size)])

    owner = jnp.arange(emb_size, dtype=jnp.int32)
    place = ((owner % 2) ^ core) * chips + (owner // 2 - chip) % chips

    def gathered(values):
        return [values] + [along_hid(values, step) for step in range(1, hid_size)]

    grads = gathered(out_grad)
    piece = hidden // CHUNKS
    quarter = piece // 2

    def tied(values, others):
        return lax.optimization_barrier((values, others))

    def halved(partial, behind=()):
        send, keep = partial
        return keep + tied(other_core(send), behind)[0]

    def exchanged(summed):
        terms = [summed[d * tokens : (d + 1) * tokens] for d in range(chips)]
        arrival = next_chip(terms[chips - 1])
        for step in range(2, chips):
            arrival = next_chip(arrival + terms[chips - step])
        return arrival, terms[0]

    def prepared(c, after):
        return prepare(in_weight, (0, depth), (c * quarter, quarter), after)

    moments = call(moments_kernel, jax.ShapeDtypeStruct((2 * tokens, 128), jnp.float32), (inputs,), ())
    in_parts = prepared(0, [place, moments])
    in_parts += prepared(1, [in_parts[0]])
    moments = call(
        functools.partial(merge_kernel, depth), moments, (moments, other_core(moments)), (in_parts[2], *grads[1:])
    )
    in_parts += prepared(2, [moments])
    parts = [moments]
    for _ in range(1, chips):
        parts.append(next_chip(parts[-1]))
    normed, scaled, inv_std = call(
        functools.partial(normalise_kernel, 2 * depth),
        (inputs, inputs, jax.ShapeDtypeStruct((tokens, 128), jnp.float32)),
        (inputs, norm_gain[None, :], *parts),
        (in_parts[4],),
    )
    inv_std = inv_std[:, :1]
    scaled = gathered(scaled)
    back_0 = stream(grads, out_weight, place, 0, piece, (), [scaled[0]])
    back_0, (scaled[1], scaled[-1]) = tied(back_0, (scaled[1], scaled[-1]))
    half_0 = halved(back_0)
    back_1 = stream(grads, out_weight, place, piece, piece, (), [half_0])
    back_0 = exchanged(half_0)
    back_1, (back_0, scaled) = tied(back_1, (back_0, scaled))
    in_parts += prepared(3, [back_1[0]])
    half_1 = halved(back_1, in_parts[6])
    back_1 = exchanged(half_1)
    pre_0 = forward(scaled, in_parts[:4], place, (), [half_1])
    pre_0, back_1 = tied(pre_0, back_1)
    pre_1 = forward(scaled, in_parts[4:6], place, (), [pre_0[1]])
    half_0 = halved(pre_0, pre_1)
    pre_1 = forward(scaled, in_parts[6:], place, pre_1, [half_0])
    backs = [back_0, back_1]
    pres = [exchanged(half_0), exchanged(halved(pre_1))]

    def spread_out(c):
        act = sum(backs[c]) * gelu_slope(sum(pres[c]) + in_bias[c * piece : (c + 1) * piece])
        mine = [None] * chips
        mine[0] = act
        for step in range(1, chips):
            act = next_chip(act)
            mine[(chips - step) % chips] = act
        return mine

    def both_cores(mine):
        return mine + [other_core(block) for block in mine]

    def summed_along_hid(sums):
        return sum([along_hid(sums[step], -step) for step in range(1, hid_size)], start=sums[0])

    acts_0, acts_1 = spread_out(0), spread_out(1)
    sums = backward(both_cores(acts_0), in_parts[:4], place, (), 0, 1, [pre_1[1]])
    acts_1[1:], sums = tied(acts_1[1:], sums)
    acts_1 = both_cores(acts_1)
    parts = 2 if depth % 512 == 0 else 1
    ends = []
    for part in range(parts):
        ends.append(backward(acts_1, in_parts[4:], place, sums, part, parts, [ends[-1][0] if ends else sums[0]]))
    running = jnp.concatenate([summed_along_hid(end) for end in ends], axis=1)
    normed_grad = running * norm_gain
    totals = lax.psum(
        jnp.stack([jnp.sum(normed_grad, axis=-1), jnp.sum(normed_grad * normed, axis=-1)]), "emb"
    )
    first, second = (totals / model_width)[:, :, None]
    return inv_std * (normed_grad - first - normed * second)


def solution(mesh):
    hid_size, emb_size = mesh.shape["hid"], mesh.shape["emb"]
    assert hid_size == emb_size and emb_size % 2 == 0
    return jax.shard_map(
        functools.partial(body, hid_size, emb_size),
        mesh=mesh,
        in_specs=(
            P(("groups", "hid"), "emb"),
            P(("groups", "hid"), "emb"),
            P("emb", "hid"),
            P("hid"),
            P("hid", "emb"),
            P("emb"),
        ),
        out_specs=P(("groups", "hid"), "emb"),
        check_vma=False,
    )
```

```python
import functools
import math

import jax
import jax.numpy as jnp
from jax import lax
from jax.experimental import pallas as pl
from jax.experimental.pallas import tpu as pltpu
from jax.sharding import PartitionSpec as P

VMEM_LIMIT = 5 * 1024 * 1024
CHUNKS = 2
SHORT = pl.CostEstimate(flops=1 << 20, bytes_accessed=1 << 18, transcendentals=0)


def gelu_slope(values):
    cdf = 0.5 * (1.0 + lax.erf(values * (1.0 / math.sqrt(2.0))))
    density = jnp.exp(-0.5 * values * values) * (1.0 / math.sqrt(2.0 * math.pi))
    return cdf + values * density


def split(values):
    high = values.astype(jnp.bfloat16)
    return high, (values - high.astype(jnp.float32)).astype(jnp.bfloat16)


def divisor(extent, *choices):
    return next(c for c in choices if extent % c == 0)


def call(kernel, out_shape, operands, after):
    outs = out_shape if isinstance(out_shape, tuple) else (out_shape,)

    def run(*refs):
        kernel(*refs[: len(operands)], *refs[len(operands) + len(after) :])

    inside = pl.BlockSpec(memory_space=pltpu.VMEM)
    result = pl.pallas_call(
        run,
        out_shape=tuple(jax.ShapeDtypeStruct(o.shape, o.dtype) for o in outs),
        in_specs=[inside] * len(operands) + [pl.BlockSpec(memory_space=pl.ANY)] * len(after),
        out_specs=[inside] * len(outs),
        compiler_params=pltpu.CompilerParams(vmem_limit_bytes=VMEM_LIMIT),
        cost_estimate=SHORT,
    )(*operands, *after)
    return result if isinstance(out_shape, tuple) else result[0]


def moments_kernel(inputs_ref, out_ref):
    rows, depth = inputs_ref.shape
    mean = jnp.sum(inputs_ref[...], axis=1, keepdims=True) * (1.0 / depth)
    square = jnp.sum(jnp.square(inputs_ref[...] - mean), axis=1, keepdims=True)
    out_ref[:rows] = jnp.broadcast_to(mean, (rows, 128))
    out_ref[rows:] = jnp.broadcast_to(square, (rows, 128))


def merge(moments, count):
    rows = moments[0].shape[0] // 2
    mean = sum(part[:rows] for part in moments) * (1.0 / len(moments))
    square = sum(part[rows:] + count * jnp.square(part[:rows] - mean) for part in moments)
    return mean, square


def merge_kernel(count, first_ref, second_ref, out_ref):
    rows = out_ref.shape[0] // 2
    out_ref[:rows], out_ref[rows:] = merge((first_ref[...], second_ref[...]), count)


def normalise_kernel(count, inputs_ref, gain_ref, *refs):
    *moment_refs, normed_ref, scaled_ref, inv_std_ref = refs
    mean, square = merge([ref[...] for ref in moment_refs], count)
    inv_std = 1.0 / jnp.sqrt(square * (1.0 / (count * len(moment_refs))) + 1e-06)
    normed = (inputs_ref[...] - mean[:, :1]) * inv_std[:, :1]
    normed_ref[...] = normed
    scaled_ref[...] = normed * gain_ref[...]
    inv_std_ref[...] = inv_std


def prepare_kernel(rows, columns, block, depth, weight_ref, *refs):
    high_ref, low_ref, landed, arrived = refs[-4:]
    steps = rows[1] // block

    def fetch(step):
        start = pl.multiple_of(rows[0] + step * block, block)
        slot = lax.rem(step, depth)
        return pltpu.make_async_copy(
            weight_ref.at[pl.ds(start, block), pl.ds(*columns)], landed.at[slot], arrived.at[slot]
        )

    for step in range(min(depth, steps)):
        fetch(step).start()

    @pl.loop(0, steps)
    def _(step):
        fetch(step).wait()
        high, low = split(landed[lax.rem(step, depth)])
        at = pl.ds(pl.multiple_of(step * block, block), block)
        high_ref[at, :] = high
        low_ref[at, :] = low

        @pl.when(step + depth < steps)
        def _():
            fetch(step + depth).start()


def prepare(weight, rows, columns, after):
    block = 256 * 1536 // columns[1]
    block = divisor(rows[1], *[b for b in (256, 128, 64, 32) if b <= max(block, 32)])
    depth = 4
    out = pltpu.VMEM((rows[1], columns[1]), jnp.bfloat16)
    return pl.pallas_call(
        functools.partial(prepare_kernel, rows, columns, block, depth),
        out_shape=(out, out),
        in_specs=[pl.BlockSpec(memory_space=pl.ANY)] * (1 + len(after)),
        out_specs=[pl.BlockSpec(memory_space=pltpu.VMEM)] * 2,
        scratch_shapes=[
            pltpu.VMEM((depth, block, columns[1]), jnp.float32),
            pltpu.SemaphoreType.DMA((depth,)),
        ],
        compiler_params=pltpu.CompilerParams(vmem_limit_bytes=2 * VMEM_LIMIT),
        cost_estimate=SHORT,
    )(pltpu.with_memory_space_constraint(weight, pltpu.HBM), *after)


def three_pass(both, high, low, contract):
    rows = both.shape[0] // 2
    dot = functools.partial(
        lax.dot_general,
        dimension_numbers=(((1,), (contract,)), ((), ())),
        preferred_element_type=jnp.float32,
    )
    first = dot(both[...], high)
    return first[:rows] + first[rows:] + dot(both[:rows, :], low)


def fill(both, block_refs, place_ref):
    total = both.shape[0] // 2
    block = total // place_ref.shape[0]
    index = 0
    for ref in block_refs:
        for start in range(0, ref.shape[0], block):
            high, low = split(ref[start : start + block, :])
            row = pl.multiple_of(place_ref[index] * block, block)
            both[pl.ds(row, block), :] = high
            both[pl.ds(total + row, block), :] = low
            index += 1


def follow(earlier_refs, out_refs):
    for earlier_ref, out_ref in zip(earlier_refs, out_refs):
        out_ref[:, : earlier_ref.shape[1]] = earlier_ref[...]
    return earlier_refs[0].shape[1] if earlier_refs else 0


def forward_kernel(place_ref, slot_refs, weight_refs, earlier_refs, send_ref, keep_ref, both):
    fill(both, slot_refs, place_ref)
    half, column = send_ref.shape[0], follow(earlier_refs, (send_ref, keep_ref))
    for high_ref, low_ref in zip(weight_refs[::2], weight_refs[1::2]):
        width = divisor(high_ref.shape[1], 256, 128)

        @pl.loop(0, high_ref.shape[1] // width, unroll=2)
        def _(step):
            at = pl.ds(pl.multiple_of(step * width, width), width)
            part = three_pass(both, high_ref[:, at], low_ref[:, at], 0)
            at = pl.ds(pl.multiple_of(column + step * width, width), width)
            keep_ref[:, at] = part[:half]
            send_ref[:, at] = part[half:]

        column += high_ref.shape[1]


def forward(slots, weights, place, earlier, after):
    tokens, depth = slots[0].shape[0] * len(slots), slots[0].shape[1]
    hidden = sum(w.shape[1] for w in weights[::2]) + (earlier[0].shape[1] if earlier else 0)
    out = jax.ShapeDtypeStruct((tokens // 2, hidden), jnp.float32)
    inside, anywhere = pl.BlockSpec(memory_space=pltpu.VMEM), pl.BlockSpec(memory_space=pl.ANY)
    ends = [1 + len(slots), 1 + len(slots) + len(weights), 1 + len(slots) + len(weights) + len(earlier)]
    return pl.pallas_call(
        lambda *refs: forward_kernel(
            refs[0], refs[1 : ends[0]], refs[ends[0] : ends[1]], refs[ends[1] : ends[2]], *refs[-3:]
        ),
        out_shape=(out, out),
        in_specs=[pl.BlockSpec(memory_space=pltpu.SMEM)] + [inside] * (ends[2] - 1) + [anywhere] * len(after),
        out_specs=[inside] * 2,
        scratch_shapes=[pltpu.VMEM((2 * tokens, depth), jnp.bfloat16)],
        compiler_params=pltpu.CompilerParams(vmem_limit_bytes=VMEM_LIMIT),
        cost_estimate=SHORT,
    )(place, *slots, *[pltpu.with_memory_space_constraint(w, pltpu.VMEM) for w in weights], *earlier, *after)


def stream_kernel(first, depth, place_ref, slot_refs, weight_ref, earlier_refs, send_ref, keep_ref, both, landed, arrived):
    half = send_ref.shape[0]
    width = landed.shape[1]
    column = follow(earlier_refs, (send_ref, keep_ref))
    steps = (send_ref.shape[1] - column) // width

    def fetch(step):
        start = pl.multiple_of(first + step * width, width)
        slot = lax.rem(step, depth)
        return pltpu.make_async_copy(weight_ref.at[pl.ds(start, width), :], landed.at[slot], arrived.at[slot])

    for step in range(min(depth, steps)):
        fetch(step).start()
    fill(both, slot_refs, place_ref)

    @pl.loop(0, steps)
    def _(step):
        fetch(step).wait()
        high, low = split(landed[lax.rem(step, depth)])
        part = three_pass(both, high, low, 1)
        at = pl.ds(pl.multiple_of(column + step * width, width), width)
        keep_ref[:, at] = part[:half]
        send_ref[:, at] = part[half:]

        @pl.when(step + depth < steps)
        def _():
            fetch(step + depth).start()


def stream(slots, weight, place, first, hidden, earlier, after):
    tokens, columns = slots[0].shape[0] * len(slots), slots[0].shape[1]
    width, depth = divisor(hidden, 256, 128), 4
    out = jax.ShapeDtypeStruct((tokens // 2, hidden + (earlier[0].shape[1] if earlier else 0)), jnp.float32)
    inside, anywhere = pl.BlockSpec(memory_space=pltpu.VMEM), pl.BlockSpec(memory_space=pl.ANY)
    last = 1 + len(slots)
    return pl.pallas_call(
        lambda *refs: stream_kernel(
            first, depth, refs[0], refs[1:last], refs[last], refs[last + 1 : last + 1 + len(earlier)], *refs[-5:]
        ),
        out_shape=(out, out),
        in_specs=[pl.BlockSpec(memory_space=pltpu.SMEM)]
        + [inside] * len(slots)
        + [anywhere]
        + [inside] * len(earlier)
        + [anywhere] * len(after),
        out_specs=[inside] * 2,
        scratch_shapes=[
            pltpu.VMEM((2 * tokens, columns), jnp.bfloat16),
            pltpu.VMEM((depth, width, columns), jnp.float32),
            pltpu.SemaphoreType.DMA((depth,)),
        ],
        compiler_params=pltpu.CompilerParams(vmem_limit_bytes=2 * VMEM_LIMIT),
        cost_estimate=SHORT,
    )(place, *slots, pltpu.with_memory_space_constraint(weight, pltpu.HBM), *earlier, *after)


def backward_kernel(slots, pieces, earlier, first_column, place_ref, *refs):
    act_refs, weight_refs = refs[:slots], refs[slots : slots + 2 * pieces]
    earlier_refs = refs[slots + 2 * pieces : slots + 2 * pieces + earlier]
    out_refs = refs[-2 - slots : -2]
    both, result = refs[-2:]
    block = act_refs[0].shape[0]
    total = block * slots
    for p in range(slots):
        high, low = split(act_refs[p][...])
        both[p * block : (p + 1) * block, :] = high
        both[total + p * block : total + (p + 1) * block, :] = low

    depth = out_refs[0].shape[1]
    width = result.shape[1]

    @pl.loop(0, depth // width)
    def _(step):
        start = pl.multiple_of(step * width, width)
        tile = (pl.ds(pl.multiple_of(first_column + start, width), width), slice(None))
        total_sum, column = 0.0, 0
        for high_ref, low_ref in zip(weight_refs[::2], weight_refs[1::2]):
            columns = slice(column, column + high_ref.shape[1])
            total_sum += three_pass(both[:, columns], high_ref[tile], low_ref[tile], 1)
            column = columns.stop
        result[...] = total_sum
        for b in range(slots):
            row = pl.multiple_of(place_ref[b] * block, block)
            rows = result[pl.ds(row, block), :]
            if earlier:
                rows = rows + earlier_refs[b][:, pl.ds(pl.multiple_of(first_column + start, width), width)]
            out_refs[b][:, pl.ds(start, width)] = rows


def backward(acts, weights, place, earlier, part, parts, after):
    slots, (block, hidden) = len(acts), acts[0].shape
    depth = weights[0].shape[0] // parts
    width = divisor(depth, 256, 128)
    out = jax.ShapeDtypeStruct((block, depth), jnp.float32)
    inside = pl.BlockSpec(memory_space=pltpu.VMEM)
    return pl.pallas_call(
        functools.partial(backward_kernel, slots, len(weights) // 2, len(earlier), part * depth),
        out_shape=[out] * slots,
        in_specs=[pl.BlockSpec(memory_space=pltpu.SMEM)]
        + [inside] * (slots + len(weights) + len(earlier))
        + [pl.BlockSpec(memory_space=pl.ANY)] * len(after),
        out_specs=[inside] * slots,
        scratch_shapes=[
            pltpu.VMEM((2 * block * slots, hidden), jnp.bfloat16),
            pltpu.VMEM((block * slots, width), jnp.float32),
        ],
        compiler_params=pltpu.CompilerParams(vmem_limit_bytes=VMEM_LIMIT),
        cost_estimate=SHORT,
    )(place, *acts, *[pltpu.with_memory_space_constraint(part, pltpu.VMEM) for part in weights], *earlier, *after)


def body(hid_size, emb_size, inputs, out_grad, in_weight, in_bias, out_weight, norm_gain):
    chips = emb_size // 2
    tokens, depth = inputs.shape
    model_width = depth * emb_size
    hidden = in_weight.shape[1]
    me = lax.axis_index("emb")
    chip, core = me // 2, me % 2

    def along_hid(values, steps=1):
        return lax.ppermute(values, "hid", [(i, (i + steps) % hid_size) for i in range(hid_size)])

    def other_core(values):
        return lax.ppermute(values, "emb", [(i, i ^ 1) for i in range(emb_size)])

    def next_chip(values):
        return lax.ppermute(values, "emb", [(i, (i + 2) % emb_size) for i in range(emb_size)])

    owner = jnp.arange(emb_size, dtype=jnp.int32)
    place = ((owner % 2) ^ core) * chips + (owner // 2 - chip) % chips

    def gathered(values):
        return [values] + [along_hid(values, step) for step in range(1, hid_size)]

    grads = gathered(out_grad)
    piece = hidden // CHUNKS
    quarter = piece // 2

    def tied(values, others):
        return lax.optimization_barrier((values, others))

    def halved(partial, behind=()):
        (send_own, send), (keep_own, keep) = [(rows[:tokens], rows[tokens:]) for rows in partial]
        return keep + tied(other_core(send), behind)[0], (keep_own, other_core(send_own))

    def exchanged(half):
        summed, own = half
        terms = [summed[d * tokens : (d + 1) * tokens] for d in range(chips - 1)]
        arrival = next_chip(terms[chips - 2])
        for step in range(chips - 3, -1, -1):
            arrival = next_chip(arrival + terms[step])
        return arrival, *own

    def prepared(c, after):
        return prepare(in_weight, (0, depth), (c * quarter, quarter), after)

    moments = call(moments_kernel, jax.ShapeDtypeStruct((2 * tokens, 128), jnp.float32), (inputs,), ())
    in_parts = prepared(0, [place, moments])
    in_parts += prepared(1, [in_parts[0]])
    moments = call(
        functools.partial(merge_kernel, depth), moments, (moments, other_core(moments)), (in_parts[2], *grads[1:])
    )
    in_parts += prepared(2, [moments])
    parts = [moments]
    for _ in range(1, chips):
        parts.append(next_chip(parts[-1]))
    normed, scaled, inv_std = call(
        functools.partial(normalise_kernel, 2 * depth),
        (inputs, inputs, jax.ShapeDtypeStruct((tokens, 128), jnp.float32)),
        (inputs, norm_gain[None, :], *parts),
        (in_parts[4],),
    )
    inv_std = inv_std[:, :1]
    scaled = gathered(scaled)
    back_0 = stream(grads, out_weight, place, 0, piece, (), [scaled[0]])
    back_0, (scaled[1], scaled[-1]) = tied(back_0, (scaled[1], scaled[-1]))
    half_0 = halved(back_0)
    back_1 = stream(grads, out_weight, place, piece, piece, (), [half_0[0]])
    back_0 = exchanged(half_0)
    back_1, (back_0, scaled) = tied(back_1, (back_0, scaled))
    in_parts += prepared(3, [back_1[0]])
    half_1 = halved(back_1, in_parts[6])
    back_1 = exchanged(half_1)
    pre_0 = forward(scaled, in_parts[:4], place, (), [half_1[0]])
    pre_1 = forward(scaled, in_parts[4:6], place, (), [pre_0[1], back_1[0]])
    half_0 = halved(pre_0, pre_1)
    pre_1 = forward(scaled, in_parts[6:], place, pre_1, [half_0[0]])
    pre_0 = exchanged(half_0)

    def slope_product(c, back, pre):
        return sum(back) * gelu_slope(sum(pre) + in_bias[c * piece : (c + 1) * piece])

    def spread_out(act):
        mine = [None] * chips
        mine[0] = act
        for step in range(1, chips):
            act = next_chip(act)
            mine[(chips - step) % chips] = act
        return mine

    act_0 = slope_product(0, back_0, pre_0)
    pre_1 = exchanged(halved(pre_1, act_0))
    act_1 = slope_product(1, back_1, pre_1)

    def both_cores(mine):
        return mine + [other_core(block) for block in mine]

    def summed_along_hid(sums):
        return sum([along_hid(sums[step], -step) for step in range(1, hid_size)], start=sums[0])

    acts_0, acts_1 = spread_out(act_0), spread_out(act_1)
    sums = backward(both_cores(acts_0), in_parts[:4], place, (), 0, 1, [pre_1[1]])
    acts_1[1:], sums = tied(acts_1[1:], sums)
    acts_1 = both_cores(acts_1)
    parts = 2 if depth % 512 == 0 else 1
    ends = []
    for part in range(parts):
        ends.append(backward(acts_1, in_parts[4:], place, sums, part, parts, [ends[-1][0] if ends else sums[0]]))
    running = jnp.concatenate([summed_along_hid(end) for end in ends], axis=1)
    normed_grad = running * norm_gain
    totals = lax.psum(
        jnp.stack([jnp.sum(normed_grad, axis=-1), jnp.sum(normed_grad * normed, axis=-1)]), "emb"
    )
    first, second = (totals / model_width)[:, :, None]
    return inv_std * (normed_grad - first - normed * second)


def solution(mesh):
    hid_size, emb_size = mesh.shape["hid"], mesh.shape["emb"]
    assert hid_size == emb_size and emb_size % 2 == 0
    return jax.shard_map(
        functools.partial(body, hid_size, emb_size),
        mesh=mesh,
        in_specs=(
            P(("groups", "hid"), "emb"),
            P(("groups", "hid"), "emb"),
            P("emb", "hid"),
            P("hid"),
            P("hid", "emb"),
            P("emb"),
        ),
        out_specs=P(("groups", "hid"), "emb"),
        check_vma=False,
    )
```

```python
import functools
import math

import jax
import jax.numpy as jnp
from jax import lax
from jax.experimental import pallas as pl
from jax.experimental.pallas import tpu as pltpu
from jax.sharding import PartitionSpec as P

VMEM_LIMIT = 5 * 1024 * 1024
CHUNKS = 2
SHORT = pl.CostEstimate(flops=1 << 20, bytes_accessed=1 << 18, transcendentals=0)


def gelu_slope(values):
    cdf = 0.5 * (1.0 + lax.erf(values * (1.0 / math.sqrt(2.0))))
    density = jnp.exp(-0.5 * values * values) * (1.0 / math.sqrt(2.0 * math.pi))
    return cdf + values * density


def split(values):
    high = values.astype(jnp.bfloat16)
    return high, (values - high.astype(jnp.float32)).astype(jnp.bfloat16)


def divisor(extent, *choices):
    return next(c for c in choices if extent % c == 0)


def call(kernel, out_shape, operands, after):
    outs = out_shape if isinstance(out_shape, tuple) else (out_shape,)

    def run(*refs):
        kernel(*refs[: len(operands)], *refs[len(operands) + len(after) :])

    inside = pl.BlockSpec(memory_space=pltpu.VMEM)
    result = pl.pallas_call(
        run,
        out_shape=tuple(jax.ShapeDtypeStruct(o.shape, o.dtype) for o in outs),
        in_specs=[inside] * len(operands) + [pl.BlockSpec(memory_space=pl.ANY)] * len(after),
        out_specs=[inside] * len(outs),
        compiler_params=pltpu.CompilerParams(vmem_limit_bytes=VMEM_LIMIT),
        cost_estimate=SHORT,
    )(*operands, *after)
    return result if isinstance(out_shape, tuple) else result[0]


def moments_kernel(inputs_ref, out_ref):
    rows, depth = inputs_ref.shape
    mean = jnp.sum(inputs_ref[...], axis=1, keepdims=True) * (1.0 / depth)
    square = jnp.sum(jnp.square(inputs_ref[...] - mean), axis=1, keepdims=True)
    out_ref[:rows] = jnp.broadcast_to(mean, (rows, 128))
    out_ref[rows:] = jnp.broadcast_to(square, (rows, 128))


def merge(moments, count):
    rows = moments[0].shape[0] // 2
    mean = sum(part[:rows] for part in moments) * (1.0 / len(moments))
    square = sum(part[rows:] + count * jnp.square(part[:rows] - mean) for part in moments)
    return mean, square


def merge_kernel(count, first_ref, second_ref, out_ref):
    rows = out_ref.shape[0] // 2
    out_ref[:rows], out_ref[rows:] = merge((first_ref[...], second_ref[...]), count)


def normalise_kernel(count, inputs_ref, gain_ref, *refs):
    *moment_refs, normed_ref, scaled_ref, inv_std_ref = refs
    mean, square = merge([ref[...] for ref in moment_refs], count)
    inv_std = 1.0 / jnp.sqrt(square * (1.0 / (count * len(moment_refs))) + 1e-06)
    normed = (inputs_ref[...] - mean[:, :1]) * inv_std[:, :1]
    normed_ref[...] = normed
    scaled_ref[...] = normed * gain_ref[...]
    inv_std_ref[...] = inv_std


def prepare_kernel(rows, columns, block, depth, weight_ref, *refs):
    high_ref, low_ref, landed, arrived = refs[-4:]
    steps = rows[1] // block

    def fetch(step):
        start = pl.multiple_of(rows[0] + step * block, block)
        slot = lax.rem(step, depth)
        return pltpu.make_async_copy(
            weight_ref.at[pl.ds(start, block), pl.ds(*columns)], landed.at[slot], arrived.at[slot]
        )

    for step in range(min(depth, steps)):
        fetch(step).start()

    @pl.loop(0, steps)
    def _(step):
        fetch(step).wait()
        high, low = split(landed[lax.rem(step, depth)])
        at = pl.ds(pl.multiple_of(step * block, block), block)
        high_ref[at, :] = high
        low_ref[at, :] = low

        @pl.when(step + depth < steps)
        def _():
            fetch(step + depth).start()


def prepare(weight, rows, columns, after):
    block = 256 * 1536 // columns[1]
    block = divisor(rows[1], *[b for b in (256, 128, 64, 32) if b <= max(block, 32)])
    depth = 4
    out = pltpu.VMEM((rows[1], columns[1]), jnp.bfloat16)
    return pl.pallas_call(
        functools.partial(prepare_kernel, rows, columns, block, depth),
        out_shape=(out, out),
        in_specs=[pl.BlockSpec(memory_space=pl.ANY)] * (1 + len(after)),
        out_specs=[pl.BlockSpec(memory_space=pltpu.VMEM)] * 2,
        scratch_shapes=[
            pltpu.VMEM((depth, block, columns[1]), jnp.float32),
            pltpu.SemaphoreType.DMA((depth,)),
        ],
        compiler_params=pltpu.CompilerParams(vmem_limit_bytes=2 * VMEM_LIMIT),
        cost_estimate=SHORT,
    )(pltpu.with_memory_space_constraint(weight, pltpu.HBM), *after)


def three_pass(both, high, low, contract):
    rows = both.shape[0] // 2
    dot = functools.partial(
        lax.dot_general,
        dimension_numbers=(((1,), (contract,)), ((), ())),
        preferred_element_type=jnp.float32,
    )
    first = dot(both[...], high)
    return first[:rows] + first[rows:] + dot(both[:rows, :], low)


def fill(both, block_refs, place_ref):
    total = both.shape[0] // 2
    block = total // place_ref.shape[0]
    index = 0
    for ref in block_refs:
        for start in range(0, ref.shape[0], block):
            high, low = split(ref[start : start + block, :])
            row = pl.multiple_of(place_ref[index] * block, block)
            both[pl.ds(row, block), :] = high
            both[pl.ds(total + row, block), :] = low
            index += 1


def follow(earlier_refs, out_refs):
    for earlier_ref, out_ref in zip(earlier_refs, out_refs):
        out_ref[:, : earlier_ref.shape[1]] = earlier_ref[...]
    return earlier_refs[0].shape[1] if earlier_refs else 0


def forward_kernel(place_ref, slot_refs, weight_refs, earlier_refs, send_ref, keep_ref, both):
    fill(both, slot_refs, place_ref)
    half, column = send_ref.shape[0], follow(earlier_refs, (send_ref, keep_ref))
    for high_ref, low_ref in zip(weight_refs[::2], weight_refs[1::2]):
        width = divisor(high_ref.shape[1], 256, 128)

        @pl.loop(0, high_ref.shape[1] // width, unroll=2)
        def _(step):
            at = pl.ds(pl.multiple_of(step * width, width), width)
            part = three_pass(both, high_ref[:, at], low_ref[:, at], 0)
            at = pl.ds(pl.multiple_of(column + step * width, width), width)
            keep_ref[:, at] = part[:half]
            send_ref[:, at] = part[half:]

        column += high_ref.shape[1]


def forward(slots, weights, place, earlier, after):
    tokens, depth = slots[0].shape[0] * len(slots), slots[0].shape[1]
    hidden = sum(w.shape[1] for w in weights[::2]) + (earlier[0].shape[1] if earlier else 0)
    out = jax.ShapeDtypeStruct((tokens // 2, hidden), jnp.float32)
    inside, anywhere = pl.BlockSpec(memory_space=pltpu.VMEM), pl.BlockSpec(memory_space=pl.ANY)
    ends = [1 + len(slots), 1 + len(slots) + len(weights), 1 + len(slots) + len(weights) + len(earlier)]
    return pl.pallas_call(
        lambda *refs: forward_kernel(
            refs[0], refs[1 : ends[0]], refs[ends[0] : ends[1]], refs[ends[1] : ends[2]], *refs[-3:]
        ),
        out_shape=(out, out),
        in_specs=[pl.BlockSpec(memory_space=pltpu.SMEM)] + [inside] * (ends[2] - 1) + [anywhere] * len(after),
        out_specs=[inside] * 2,
        scratch_shapes=[pltpu.VMEM((2 * tokens, depth), jnp.bfloat16)],
        compiler_params=pltpu.CompilerParams(vmem_limit_bytes=VMEM_LIMIT),
        cost_estimate=SHORT,
    )(place, *slots, *[pltpu.with_memory_space_constraint(w, pltpu.VMEM) for w in weights], *earlier, *after)


def stream_kernel(first, depth, place_ref, slot_refs, weight_ref, earlier_refs, send_ref, keep_ref, both, landed, arrived):
    half = send_ref.shape[0]
    width = landed.shape[1]
    column = follow(earlier_refs, (send_ref, keep_ref))
    steps = (send_ref.shape[1] - column) // width

    def fetch(step):
        start = pl.multiple_of(first + step * width, width)
        slot = lax.rem(step, depth)
        return pltpu.make_async_copy(weight_ref.at[pl.ds(start, width), :], landed.at[slot], arrived.at[slot])

    for step in range(min(depth, steps)):
        fetch(step).start()
    fill(both, slot_refs, place_ref)

    @pl.loop(0, steps)
    def _(step):
        fetch(step).wait()
        high, low = split(landed[lax.rem(step, depth)])
        part = three_pass(both, high, low, 1)
        at = pl.ds(pl.multiple_of(column + step * width, width), width)
        keep_ref[:, at] = part[:half]
        send_ref[:, at] = part[half:]

        @pl.when(step + depth < steps)
        def _():
            fetch(step + depth).start()


def stream(slots, weight, place, first, hidden, earlier, after):
    tokens, columns = slots[0].shape[0] * len(slots), slots[0].shape[1]
    width, depth = divisor(hidden, 256, 128), 4
    out = jax.ShapeDtypeStruct((tokens // 2, hidden + (earlier[0].shape[1] if earlier else 0)), jnp.float32)
    inside, anywhere = pl.BlockSpec(memory_space=pltpu.VMEM), pl.BlockSpec(memory_space=pl.ANY)
    last = 1 + len(slots)
    return pl.pallas_call(
        lambda *refs: stream_kernel(
            first, depth, refs[0], refs[1:last], refs[last], refs[last + 1 : last + 1 + len(earlier)], *refs[-5:]
        ),
        out_shape=(out, out),
        in_specs=[pl.BlockSpec(memory_space=pltpu.SMEM)]
        + [inside] * len(slots)
        + [anywhere]
        + [inside] * len(earlier)
        + [anywhere] * len(after),
        out_specs=[inside] * 2,
        scratch_shapes=[
            pltpu.VMEM((2 * tokens, columns), jnp.bfloat16),
            pltpu.VMEM((depth, width, columns), jnp.float32),
            pltpu.SemaphoreType.DMA((depth,)),
        ],
        compiler_params=pltpu.CompilerParams(vmem_limit_bytes=2 * VMEM_LIMIT),
        cost_estimate=SHORT,
    )(place, *slots, pltpu.with_memory_space_constraint(weight, pltpu.HBM), *earlier, *after)


def backward_kernel(slots, pieces, earlier, first_column, place_ref, *refs):
    act_refs, weight_refs = refs[:slots], refs[slots : slots + 2 * pieces]
    earlier_refs = refs[slots + 2 * pieces : slots + 2 * pieces + earlier]
    out_refs = refs[-2 - slots : -2]
    both, result = refs[-2:]
    block = act_refs[0].shape[0]
    total = block * slots
    for p in range(slots):
        high, low = split(act_refs[p][...])
        both[p * block : (p + 1) * block, :] = high
        both[total + p * block : total + (p + 1) * block, :] = low

    depth = out_refs[0].shape[1]
    width = result.shape[1]

    @pl.loop(0, depth // width)
    def _(step):
        start = pl.multiple_of(step * width, width)
        tile = (pl.ds(pl.multiple_of(first_column + start, width), width), slice(None))
        total_sum, column = 0.0, 0
        for high_ref, low_ref in zip(weight_refs[::2], weight_refs[1::2]):
            columns = slice(column, column + high_ref.shape[1])
            total_sum += three_pass(both[:, columns], high_ref[tile], low_ref[tile], 1)
            column = columns.stop
        result[...] = total_sum
        for b in range(slots):
            row = pl.multiple_of(place_ref[b] * block, block)
            rows = result[pl.ds(row, block), :]
            if earlier:
                rows = rows + earlier_refs[b][:, pl.ds(pl.multiple_of(first_column + start, width), width)]
            out_refs[b][:, pl.ds(start, width)] = rows


def backward(acts, weights, place, earlier, part, parts, after):
    slots, (block, hidden) = len(acts), acts[0].shape
    depth = weights[0].shape[0] // parts
    width = divisor(depth, 256, 128)
    out = jax.ShapeDtypeStruct((block, depth), jnp.float32)
    inside = pl.BlockSpec(memory_space=pltpu.VMEM)
    return pl.pallas_call(
        functools.partial(backward_kernel, slots, len(weights) // 2, len(earlier), part * depth),
        out_shape=[out] * slots,
        in_specs=[pl.BlockSpec(memory_space=pltpu.SMEM)]
        + [inside] * (slots + len(weights) + len(earlier))
        + [pl.BlockSpec(memory_space=pl.ANY)] * len(after),
        out_specs=[inside] * slots,
        scratch_shapes=[
            pltpu.VMEM((2 * block * slots, hidden), jnp.bfloat16),
            pltpu.VMEM((block * slots, width), jnp.float32),
        ],
        compiler_params=pltpu.CompilerParams(vmem_limit_bytes=VMEM_LIMIT),
        cost_estimate=SHORT,
    )(place, *acts, *[pltpu.with_memory_space_constraint(part, pltpu.VMEM) for part in weights], *earlier, *after)


def body(hid_size, emb_size, inputs, out_grad, in_weight, in_bias, out_weight, norm_gain):
    chips = emb_size // 2
    tokens, depth = inputs.shape
    model_width = depth * emb_size
    hidden = in_weight.shape[1]
    me = lax.axis_index("emb")
    chip, core = me // 2, me % 2

    def along_hid(values, steps=1):
        return lax.ppermute(values, "hid", [(i, (i + steps) % hid_size) for i in range(hid_size)])

    def other_core(values):
        return lax.ppermute(values, "emb", [(i, i ^ 1) for i in range(emb_size)])

    def next_chip(values):
        return lax.ppermute(values, "emb", [(i, (i + 2) % emb_size) for i in range(emb_size)])

    owner = jnp.arange(emb_size, dtype=jnp.int32)
    place = ((owner % 2) ^ core) * chips + (owner // 2 - chip) % chips

    def gathered(values):
        return [values] + [along_hid(values, step) for step in range(1, hid_size)]

    grads = gathered(out_grad)
    piece = hidden // CHUNKS
    quarter = piece // 2

    def tied(values, others):
        return lax.optimization_barrier((values, others))

    def halved(partial, behind=()):
        (send_own, send), (keep_own, keep) = [(rows[:tokens], rows[tokens:]) for rows in partial]
        return keep + tied(other_core(send), behind)[0], (keep_own, other_core(send_own))

    def exchanged(half):
        summed, own = half
        terms = [summed[d * tokens : (d + 1) * tokens] for d in range(chips - 1)]
        arrival = next_chip(terms[chips - 2])
        for step in range(chips - 3, -1, -1):
            arrival = next_chip(arrival + terms[step])
        return arrival, *own

    def prepared(c, after):
        return prepare(in_weight, (0, depth), (c * quarter, quarter), after)

    moments = call(moments_kernel, jax.ShapeDtypeStruct((2 * tokens, 128), jnp.float32), (inputs,), ())
    in_parts = prepared(0, [place, moments])
    in_parts += prepared(1, [in_parts[0]])
    moments = call(
        functools.partial(merge_kernel, depth), moments, (moments, other_core(moments)), (in_parts[2], *grads[1:])
    )
    parts = [moments]
    for _ in range(1, chips):
        parts.append(next_chip(parts[-1]))
    normed, scaled, inv_std = call(
        functools.partial(normalise_kernel, 2 * depth),
        (inputs, inputs, jax.ShapeDtypeStruct((tokens, 128), jnp.float32)),
        (inputs, norm_gain[None, :], *parts),
        (),
    )
    inv_std = inv_std[:, :1]
    scaled = gathered(scaled)
    back_0 = stream(grads, out_weight, place, 0, piece, (), [scaled[0]])
    back_0, (scaled[1], scaled[-1]) = tied(back_0, (scaled[1], scaled[-1]))
    half_0 = halved(back_0)
    back_1 = stream(grads, out_weight, place, piece, piece, (), [half_0[0]])
    back_0 = exchanged(half_0)
    back_1, (back_0, scaled) = tied(back_1, (back_0, scaled))
    in_parts += prepared(2, [back_1[0]])
    half_1 = halved(back_1, in_parts[4])
    back_1 = exchanged(half_1)
    pre_0 = forward(scaled, in_parts[:4], place, (), [half_1[0]])
    in_parts += prepared(3, [pre_0[1]])
    half_0 = halved(pre_0, (in_parts[6], back_1[0]))
    pre_1 = forward(scaled, in_parts[4:], place, (), [half_0[0]])
    pre_0 = exchanged(half_0)

    def slope_product(c, back, pre):
        return sum(back) * gelu_slope(sum(pre) + in_bias[c * piece : (c + 1) * piece])

    def spread_out(act):
        mine = [None] * chips
        mine[0] = act
        for step in range(1, chips):
            act = next_chip(act)
            mine[(chips - step) % chips] = act
        return mine

    act_0 = slope_product(0, back_0, pre_0)
    pre_1 = exchanged(halved(pre_1, act_0))
    act_1 = slope_product(1, back_1, pre_1)

    def both_cores(mine):
        return mine + [other_core(block) for block in mine]

    def summed_along_hid(sums):
        return sum([along_hid(sums[step], -step) for step in range(1, hid_size)], start=sums[0])

    acts_0, acts_1 = spread_out(act_0), spread_out(act_1)
    sums = backward(both_cores(acts_0), in_parts[:4], place, (), 0, 1, [pre_1[1]])
    acts_1[1:], sums = tied(acts_1[1:], sums)
    acts_1 = both_cores(acts_1)
    parts = 2 if depth % 512 == 0 else 1
    ends = []
    for part in range(parts):
        ends.append(backward(acts_1, in_parts[4:], place, sums, part, parts, [ends[-1][0] if ends else sums[0]]))
    running = jnp.concatenate([summed_along_hid(end) for end in ends], axis=1)
    normed_grad = running * norm_gain
    totals = lax.psum(
        jnp.stack([jnp.sum(normed_grad, axis=-1), jnp.sum(normed_grad * normed, axis=-1)]), "emb"
    )
    first, second = (totals / model_width)[:, :, None]
    return inv_std * (normed_grad - first - normed * second)


def solution(mesh):
    hid_size, emb_size = mesh.shape["hid"], mesh.shape["emb"]
    assert hid_size == emb_size and emb_size % 2 == 0
    return jax.shard_map(
        functools.partial(body, hid_size, emb_size),
        mesh=mesh,
        in_specs=(
            P(("groups", "hid"), "emb"),
            P(("groups", "hid"), "emb"),
            P("emb", "hid"),
            P("hid"),
            P("hid", "emb"),
            P("emb"),
        ),
        out_specs=P(("groups", "hid"), "emb"),
        check_vma=False,
    )
```

```python
import functools
import math

import jax
import jax.numpy as jnp
from jax import lax
from jax.experimental import pallas as pl
from jax.experimental.pallas import tpu as pltpu
from jax.sharding import PartitionSpec as P

VMEM_LIMIT = 5 * 1024 * 1024
SHORT = pl.CostEstimate(flops=1 << 20, bytes_accessed=1 << 18, transcendentals=0)


def gelu_slope(values):
    cdf = 0.5 * (1.0 + lax.erf(values * (1.0 / math.sqrt(2.0))))
    density = jnp.exp(-0.5 * values * values) * (1.0 / math.sqrt(2.0 * math.pi))
    return cdf + values * density


def split(values):
    high = values.astype(jnp.bfloat16)
    return high, (values - high.astype(jnp.float32)).astype(jnp.bfloat16)


def divisor(extent, *choices):
    return next(c for c in choices if extent % c == 0)


def call(kernel, out_shape, operands, after):
    outs = out_shape if isinstance(out_shape, tuple) else (out_shape,)

    def run(*refs):
        kernel(*refs[: len(operands)], *refs[len(operands) + len(after) :])

    inside = pl.BlockSpec(memory_space=pltpu.VMEM)
    result = pl.pallas_call(
        run,
        out_shape=tuple(jax.ShapeDtypeStruct(o.shape, o.dtype) for o in outs),
        in_specs=[inside] * len(operands) + [pl.BlockSpec(memory_space=pl.ANY)] * len(after),
        out_specs=[inside] * len(outs),
        compiler_params=pltpu.CompilerParams(vmem_limit_bytes=VMEM_LIMIT),
        cost_estimate=SHORT,
    )(*operands, *after)
    return result if isinstance(out_shape, tuple) else result[0]


def moments_kernel(inputs_ref, out_ref):
    rows, depth = inputs_ref.shape
    mean = jnp.sum(inputs_ref[...], axis=1, keepdims=True) * (1.0 / depth)
    square = jnp.sum(jnp.square(inputs_ref[...] - mean), axis=1, keepdims=True)
    out_ref[:rows] = jnp.broadcast_to(mean, (rows, 128))
    out_ref[rows:] = jnp.broadcast_to(square, (rows, 128))


def merge(moments, count):
    rows = moments[0].shape[0] // 2
    mean = sum(part[:rows] for part in moments) * (1.0 / len(moments))
    square = sum(part[rows:] + count * jnp.square(part[:rows] - mean) for part in moments)
    return mean, square


def merge_kernel(count, first_ref, second_ref, out_ref):
    rows = out_ref.shape[0] // 2
    out_ref[:rows], out_ref[rows:] = merge((first_ref[...], second_ref[...]), count)


def normalise_kernel(count, inputs_ref, gain_ref, *refs):
    *moment_refs, normed_ref, scaled_ref, inv_std_ref = refs
    mean, square = merge([ref[...] for ref in moment_refs], count)
    inv_std = 1.0 / jnp.sqrt(square * (1.0 / (count * len(moment_refs))) + 1e-06)
    normed = (inputs_ref[...] - mean[:, :1]) * inv_std[:, :1]
    normed_ref[...] = normed
    scaled_ref[...] = normed * gain_ref[...]
    inv_std_ref[...] = inv_std


def prepare_kernel(rows, columns, block, depth, weight_ref, *refs):
    *part_refs, landed, arrived = refs
    width = part_refs[0].shape[1]
    steps = rows[1] // block

    def fetch(step):
        start = pl.multiple_of(rows[0] + step * block, block)
        slot = lax.rem(step, depth)
        return pltpu.make_async_copy(
            weight_ref.at[pl.ds(start, block), pl.ds(*columns)], landed.at[slot], arrived.at[slot]
        )

    for step in range(min(depth, steps)):
        fetch(step).start()

    @pl.loop(0, steps)
    def _(step):
        fetch(step).wait()
        high, low = split(landed[lax.rem(step, depth)])
        at = pl.ds(pl.multiple_of(step * block, block), block)
        for n, part_ref in enumerate(part_refs):
            part_ref[at, :] = (low if n % 2 else high)[:, n // 2 * width : (n // 2 + 1) * width]

        @pl.when(step + depth < steps)
        def _():
            fetch(step + depth).start()


def prepare(weight, rows, columns, after):
    block = divisor(rows[1], *[b for b in (256, 128, 64, 32) if b <= max(256 * 1536 // columns[1], 32)])
    depth = 4
    outs = (pltpu.VMEM((rows[1], columns[1] // 2), jnp.bfloat16),) * 4
    anywhere = pl.BlockSpec(memory_space=pl.ANY)
    return pl.pallas_call(
        lambda weight_ref, *refs: prepare_kernel(rows, columns, block, depth, weight_ref, *refs[len(after) :]),
        out_shape=outs,
        in_specs=[anywhere] * (1 + len(after)),
        out_specs=[pl.BlockSpec(memory_space=pltpu.VMEM)] * 4,
        scratch_shapes=[
            pltpu.VMEM((depth, block, columns[1]), jnp.float32),
            pltpu.SemaphoreType.DMA((depth,)),
        ],
        compiler_params=pltpu.CompilerParams(vmem_limit_bytes=VMEM_LIMIT),
        cost_estimate=SHORT,
    )(pltpu.with_memory_space_constraint(weight, pltpu.HBM), *after)


def three_pass(both, high, low, contract):
    rows = both.shape[0] // 2
    dot = functools.partial(
        lax.dot_general,
        dimension_numbers=(((1,), (contract,)), ((), ())),
        preferred_element_type=jnp.float32,
    )
    first = dot(both[...], high)
    return first[:rows] + first[rows:] + dot(both[:rows, :], low)


def fill(both, block_refs, place_ref):
    total = both.shape[0] // 2
    block = total // place_ref.shape[0]
    index = 0
    for ref in block_refs:
        for start in range(0, ref.shape[0], block):
            high, low = split(ref[start : start + block, :])
            row = pl.multiple_of(place_ref[index] * block, block)
            both[pl.ds(row, block), :] = high
            both[pl.ds(total + row, block), :] = low
            index += 1


def follow(earlier_refs, out_refs):
    for earlier_ref, out_ref in zip(earlier_refs, out_refs):
        out_ref[:, : earlier_ref.shape[1]] = earlier_ref[...]
    return earlier_refs[0].shape[1] if earlier_refs else 0


def forward_kernel(place_ref, slot_refs, weight_refs, earlier_refs, send_ref, keep_ref, both):
    fill(both, slot_refs, place_ref)
    half, column = send_ref.shape[0], follow(earlier_refs, (send_ref, keep_ref))
    for high_ref, low_ref in zip(weight_refs[::2], weight_refs[1::2]):
        width = divisor(high_ref.shape[1], 256, 128)

        @pl.loop(0, high_ref.shape[1] // width, unroll=2)
        def _(step):
            at = pl.ds(pl.multiple_of(step * width, width), width)
            part = three_pass(both, high_ref[:, at], low_ref[:, at], 0)
            at = pl.ds(pl.multiple_of(column + step * width, width), width)
            keep_ref[:, at] = part[:half]
            send_ref[:, at] = part[half:]

        column += high_ref.shape[1]


def forward(slots, weights, place, earlier, after):
    tokens, depth = slots[0].shape[0] * len(slots), slots[0].shape[1]
    hidden = sum(w.shape[1] for w in weights[::2]) + (earlier[0].shape[1] if earlier else 0)
    out = jax.ShapeDtypeStruct((tokens // 2, hidden), jnp.float32)
    inside, anywhere = pl.BlockSpec(memory_space=pltpu.VMEM), pl.BlockSpec(memory_space=pl.ANY)
    ends = [1 + len(slots), 1 + len(slots) + len(weights), 1 + len(slots) + len(weights) + len(earlier)]
    return pl.pallas_call(
        lambda *refs: forward_kernel(
            refs[0], refs[1 : ends[0]], refs[ends[0] : ends[1]], refs[ends[1] : ends[2]], *refs[-3:]
        ),
        out_shape=(out, out),
        in_specs=[pl.BlockSpec(memory_space=pltpu.SMEM)] + [inside] * (ends[2] - 1) + [anywhere] * len(after),
        out_specs=[inside] * 2,
        scratch_shapes=[pltpu.VMEM((2 * tokens, depth), jnp.bfloat16)],
        compiler_params=pltpu.CompilerParams(vmem_limit_bytes=VMEM_LIMIT),
        cost_estimate=SHORT,
    )(place, *slots, *[pltpu.with_memory_space_constraint(w, pltpu.VMEM) for w in weights], *earlier, *after)


def stream_kernel(first, depth, place_ref, slot_refs, weight_ref, earlier_refs, send_ref, keep_ref, both, landed, arrived):
    half = send_ref.shape[0]
    width = landed.shape[1]
    column = follow(earlier_refs, (send_ref, keep_ref))
    steps = (send_ref.shape[1] - column) // width

    def fetch(step):
        start = pl.multiple_of(first + step * width, width)
        slot = lax.rem(step, depth)
        return pltpu.make_async_copy(weight_ref.at[pl.ds(start, width), :], landed.at[slot], arrived.at[slot])

    for step in range(min(depth, steps)):
        fetch(step).start()
    fill(both, slot_refs, place_ref)

    @pl.loop(0, steps)
    def _(step):
        fetch(step).wait()
        high, low = split(landed[lax.rem(step, depth)])
        part = three_pass(both, high, low, 1)
        at = pl.ds(pl.multiple_of(column + step * width, width), width)
        keep_ref[:, at] = part[:half]
        send_ref[:, at] = part[half:]

        @pl.when(step + depth < steps)
        def _():
            fetch(step + depth).start()


def stream(slots, weight, place, first, hidden, earlier, after):
    tokens, columns = slots[0].shape[0] * len(slots), slots[0].shape[1]
    width, depth = divisor(hidden, 256, 128), 4
    out = jax.ShapeDtypeStruct((tokens // 2, hidden + (earlier[0].shape[1] if earlier else 0)), jnp.float32)
    inside, anywhere = pl.BlockSpec(memory_space=pltpu.VMEM), pl.BlockSpec(memory_space=pl.ANY)
    last = 1 + len(slots)
    return pl.pallas_call(
        lambda *refs: stream_kernel(
            first, depth, refs[0], refs[1:last], refs[last], refs[last + 1 : last + 1 + len(earlier)], *refs[-5:]
        ),
        out_shape=(out, out),
        in_specs=[pl.BlockSpec(memory_space=pltpu.SMEM)]
        + [inside] * len(slots)
        + [anywhere]
        + [inside] * len(earlier)
        + [anywhere] * len(after),
        out_specs=[inside] * 2,
        scratch_shapes=[
            pltpu.VMEM((2 * tokens, columns), jnp.bfloat16),
            pltpu.VMEM((depth, width, columns), jnp.float32),
            pltpu.SemaphoreType.DMA((depth,)),
        ],
        compiler_params=pltpu.CompilerParams(vmem_limit_bytes=8 * 1024 * 1024),
        cost_estimate=SHORT,
    )(place, *slots, pltpu.with_memory_space_constraint(weight, pltpu.HBM), *earlier, *after)


def backward_kernel(slots, pieces, earlier, first_column, place_ref, *refs):
    act_refs, weight_refs = refs[:slots], refs[slots : slots + 2 * pieces]
    earlier_refs = refs[slots + 2 * pieces : slots + 2 * pieces + earlier]
    out_refs = refs[-2 - slots : -2]
    both, result = refs[-2:]
    block = act_refs[0].shape[0]
    total = block * slots
    for p in range(slots):
        high, low = split(act_refs[p][...])
        both[p * block : (p + 1) * block, :] = high
        both[total + p * block : total + (p + 1) * block, :] = low

    depth = out_refs[0].shape[1]
    width = result.shape[1]

    @pl.loop(0, depth // width)
    def _(step):
        start = pl.multiple_of(step * width, width)
        tile = (pl.ds(pl.multiple_of(first_column + start, width), width), slice(None))
        total_sum, column = 0.0, 0
        for high_ref, low_ref in zip(weight_refs[::2], weight_refs[1::2]):
            columns = slice(column, column + high_ref.shape[1])
            total_sum += three_pass(both[:, columns], high_ref[tile], low_ref[tile], 1)
            column = columns.stop
        result[...] = total_sum
        for b in range(slots):
            row = pl.multiple_of(place_ref[b] * block, block)
            rows = result[pl.ds(row, block), :]
            if earlier:
                rows = rows + earlier_refs[b][:, pl.ds(pl.multiple_of(first_column + start, width), width)]
            out_refs[b][:, pl.ds(start, width)] = rows


def backward(acts, weights, place, earlier, part, parts, after):
    slots, (block, hidden) = len(acts), acts[0].shape
    depth = weights[0].shape[0] // parts
    width = divisor(depth, 256, 128)
    out = jax.ShapeDtypeStruct((block, depth), jnp.float32)
    inside = pl.BlockSpec(memory_space=pltpu.VMEM)
    return pl.pallas_call(
        functools.partial(backward_kernel, slots, len(weights) // 2, len(earlier), part * depth),
        out_shape=[out] * slots,
        in_specs=[pl.BlockSpec(memory_space=pltpu.SMEM)]
        + [inside] * (slots + len(weights) + len(earlier))
        + [pl.BlockSpec(memory_space=pl.ANY)] * len(after),
        out_specs=[inside] * slots,
        scratch_shapes=[
            pltpu.VMEM((2 * block * slots, hidden), jnp.bfloat16),
            pltpu.VMEM((block * slots, width), jnp.float32),
        ],
        compiler_params=pltpu.CompilerParams(vmem_limit_bytes=VMEM_LIMIT),
        cost_estimate=SHORT,
    )(place, *acts, *[pltpu.with_memory_space_constraint(part, pltpu.VMEM) for part in weights], *earlier, *after)


def body(hid_size, emb_size, inputs, out_grad, in_weight, in_bias, out_weight, norm_gain):
    chips = emb_size // 2
    tokens, depth = inputs.shape
    model_width = depth * emb_size
    hidden = in_weight.shape[1]
    me = lax.axis_index("emb")
    chip, core = me // 2, me % 2

    def along_hid(values, steps=1):
        return lax.ppermute(values, "hid", [(i, (i + steps) % hid_size) for i in range(hid_size)])

    def other_core(values):
        return lax.ppermute(values, "emb", [(i, i ^ 1) for i in range(emb_size)])

    def next_chip(values):
        return lax.ppermute(values, "emb", [(i, (i + 2) % emb_size) for i in range(emb_size)])

    owner = jnp.arange(emb_size, dtype=jnp.int32)
    place = ((owner % 2) ^ core) * chips + (owner // 2 - chip) % chips

    def gathered(values):
        return [values] + [along_hid(values, step) for step in range(1, hid_size)]

    def relayed(values):
        blocks = [values] + [None] * (hid_size - 1)
        for step in range(1, hid_size // 2 + 1):
            blocks[step] = along_hid(blocks[step - 1], 1)
        for step in range(1, hid_size - hid_size // 2):
            blocks[-step] = along_hid(blocks[(1 - step) % hid_size], -1)
        return blocks

    grads = gathered(out_grad)
    third = hidden // 3

    def tied(values, others):
        return lax.optimization_barrier((values, others))

    def halved(partial, behind=()):
        (send_own, send), (keep_own, keep) = [(rows[:tokens], rows[tokens:]) for rows in partial]
        return keep + tied(other_core(send), behind)[0], (keep_own, other_core(send_own))

    def exchanged(half):
        summed, own = half
        terms = [summed[d * tokens : (d + 1) * tokens] for d in range(chips - 1)]
        arrival = next_chip(terms[chips - 2])
        for step in range(chips - 3, -1, -1):
            arrival = next_chip(arrival + terms[step])
        return arrival, *own

    def prepared(c, after):
        return prepare(in_weight, (0, depth), (c * third, third), after)

    moments = call(moments_kernel, jax.ShapeDtypeStruct((2 * tokens, 128), jnp.float32), (inputs,), ())
    in_parts = prepared(0, [place, moments])
    in_parts += prepared(1, [in_parts[0]])
    moments = call(
        functools.partial(merge_kernel, depth), moments, (moments, other_core(moments)), (in_parts[4], *grads[:0:-1])
    )
    parts = [moments]
    for _ in range(1, chips):
        parts.append(next_chip(parts[-1]))
    normed, scaled, inv_std = call(
        functools.partial(normalise_kernel, 2 * depth),
        (inputs, inputs, jax.ShapeDtypeStruct((tokens, 128), jnp.float32)),
        (inputs, norm_gain[None, :], *parts),
        (),
    )
    inv_std = inv_std[:, :1]
    scaled = relayed(scaled)
    back_0 = stream(grads, out_weight, place, 0, 2 * third, (), [scaled[0]])
    back_0, (scaled[1], scaled[-1]) = tied(back_0, (scaled[1], scaled[-1]))
    half_0 = halved(back_0)
    back_1 = stream(grads, out_weight, place, 2 * third, third, (), [half_0[0]])
    back_0 = exchanged(half_0)
    back_1, scaled = tied(back_1, scaled)
    pre_0 = forward(scaled, in_parts[:8], place, (), [back_1[0]])
    half_1 = halved(back_1, (pre_0, back_0[0]))
    back_1 = exchanged(half_1)
    in_parts += prepared(2, [pre_0[1], half_1[0]])
    half_0 = halved(pre_0, (in_parts[8], back_1[0]))
    pre_1 = forward(scaled, in_parts[8:], place, (), [half_0[0]])
    pre_0 = exchanged(half_0)

    def slope_product(bias, back, pre):
        return sum(back) * gelu_slope(sum(pre) + bias)

    def spread_out(act):
        mine = [None] * chips
        mine[0] = act
        for step in range(1, chips):
            act = next_chip(act)
            mine[(chips - step) % chips] = act
        return mine

    act_0 = slope_product(in_bias[: 2 * third], back_0, pre_0)
    pre_1 = exchanged(halved(pre_1, act_0))
    act_1 = slope_product(in_bias[2 * third :], back_1, pre_1)

    def both_cores(mine):
        return mine + [other_core(block) for block in mine]

    def summed_along_hid(sums):
        return sum([along_hid(sums[step], -step) for step in range(1, hid_size)], start=sums[0])

    acts_0, acts_1 = spread_out(act_0), spread_out(act_1)
    sums = backward(both_cores(acts_0), in_parts[:8], place, (), 0, 1, [pre_1[1]])
    acts_1[1:], sums = tied(acts_1[1:], sums)
    acts_1 = both_cores(acts_1)
    parts = 2 if depth % 512 == 0 else 1
    ends = []
    for part in range(parts):
        ends.append(backward(acts_1, in_parts[8:], place, sums, part, parts, [ends[-1][0] if ends else sums[0]]))
    running = jnp.concatenate([summed_along_hid(end) for end in ends], axis=1)
    normed_grad = running * norm_gain
    totals = lax.psum(
        jnp.stack([jnp.sum(normed_grad, axis=-1), jnp.sum(normed_grad * normed, axis=-1)]), "emb"
    )
    first, second = (totals / model_width)[:, :, None]
    return inv_std * (normed_grad - first - normed * second)


def solution(mesh):
    hid_size, emb_size = mesh.shape["hid"], mesh.shape["emb"]
    assert hid_size == emb_size and emb_size % 2 == 0
    return jax.shard_map(
        functools.partial(body, hid_size, emb_size),
        mesh=mesh,
        in_specs=(
            P(("groups", "hid"), "emb"),
            P(("groups", "hid"), "emb"),
            P("emb", "hid"),
            P("hid"),
            P("hid", "emb"),
            P("emb"),
        ),
        out_specs=P(("groups", "hid"), "emb"),
        check_vma=False,
    )
```

```python
import functools
import math

import jax
import jax.numpy as jnp
from jax import lax
from jax.experimental import pallas as pl
from jax.experimental.pallas import tpu as pltpu
from jax.sharding import PartitionSpec as P

VMEM_LIMIT = 5 * 1024 * 1024
SHORT = pl.CostEstimate(flops=1 << 20, bytes_accessed=1 << 18, transcendentals=0)


def gelu_slope(values):
    cdf = 0.5 * (1.0 + lax.erf(values * (1.0 / math.sqrt(2.0))))
    density = jnp.exp(-0.5 * values * values) * (1.0 / math.sqrt(2.0 * math.pi))
    return cdf + values * density


def split(values):
    high = values.astype(jnp.bfloat16)
    return high, (values - high.astype(jnp.float32)).astype(jnp.bfloat16)


def divisor(extent, *choices):
    return next(c for c in choices if extent % c == 0)


def call(kernel, out_shape, operands, after):
    outs = out_shape if isinstance(out_shape, tuple) else (out_shape,)

    def run(*refs):
        kernel(*refs[: len(operands)], *refs[len(operands) + len(after) :])

    inside = pl.BlockSpec(memory_space=pltpu.VMEM)
    result = pl.pallas_call(
        run,
        out_shape=tuple(jax.ShapeDtypeStruct(o.shape, o.dtype) for o in outs),
        in_specs=[inside] * len(operands) + [pl.BlockSpec(memory_space=pl.ANY)] * len(after),
        out_specs=[inside] * len(outs),
        compiler_params=pltpu.CompilerParams(vmem_limit_bytes=VMEM_LIMIT),
        cost_estimate=SHORT,
    )(*operands, *after)
    return result if isinstance(out_shape, tuple) else result[0]


def moments_kernel(inputs_ref, out_ref):
    rows, depth = inputs_ref.shape
    mean = jnp.sum(inputs_ref[...], axis=1, keepdims=True) * (1.0 / depth)
    square = jnp.sum(jnp.square(inputs_ref[...] - mean), axis=1, keepdims=True)
    out_ref[:rows] = jnp.broadcast_to(mean, (rows, 128))
    out_ref[rows:] = jnp.broadcast_to(square, (rows, 128))


def merge(moments, count):
    rows = moments[0].shape[0] // 2
    mean = sum(part[:rows] for part in moments) * (1.0 / len(moments))
    square = sum(part[rows:] + count * jnp.square(part[:rows] - mean) for part in moments)
    return mean, square


def merge_kernel(count, first_ref, second_ref, out_ref):
    rows = out_ref.shape[0] // 2
    out_ref[:rows], out_ref[rows:] = merge((first_ref[...], second_ref[...]), count)


def normalise_kernel(count, inputs_ref, gain_ref, *refs):
    *moment_refs, normed_ref, scaled_ref, inv_std_ref = refs
    mean, square = merge([ref[...] for ref in moment_refs], count)
    inv_std = 1.0 / jnp.sqrt(square * (1.0 / (count * len(moment_refs))) + 1e-06)
    normed = (inputs_ref[...] - mean[:, :1]) * inv_std[:, :1]
    normed_ref[...] = normed
    scaled_ref[...] = normed * gain_ref[...]
    inv_std_ref[...] = inv_std


def prepare_kernel(rows, columns, block, depth, weight_ref, *refs):
    *part_refs, landed, arrived = refs
    width = part_refs[0].shape[1]
    steps = rows[1] // block

    def fetch(step):
        start = pl.multiple_of(rows[0] + step * block, block)
        slot = lax.rem(step, depth)
        return pltpu.make_async_copy(
            weight_ref.at[pl.ds(start, block), pl.ds(*columns)], landed.at[slot], arrived.at[slot]
        )

    for step in range(min(depth, steps)):
        fetch(step).start()

    @pl.loop(0, steps)
    def _(step):
        fetch(step).wait()
        high, low = split(landed[lax.rem(step, depth)])
        at = pl.ds(pl.multiple_of(step * block, block), block)
        for n, part_ref in enumerate(part_refs):
            part_ref[at, :] = (low if n % 2 else high)[:, n // 2 * width : (n // 2 + 1) * width]

        @pl.when(step + depth < steps)
        def _():
            fetch(step + depth).start()


def prepare(weight, rows, columns, after):
    block = divisor(rows[1], *[b for b in (256, 128, 64, 32) if b <= max(256 * 1536 // columns[1], 32)])
    depth = 4
    outs = (pltpu.VMEM((rows[1], columns[1] // 2), jnp.bfloat16),) * 4
    anywhere = pl.BlockSpec(memory_space=pl.ANY)
    return pl.pallas_call(
        lambda weight_ref, *refs: prepare_kernel(rows, columns, block, depth, weight_ref, *refs[len(after) :]),
        out_shape=outs,
        in_specs=[anywhere] * (1 + len(after)),
        out_specs=[pl.BlockSpec(memory_space=pltpu.VMEM)] * 4,
        scratch_shapes=[
            pltpu.VMEM((depth, block, columns[1]), jnp.float32),
            pltpu.SemaphoreType.DMA((depth,)),
        ],
        compiler_params=pltpu.CompilerParams(vmem_limit_bytes=VMEM_LIMIT),
        cost_estimate=SHORT,
    )(pltpu.with_memory_space_constraint(weight, pltpu.HBM), *after)


def three_pass(both, high, low, contract):
    rows = both.shape[0] // 2
    dot = functools.partial(
        lax.dot_general,
        dimension_numbers=(((1,), (contract,)), ((), ())),
        preferred_element_type=jnp.float32,
    )
    first = dot(both[...], high)
    return first[:rows] + first[rows:] + dot(both[:rows, :], low)


def fill(both, block_refs, place_ref, rows):
    first, count = rows
    total = both.shape[0] // 2
    for index, ref in enumerate(block_refs):
        high, low = split(ref[first : first + count, :])
        row = pl.multiple_of(place_ref[index] * count, count)
        both[pl.ds(row, count), :] = high
        both[pl.ds(total + row, count), :] = low


def follow(earlier_refs, out_refs):
    for earlier_ref, out_ref in zip(earlier_refs, out_refs):
        out_ref[:, : earlier_ref.shape[1]] = earlier_ref[...]
    return earlier_refs[0].shape[1] if earlier_refs else 0


def put(out_refs, at, value):
    row = 0
    for out_ref in out_refs:
        out_ref[:, at] = value[row : row + out_ref.shape[0]]
        row += out_ref.shape[0]


def parts_of(tokens, chips, hidden):
    block = tokens // (2 * chips)
    return [jax.ShapeDtypeStruct((n, hidden), jnp.float32) for n in (block, block * (chips - 1))] * 2


def forward_kernel(rows, place_ref, slot_refs, weight_refs, earlier_refs, out_refs, both):
    fill(both, slot_refs, place_ref, rows)
    column = follow(earlier_refs, out_refs)
    for high_ref, low_ref in zip(weight_refs[::2], weight_refs[1::2]):
        width = divisor(high_ref.shape[1], 256, 128)

        @pl.loop(0, high_ref.shape[1] // width, unroll=2)
        def _(step):
            at = pl.ds(pl.multiple_of(step * width, width), width)
            part = three_pass(both, high_ref[:, at], low_ref[:, at], 0)
            put(out_refs, pl.ds(pl.multiple_of(column + step * width, width), width), part)

        column += high_ref.shape[1]


def forward(slots, rows, weights, place, earlier, after):
    tokens, depth = rows[1] * len(slots), slots[0].shape[1]
    hidden = sum(w.shape[1] for w in weights[::2]) + (earlier[0].shape[1] if earlier else 0)
    inside, anywhere = pl.BlockSpec(memory_space=pltpu.VMEM), pl.BlockSpec(memory_space=pl.ANY)
    ends = [1 + len(slots), 1 + len(slots) + len(weights), 1 + len(slots) + len(weights) + len(earlier)]
    return pl.pallas_call(
        lambda *refs: forward_kernel(
            rows, refs[0], refs[1 : ends[0]], refs[ends[0] : ends[1]], refs[ends[1] : ends[2]], refs[-5:-1], refs[-1]
        ),
        out_shape=parts_of(tokens, len(slots) // 2, hidden),
        in_specs=[pl.BlockSpec(memory_space=pltpu.SMEM)] + [inside] * (ends[2] - 1) + [anywhere] * len(after),
        out_specs=[inside] * 4,
        scratch_shapes=[pltpu.VMEM((2 * tokens, depth), jnp.bfloat16)],
        compiler_params=pltpu.CompilerParams(vmem_limit_bytes=VMEM_LIMIT),
        cost_estimate=SHORT,
    )(place, *slots, *[pltpu.with_memory_space_constraint(w, pltpu.VMEM) for w in weights], *earlier, *after)


def stream_kernel(first, depth, place_ref, slot_refs, weight_ref, out_refs, both, landed, arrived):
    width = landed.shape[1]
    steps = out_refs[0].shape[1] // width

    def fetch(step):
        start = pl.multiple_of(first + step * width, width)
        slot = lax.rem(step, depth)
        return pltpu.make_async_copy(weight_ref.at[pl.ds(start, width), :], landed.at[slot], arrived.at[slot])

    for step in range(min(depth, steps)):
        fetch(step).start()
    fill(both, slot_refs, place_ref, (0, slot_refs[0].shape[0]))

    @pl.loop(0, steps)
    def _(step):
        fetch(step).wait()
        high, low = split(landed[lax.rem(step, depth)])
        put(out_refs, pl.ds(pl.multiple_of(step * width, width), width), three_pass(both, high, low, 1))

        @pl.when(step + depth < steps)
        def _():
            fetch(step + depth).start()


def stream(slots, weight, place, first, hidden, after):
    tokens, columns = slots[0].shape[0] * len(slots), slots[0].shape[1]
    width, depth = divisor(hidden, 256, 128), 4
    inside, anywhere = pl.BlockSpec(memory_space=pltpu.VMEM), pl.BlockSpec(memory_space=pl.ANY)
    last = 1 + len(slots)
    return pl.pallas_call(
        lambda *refs: stream_kernel(first, depth, refs[0], refs[1:last], refs[last], refs[-7:-3], *refs[-3:]),
        out_shape=parts_of(tokens, len(slots) // 2, hidden),
        in_specs=[pl.BlockSpec(memory_space=pltpu.SMEM)] + [inside] * len(slots) + [anywhere] * (1 + len(after)),
        out_specs=[inside] * 4,
        scratch_shapes=[
            pltpu.VMEM((2 * tokens, columns), jnp.bfloat16),
            pltpu.VMEM((depth, width, columns), jnp.float32),
            pltpu.SemaphoreType.DMA((depth,)),
        ],
        compiler_params=pltpu.CompilerParams(vmem_limit_bytes=8 * 1024 * 1024),
        cost_estimate=SHORT,
    )(place, *slots, pltpu.with_memory_space_constraint(weight, pltpu.HBM), *after)


def backward_kernel(place_ref, act_refs, weight_refs, out_refs, both, result):
    block = act_refs[0].shape[0]
    total = block * len(act_refs)
    for p, act_ref in enumerate(act_refs):
        high, low = split(act_ref[...])
        both[p * block : (p + 1) * block, :] = high
        both[total + p * block : total + (p + 1) * block, :] = low
    width = result.shape[1]

    @pl.loop(0, out_refs[0].shape[1] // width)
    def _(step):
        at = pl.ds(pl.multiple_of(step * width, width), width)
        value, column = 0.0, 0
        for high_ref, low_ref in zip(weight_refs[::2], weight_refs[1::2]):
            columns = slice(column, column + high_ref.shape[1])
            value += three_pass(both[:, columns], high_ref[at, :], low_ref[at, :], 1)
            column = columns.stop
        result[...] = value
        for b, out_ref in enumerate(out_refs):
            row = pl.multiple_of(place_ref[b] * block, block)
            out_ref[:, at] = result[pl.ds(row, block), :]


def backward(acts, weights, place, after):
    slots, (block, hidden) = len(acts), acts[0].shape
    depth = weights[0].shape[0]
    width = divisor(depth, 256, 128)
    out = jax.ShapeDtypeStruct((block, depth), jnp.float32)
    inside, anywhere = pl.BlockSpec(memory_space=pltpu.VMEM), pl.BlockSpec(memory_space=pl.ANY)
    last = 1 + slots + len(weights)
    return pl.pallas_call(
        lambda *refs: backward_kernel(
            refs[0], refs[1 : 1 + slots], refs[1 + slots : last], refs[-2 - slots : -2], *refs[-2:]
        ),
        out_shape=[out] * slots,
        in_specs=[pl.BlockSpec(memory_space=pltpu.SMEM)] + [inside] * (last - 1) + [anywhere] * len(after),
        out_specs=[inside] * slots,
        scratch_shapes=[
            pltpu.VMEM((2 * block * slots, hidden), jnp.bfloat16),
            pltpu.VMEM((block * slots, width), jnp.float32),
        ],
        compiler_params=pltpu.CompilerParams(vmem_limit_bytes=VMEM_LIMIT),
        cost_estimate=SHORT,
    )(place, *acts, *[pltpu.with_memory_space_constraint(w, pltpu.VMEM) for w in weights], *after)


def body(hid_size, emb_size, inputs, out_grad, in_weight, in_bias, out_weight, norm_gain):
    chips = emb_size // 2
    tokens, depth = inputs.shape
    model_width = depth * emb_size
    hidden = in_weight.shape[1]
    me = lax.axis_index("emb")
    chip, core = me // 2, me % 2

    def along_hid(values, steps=1):
        return lax.ppermute(values, "hid", [(i, (i + steps) % hid_size) for i in range(hid_size)])

    def other_core(values):
        return lax.ppermute(values, "emb", [(i, i ^ 1) for i in range(emb_size)])

    def next_chip(values):
        return lax.ppermute(values, "emb", [(i, (i + 2) % emb_size) for i in range(emb_size)])

    owner = jnp.arange(emb_size, dtype=jnp.int32)
    place = ((owner % 2) ^ core) * chips + (owner // 2 - chip) % chips

    def gathered(values):
        return [values] + [along_hid(values, step) for step in range(1, hid_size)]

    def relayed(values):
        blocks = [values] + [None] * (hid_size - 1)
        for step in range(1, hid_size // 2 + 1):
            blocks[step] = along_hid(blocks[step - 1], 1)
        for step in range(1, hid_size - hid_size // 2):
            blocks[-step] = along_hid(blocks[(1 - step) % hid_size], -1)
        return blocks

    grads = gathered(out_grad)
    third = hidden // 3

    def tied(values, others):
        return lax.optimization_barrier((values, others))

    def halved(partial, behind=()):
        keep_own, keep, send_own, send = partial
        return keep + tied(other_core(send), behind)[0], (keep_own, other_core(send_own))

    def exchanged(half):
        summed, own = half
        terms = jnp.split(summed, chips - 1)
        arrival = next_chip(terms[chips - 2])
        for step in range(chips - 3, -1, -1):
            arrival = next_chip(arrival + terms[step])
        return arrival, *own

    def prepared(c, after):
        return prepare(in_weight, (0, depth), (c * third, third), after)

    moments = call(moments_kernel, jax.ShapeDtypeStruct((2 * tokens, 128), jnp.float32), (inputs,), ())
    in_parts = prepared(0, [place, moments])
    in_parts += prepared(1, [in_parts[0]])
    moments = call(
        functools.partial(merge_kernel, depth), moments, (moments, other_core(moments)), (in_parts[4], *grads[:0:-1])
    )
    parts = [moments]
    for _ in range(1, chips):
        parts.append(next_chip(parts[-1]))
    normed, scaled, inv_std = call(
        functools.partial(normalise_kernel, 2 * depth),
        (inputs, inputs, jax.ShapeDtypeStruct((tokens, 128), jnp.float32)),
        (inputs, norm_gain[None, :], *parts),
        (),
    )
    inv_std = inv_std[:, :1]
    scaled = relayed(scaled)
    back_0 = stream(grads, out_weight, place, 0, 2 * third, [scaled[0]])
    back_0, (scaled[1], scaled[-1]) = tied(back_0, (scaled[1], scaled[-1]))
    half_0 = halved(back_0)
    back_1 = stream(grads, out_weight, place, 2 * third, third, [half_0[0]])
    back_0 = exchanged(half_0)
    back_1, scaled = tied(back_1, scaled)
    in_parts += prepared(2, [back_1[0]])
    half_1 = halved(back_1, (in_parts[8], back_0[0]))
    back_1 = exchanged(half_1)
    early, late = (0, tokens // 2), (tokens // 2, tokens // 2)
    pre_0 = forward(scaled, early, in_parts, place, (), [half_1[0]])
    pre_1 = forward(scaled, late, in_parts[:8], place, (), [pre_0[0]])
    half_0 = halved(pre_0, (pre_1, back_1[0]))
    pre_1 = forward(scaled, late, in_parts[8:], place, pre_1, [half_0[0]])
    pre_0 = exchanged(half_0)
    back_sum = jnp.concatenate([sum(back_0), sum(back_1)], axis=1)

    def slope_product(rows, pre):
        return back_sum[rows[0] : sum(rows)] * gelu_slope(sum(pre) + in_bias)

    def spread_out(act):
        mine = [None] * chips
        mine[0] = act
        for step in range(1, chips):
            act = next_chip(act)
            mine[(chips - step) % chips] = act
        return mine

    act_0 = slope_product(early, pre_0)
    pre_1 = exchanged(halved(pre_1, act_0))
    act_1 = slope_product(late, pre_1)

    def both_cores(mine):
        return mine + [other_core(block) for block in mine]

    def summed_along_hid(sums):
        return sum([along_hid(sums[step], -step) for step in range(1, hid_size)], start=sums[0])

    acts_0, acts_1 = spread_out(act_0), spread_out(act_1)
    sums_0 = backward(both_cores(acts_0), in_parts, place, [])
    acts_1[1:], sums_0 = tied(acts_1[1:], sums_0)
    sums_1 = backward(both_cores(acts_1), in_parts, place, [])
    running = jnp.concatenate([summed_along_hid(sums_0), summed_along_hid(sums_1)])
    normed_grad = running * norm_gain
    totals = lax.psum(
        jnp.stack([jnp.sum(normed_grad, axis=-1), jnp.sum(normed_grad * normed, axis=-1)]), "emb"
    )
    first, second = (totals / model_width)[:, :, None]
    return inv_std * (normed_grad - first - normed * second)


def solution(mesh):
    hid_size, emb_size = mesh.shape["hid"], mesh.shape["emb"]
    assert hid_size == emb_size and emb_size % 2 == 0
    return jax.shard_map(
        functools.partial(body, hid_size, emb_size),
        mesh=mesh,
        in_specs=(
            P(("groups", "hid"), "emb"),
            P(("groups", "hid"), "emb"),
            P("emb", "hid"),
            P("hid"),
            P("hid", "emb"),
            P("emb"),
        ),
        out_specs=P(("groups", "hid"), "emb"),
        check_vma=False,
    )
```

```python
import functools
import math

import jax
import jax.numpy as jnp
from jax import lax
from jax.experimental import pallas as pl
from jax.experimental.pallas import tpu as pltpu
from jax.sharding import PartitionSpec as P

VMEM_LIMIT = 5 * 1024 * 1024
SHORT = pl.CostEstimate(flops=1 << 20, bytes_accessed=1 << 18, transcendentals=0)


def gelu_slope(values):
    cdf = 0.5 * (1.0 + lax.erf(values * (1.0 / math.sqrt(2.0))))
    density = jnp.exp(-0.5 * values * values) * (1.0 / math.sqrt(2.0 * math.pi))
    return cdf + values * density


def split(values):
    high = values.astype(jnp.bfloat16)
    return high, (values - high.astype(jnp.float32)).astype(jnp.bfloat16)


def divisor(extent, *choices):
    return next(c for c in choices if extent % c == 0)


def call(kernel, out_shape, operands, after):
    outs = out_shape if isinstance(out_shape, tuple) else (out_shape,)

    def run(*refs):
        kernel(*refs[: len(operands)], *refs[len(operands) + len(after) :])

    inside = pl.BlockSpec(memory_space=pltpu.VMEM)
    result = pl.pallas_call(
        run,
        out_shape=tuple(jax.ShapeDtypeStruct(o.shape, o.dtype) for o in outs),
        in_specs=[inside] * len(operands) + [pl.BlockSpec(memory_space=pl.ANY)] * len(after),
        out_specs=[inside] * len(outs),
        compiler_params=pltpu.CompilerParams(vmem_limit_bytes=VMEM_LIMIT),
        cost_estimate=SHORT,
    )(*operands, *after)
    return result if isinstance(out_shape, tuple) else result[0]


def moments_kernel(inputs_ref, out_ref):
    rows, depth = inputs_ref.shape
    mean = jnp.sum(inputs_ref[...], axis=1, keepdims=True) * (1.0 / depth)
    square = jnp.sum(jnp.square(inputs_ref[...] - mean), axis=1, keepdims=True)
    out_ref[:rows] = jnp.broadcast_to(mean, (rows, 128))
    out_ref[rows:] = jnp.broadcast_to(square, (rows, 128))


def merge(moments, count):
    rows = moments[0].shape[0] // 2
    mean = sum(part[:rows] for part in moments) * (1.0 / len(moments))
    square = sum(part[rows:] + count * jnp.square(part[:rows] - mean) for part in moments)
    return mean, square


def merge_kernel(count, first_ref, second_ref, out_ref):
    rows = out_ref.shape[0] // 2
    out_ref[:rows], out_ref[rows:] = merge((first_ref[...], second_ref[...]), count)


def normalise_kernel(count, inputs_ref, gain_ref, *refs):
    *moment_refs, normed_ref, scaled_ref, inv_std_ref = refs
    mean, square = merge([ref[...] for ref in moment_refs], count)
    inv_std = 1.0 / jnp.sqrt(square * (1.0 / (count * len(moment_refs))) + 1e-06)
    normed = (inputs_ref[...] - mean[:, :1]) * inv_std[:, :1]
    normed_ref[...] = normed
    scaled_ref[...] = normed * gain_ref[...]
    inv_std_ref[...] = inv_std


def slope_kernel(terms, *refs):
    back_refs, pre_refs, (bias_ref, weight_ref) = refs[:terms], refs[terms : 2 * terms], refs[2 * terms : 2 * terms + 2]
    *sums_refs, act_ref, out_sums_ref = refs[2 * terms + 2 :]
    hidden = bias_ref.shape[1]
    product = sum(ref[...] for ref in pre_refs)
    act = sum(ref[...] for ref in back_refs) * gelu_slope(product + bias_ref[...])
    act_ref[:, :hidden] = act
    lane = lax.broadcasted_iota(jnp.int32, out_sums_ref.shape, 1)
    first = jnp.sum(act * weight_ref[...], axis=1, keepdims=True)
    second = jnp.sum(act * product, axis=1, keepdims=True)
    sums = jnp.where(lane == 0, first, jnp.where(lane == 1, second, 0.0)) + sum(ref[...] for ref in sums_refs)
    out_sums_ref[...] = sums
    if act_ref.shape[1] > hidden:
        act_ref[:, hidden:] = sums


def prepare_kernel(rows, columns, block, depth, weight_ref, gain_ref, *refs):
    *part_refs, sums_ref, landed, arrived, totals = refs
    totals[...] = jnp.zeros_like(totals)
    width = part_refs[0].shape[1]
    steps = rows[1] // block

    def fetch(step):
        start = pl.multiple_of(rows[0] + step * block, block)
        slot = lax.rem(step, depth)
        return pltpu.make_async_copy(
            weight_ref.at[pl.ds(start, block), pl.ds(*columns)], landed.at[slot], arrived.at[slot]
        )

    for step in range(min(depth, steps)):
        fetch(step).start()

    @pl.loop(0, steps)
    def _(step):
        fetch(step).wait()
        tile = landed[lax.rem(step, depth)]
        high, low = split(tile)
        at = pl.ds(pl.multiple_of(step * block, block), block)
        totals[...] += jnp.sum((tile * gain_ref[at, :]).reshape(block // 8, 8, columns[1]), axis=0)
        for n, part_ref in enumerate(part_refs):
            part_ref[at, :] = (low if n % 2 else high)[:, n // 2 * width : (n // 2 + 1) * width]

        @pl.when(step + depth < steps)
        def _():
            fetch(step + depth).start()

    sums_ref[...] = jnp.sum(totals[...], axis=0, keepdims=True)


def prepare(weight, gain, rows, columns, after):
    block = divisor(rows[1], *[b for b in (256, 128, 64, 32) if b <= max(256 * 1536 // columns[1], 32)])
    depth = 4
    outs = (pltpu.VMEM((rows[1], columns[1] // 2), jnp.bfloat16),) * 4
    inside, anywhere = pl.BlockSpec(memory_space=pltpu.VMEM), pl.BlockSpec(memory_space=pl.ANY)
    result = pl.pallas_call(
        lambda weight_ref, gain_ref, *refs: prepare_kernel(
            rows, columns, block, depth, weight_ref, gain_ref, *refs[len(after) :]
        ),
        out_shape=outs + (jax.ShapeDtypeStruct((1, columns[1]), jnp.float32),),
        in_specs=[anywhere, inside] + [anywhere] * len(after),
        out_specs=[inside] * 5,
        scratch_shapes=[
            pltpu.VMEM((depth, block, columns[1]), jnp.float32),
            pltpu.SemaphoreType.DMA((depth,)),
            pltpu.VMEM((8, columns[1]), jnp.float32),
        ],
        compiler_params=pltpu.CompilerParams(vmem_limit_bytes=VMEM_LIMIT),
        cost_estimate=SHORT,
    )(pltpu.with_memory_space_constraint(weight, pltpu.HBM), gain, *after)
    return list(result[:4]), result[4]


def three_pass(both, high, low, contract):
    rows = both.shape[0] // 2
    dot = functools.partial(
        lax.dot_general,
        dimension_numbers=(((1,), (contract,)), ((), ())),
        preferred_element_type=jnp.float32,
    )
    first = dot(both[...], high)
    return first[:rows] + first[rows:] + dot(both[:rows, :], low)


def fill(both, block_refs, place_ref):
    count = block_refs[0].shape[0]
    total = both.shape[0] // 2
    for index, ref in enumerate(block_refs):
        high, low = split(ref[...])
        row = pl.multiple_of(place_ref[index] * count, count)
        both[pl.ds(row, count), :] = high
        both[pl.ds(total + row, count), :] = low


def follow(earlier_refs, out_refs):
    for earlier_ref, out_ref in zip(earlier_refs, out_refs):
        out_ref[:, : earlier_ref.shape[1]] = earlier_ref[...]
    return earlier_refs[0].shape[1] if earlier_refs else 0


def put(out_refs, at, value):
    row = 0
    for out_ref in out_refs:
        out_ref[:, at] = value[row : row + out_ref.shape[0]]
        row += out_ref.shape[0]


def parts_of(tokens, chips, hidden):
    block = tokens // (2 * chips)
    return [jax.ShapeDtypeStruct((n, hidden), jnp.float32) for n in (block, block * (chips - 1))] * 2


def forward_kernel(place_ref, slot_refs, weight_refs, earlier_refs, out_refs, both):
    fill(both, slot_refs, place_ref)
    column = follow(earlier_refs, out_refs)
    for high_ref, low_ref in zip(weight_refs[::2], weight_refs[1::2]):
        width = divisor(high_ref.shape[1], 256, 128)

        @pl.loop(0, high_ref.shape[1] // width, unroll=2)
        def _(step):
            at = pl.ds(pl.multiple_of(step * width, width), width)
            part = three_pass(both, high_ref[:, at], low_ref[:, at], 0)
            put(out_refs, pl.ds(pl.multiple_of(column + step * width, width), width), part)

        column += high_ref.shape[1]


def forward(slots, weights, place, earlier, after):
    tokens, depth = slots[0].shape[0] * len(slots), slots[0].shape[1]
    hidden = sum(w.shape[1] for w in weights[::2]) + (earlier[0].shape[1] if earlier else 0)
    inside, anywhere = pl.BlockSpec(memory_space=pltpu.VMEM), pl.BlockSpec(memory_space=pl.ANY)
    ends = [1 + len(slots), 1 + len(slots) + len(weights), 1 + len(slots) + len(weights) + len(earlier)]
    return pl.pallas_call(
        lambda *refs: forward_kernel(
            refs[0], refs[1 : ends[0]], refs[ends[0] : ends[1]], refs[ends[1] : ends[2]], refs[-5:-1], refs[-1]
        ),
        out_shape=parts_of(tokens, len(slots) // 2, hidden),
        in_specs=[pl.BlockSpec(memory_space=pltpu.SMEM)] + [inside] * (ends[2] - 1) + [anywhere] * len(after),
        out_specs=[inside] * 4,
        scratch_shapes=[pltpu.VMEM((2 * tokens, depth), jnp.bfloat16)],
        compiler_params=pltpu.CompilerParams(vmem_limit_bytes=VMEM_LIMIT),
        cost_estimate=SHORT,
    )(place, *slots, *[pltpu.with_memory_space_constraint(w, pltpu.VMEM) for w in weights], *earlier, *after)


def stream_kernel(first, depth, place_ref, slot_refs, weight_ref, out_refs, both, landed, arrived):
    width = landed.shape[1]
    steps = out_refs[0].shape[1] // width

    def fetch(step):
        start = pl.multiple_of(first + step * width, width)
        slot = lax.rem(step, depth)
        return pltpu.make_async_copy(weight_ref.at[pl.ds(start, width), :], landed.at[slot], arrived.at[slot])

    for step in range(min(depth, steps)):
        fetch(step).start()
    fill(both, slot_refs, place_ref)

    @pl.loop(0, steps)
    def _(step):
        fetch(step).wait()
        high, low = split(landed[lax.rem(step, depth)])
        put(out_refs, pl.ds(pl.multiple_of(step * width, width), width), three_pass(both, high, low, 1))

        @pl.when(step + depth < steps)
        def _():
            fetch(step + depth).start()


def stream(slots, weight, place, first, hidden, after):
    tokens, columns = slots[0].shape[0] * len(slots), slots[0].shape[1]
    width, depth = divisor(hidden, 256, 128), 4
    inside, anywhere = pl.BlockSpec(memory_space=pltpu.VMEM), pl.BlockSpec(memory_space=pl.ANY)
    last = 1 + len(slots)
    return pl.pallas_call(
        lambda *refs: stream_kernel(first, depth, refs[0], refs[1:last], refs[last], refs[-7:-3], *refs[-3:]),
        out_shape=parts_of(tokens, len(slots) // 2, hidden),
        in_specs=[pl.BlockSpec(memory_space=pltpu.SMEM)] + [inside] * len(slots) + [anywhere] * (1 + len(after)),
        out_specs=[inside] * 4,
        scratch_shapes=[
            pltpu.VMEM((2 * tokens, columns), jnp.bfloat16),
            pltpu.VMEM((depth, width, columns), jnp.float32),
            pltpu.SemaphoreType.DMA((depth,)),
        ],
        compiler_params=pltpu.CompilerParams(vmem_limit_bytes=8 * 1024 * 1024),
        cost_estimate=SHORT,
    )(place, *slots, pltpu.with_memory_space_constraint(weight, pltpu.HBM), *after)


def backward_kernel(first, depth, place_ref, act_refs, weight_refs, earlier_refs, out_refs, both, result, riders):
    block = act_refs[0].shape[0]
    total = block * len(act_refs)
    hidden = both.shape[1]
    for p, act_ref in enumerate(act_refs):
        if act_ref.shape[1] > hidden:
            riders[p * block : (p + 1) * block, :] = act_ref[:, hidden:]
        high, low = split(act_ref[:, :hidden])
        both[p * block : (p + 1) * block, :] = high
        both[total + p * block : total + (p + 1) * block, :] = low
    width = result.shape[1]

    if out_refs[0].shape[1] > depth:
        for b, out_ref in enumerate(out_refs):
            out_ref[:, depth:] = riders[pl.ds(pl.multiple_of(place_ref[b] * block, block), block), :]

    @pl.loop(0, depth // width)
    def _(step):
        at = pl.ds(pl.multiple_of(first + step * width, width), width)
        value, column = 0.0, 0
        for high_ref, low_ref in zip(weight_refs[::2], weight_refs[1::2]):
            columns = slice(column, column + high_ref.shape[1])
            value += three_pass(both[:, columns], high_ref[at, :], low_ref[at, :], 1)
            column = columns.stop
        result[...] = value
        for b, out_ref in enumerate(out_refs):
            rows = result[pl.ds(pl.multiple_of(place_ref[b] * block, block), block), :]
            if earlier_refs:
                rows = rows + earlier_refs[b][:, at]
            out_ref[:, pl.ds(pl.multiple_of(step * width, width), width)] = rows


def backward(acts, weights, place, earlier, part, parts, after):
    slots, block, hidden = len(acts), acts[0].shape[0], sum(w.shape[1] for w in weights[::2])
    riding = acts[0].shape[1] - hidden if part == parts - 1 else 0
    depth = weights[0].shape[0] // parts
    width = divisor(depth, 256, 128)
    out = jax.ShapeDtypeStruct((block, depth + riding), jnp.float32)
    inside, anywhere = pl.BlockSpec(memory_space=pltpu.VMEM), pl.BlockSpec(memory_space=pl.ANY)
    ends = [1 + slots, 1 + slots + len(weights), 1 + slots + len(weights) + len(earlier)]
    return pl.pallas_call(
        lambda *refs: backward_kernel(
            part * depth,
            depth,
            refs[0],
            refs[1 : ends[0]],
            refs[ends[0] : ends[1]],
            refs[ends[1] : ends[2]],
            refs[-3 - slots : -3],
            *refs[-3:],
        ),
        out_shape=[out] * slots,
        in_specs=[pl.BlockSpec(memory_space=pltpu.SMEM)] + [inside] * (ends[2] - 1) + [anywhere] * len(after),
        out_specs=[inside] * slots,
        scratch_shapes=[
            pltpu.VMEM((2 * block * slots, hidden), jnp.bfloat16),
            pltpu.VMEM((block * slots, width), jnp.float32),
            pltpu.VMEM((block * slots, 128), jnp.float32),
        ],
        compiler_params=pltpu.CompilerParams(vmem_limit_bytes=VMEM_LIMIT),
        cost_estimate=SHORT,
    )(place, *acts, *[pltpu.with_memory_space_constraint(w, pltpu.VMEM) for w in weights], *earlier, *after)


def body(hid_size, emb_size, inputs, out_grad, in_weight, in_bias, out_weight, norm_gain):
    chips = emb_size // 2
    tokens, depth = inputs.shape
    model_width = depth * emb_size
    hidden = in_weight.shape[1]
    me = lax.axis_index("emb")
    chip, core = me // 2, me % 2

    def along_hid(values, steps=1):
        return lax.ppermute(values, "hid", [(i, (i + steps) % hid_size) for i in range(hid_size)])

    def other_core(values):
        return lax.ppermute(values, "emb", [(i, i ^ 1) for i in range(emb_size)])

    def next_chip(values):
        return lax.ppermute(values, "emb", [(i, (i + 2) % emb_size) for i in range(emb_size)])

    owner = jnp.arange(emb_size, dtype=jnp.int32)
    place = ((owner % 2) ^ core) * chips + (owner // 2 - chip) % chips

    def gathered(values):
        return [values] + [along_hid(values, step) for step in range(1, hid_size)]

    def relayed(values):
        blocks = [values] + [None] * (hid_size - 1)
        for step in range(1, hid_size // 2 + 1):
            blocks[step] = along_hid(blocks[step - 1], 1)
        for step in range(1, hid_size - hid_size // 2):
            blocks[-step] = along_hid(blocks[(1 - step) % hid_size], -1)
        return blocks

    grads = gathered(out_grad)
    third = hidden // 3

    def tied(values, others):
        return lax.optimization_barrier((values, others))

    def halved(partial, behind=()):
        keep_own, keep, send_own, send = partial
        return keep + tied(other_core(send), behind)[0], (keep_own, other_core(send_own))

    def exchanged(half):
        summed, own = half
        terms = jnp.split(summed, chips - 1)
        arrival = next_chip(terms[chips - 2])
        for step in range(chips - 3, -1, -1):
            arrival = next_chip(arrival + terms[step])
        return arrival, *own

    def prepared(c, after):
        return prepare(in_weight, norm_gain[:, None], (0, depth), (c * third, third), after)

    moments = call(moments_kernel, jax.ShapeDtypeStruct((2 * tokens, 128), jnp.float32), (inputs,), ())
    in_parts, sums_0 = prepared(0, [place, moments])
    parts, sums_1 = prepared(1, [in_parts[0]])
    in_parts += parts
    moments = call(
        functools.partial(merge_kernel, depth), moments, (moments, other_core(moments)), (in_parts[4], *grads[1:])
    )
    parts = [moments]
    for _ in range(1, chips):
        parts.append(next_chip(parts[-1]))
    normed, scaled, inv_std = call(
        functools.partial(normalise_kernel, 2 * depth),
        (inputs, inputs, jax.ShapeDtypeStruct((tokens, 128), jnp.float32)),
        (inputs, norm_gain[None, :], *parts),
        (),
    )
    inv_std = inv_std[:, :1]
    scaled = relayed(scaled)
    back_0 = stream(grads, out_weight, place, 0, 2 * third, [scaled[0]])
    back_0, (scaled[1], scaled[-1]) = tied(back_0, (scaled[1], scaled[-1]))
    half_0 = halved(back_0)
    back_1 = stream(grads, out_weight, place, 2 * third, third, [half_0[0]])
    back_0 = exchanged(half_0)
    back_1, scaled = tied(back_1, scaled)
    pre_0 = forward(scaled, in_parts[:8], place, (), [back_1[0]])
    half_1 = halved(back_1, (pre_0, back_0[0]))
    back_1 = exchanged(half_1)
    parts, sums_2 = prepared(2, [pre_0[0], half_1[0]])
    in_parts += parts
    half_0 = halved(pre_0, (parts, back_1[0]))
    pre_1 = forward(scaled, in_parts[8:], place, (), [half_0[0]])
    pre_0 = exchanged(half_0)

    gain_sums, _ = tied(jnp.concatenate([sums_0, sums_1, sums_2], axis=1), pre_1)
    gain_sums = passing = gain_sums + other_core(gain_sums)
    for _ in range(1, chips):
        passing = next_chip(passing)
        gain_sums = gain_sums + passing

    def slope_product(span, back, pre, sums):
        width = span.stop - span.start
        return call(
            functools.partial(slope_kernel, len(back)),
            tuple(
                jax.ShapeDtypeStruct((tokens, n), jnp.float32) for n in (width + 128 * len(sums), 128)
            ),
            (*back, *pre, in_bias[None, span], gain_sums[:, span], *sums),
            (),
        )

    def spread_out(act):
        mine = [None] * chips
        mine[0] = act
        for step in range(1, chips):
            act = next_chip(act)
            mine[(chips - step) % chips] = act
        return mine

    def both_cores(mine):
        return mine + [other_core(block) for block in mine]

    def summed_along_hid(sums):
        return sum([along_hid(sums[step], -step) for step in range(1, hid_size)], start=sums[0])

    act_0, sums_0 = slope_product(slice(0, 2 * third), back_0, pre_0, ())
    pre_1 = exchanged(halved(pre_1, pre_0[0]))
    act_1, _ = slope_product(slice(2 * third, hidden), back_1, pre_1, (sums_0,))
    acts_0, acts_1 = spread_out(act_0), spread_out(act_1)
    sums = backward(both_cores(acts_0), in_parts[:8], place, (), 0, 1, [])
    acts_1[1:], sums = tied(acts_1[1:], sums)
    acts_1 = both_cores(acts_1)
    parts = 2 if depth % 512 == 0 else 1
    ends = []
    for part in range(parts):
        ends.append(backward(acts_1, in_parts[8:], place, sums, part, parts, [ends[-1][0]] if ends else []))
    *columns, last = [summed_along_hid(end) for end in ends]
    width = depth // parts
    normed_grad = jnp.concatenate([*columns, last[:, :width]], axis=1) * norm_gain
    first, second = last[:, width : width + 1] / model_width, last[:, width + 1 : width + 2] / model_width
    return inv_std * (normed_grad - first - normed * second)


def solution(mesh):
    hid_size, emb_size = mesh.shape["hid"], mesh.shape["emb"]
    assert hid_size == emb_size and emb_size % 2 == 0
    return jax.shard_map(
        functools.partial(body, hid_size, emb_size),
        mesh=mesh,
        in_specs=(
            P(("groups", "hid"), "emb"),
            P(("groups", "hid"), "emb"),
            P("emb", "hid"),
            P("hid"),
            P("hid", "emb"),
            P("emb"),
        ),
        out_specs=P(("groups", "hid"), "emb"),
        check_vma=False,
    )
```

```python
import functools
import math

import jax
import jax.numpy as jnp
from jax import lax
from jax.experimental import pallas as pl
from jax.experimental.pallas import tpu as pltpu
from jax.sharding import PartitionSpec as P

VMEM_LIMIT = 5 * 1024 * 1024
SHORT = pl.CostEstimate(flops=1 << 20, bytes_accessed=1 << 18, transcendentals=0)


def gelu_slope(values):
    cdf = 0.5 * (1.0 + lax.erf(values * (1.0 / math.sqrt(2.0))))
    density = jnp.exp(-0.5 * values * values) * (1.0 / math.sqrt(2.0 * math.pi))
    return cdf + values * density


def split(values):
    high = values.astype(jnp.bfloat16)
    return high, (values - high.astype(jnp.float32)).astype(jnp.bfloat16)


def divisor(extent, *choices):
    return next(c for c in choices if extent % c == 0)


def call(kernel, out_shape, operands, after):
    outs = out_shape if isinstance(out_shape, tuple) else (out_shape,)

    def run(*refs):
        kernel(*refs[: len(operands)], *refs[len(operands) + len(after) :])

    inside = pl.BlockSpec(memory_space=pltpu.VMEM)
    result = pl.pallas_call(
        run,
        out_shape=tuple(jax.ShapeDtypeStruct(o.shape, o.dtype) for o in outs),
        in_specs=[inside] * len(operands) + [pl.BlockSpec(memory_space=pl.ANY)] * len(after),
        out_specs=[inside] * len(outs),
        compiler_params=pltpu.CompilerParams(vmem_limit_bytes=VMEM_LIMIT),
        cost_estimate=SHORT,
    )(*operands, *after)
    return result if isinstance(out_shape, tuple) else result[0]


def moments_kernel(inputs_ref, out_ref):
    rows, depth = inputs_ref.shape
    mean = jnp.sum(inputs_ref[...], axis=1, keepdims=True) * (1.0 / depth)
    square = jnp.sum(jnp.square(inputs_ref[...] - mean), axis=1, keepdims=True)
    out_ref[:rows] = jnp.broadcast_to(mean, (rows, 128))
    out_ref[rows:] = jnp.broadcast_to(square, (rows, 128))


def merge(moments, count):
    rows = moments[0].shape[0] // 2
    mean = sum(part[:rows] for part in moments) * (1.0 / len(moments))
    square = sum(part[rows:] + count * jnp.square(part[:rows] - mean) for part in moments)
    return mean, square


def merge_kernel(count, first_ref, second_ref, out_ref):
    rows = out_ref.shape[0] // 2
    out_ref[:rows], out_ref[rows:] = merge((first_ref[...], second_ref[...]), count)


def normalise_kernel(count, inputs_ref, gain_ref, *refs):
    *moment_refs, normed_ref, scaled_ref, inv_std_ref = refs
    mean, square = merge([ref[...] for ref in moment_refs], count)
    inv_std = 1.0 / jnp.sqrt(square * (1.0 / (count * len(moment_refs))) + 1e-06)
    normed = (inputs_ref[...] - mean[:, :1]) * inv_std[:, :1]
    normed_ref[...] = normed
    scaled_ref[...] = normed * gain_ref[...]
    inv_std_ref[...] = inv_std


def slope_kernel(terms, *refs):
    back_refs, pre_refs, (bias_ref, weight_ref) = refs[:terms], refs[terms : 2 * terms], refs[2 * terms : 2 * terms + 2]
    *sums_refs, act_ref, out_sums_ref = refs[2 * terms + 2 :]
    hidden = bias_ref.shape[1]
    product = sum(ref[...] for ref in pre_refs)
    act = sum(ref[...] for ref in back_refs) * gelu_slope(product + bias_ref[...])
    act_ref[:, :hidden] = act
    lane = lax.broadcasted_iota(jnp.int32, out_sums_ref.shape, 1)
    first = jnp.sum(act * weight_ref[...], axis=1, keepdims=True)
    second = jnp.sum(act * product, axis=1, keepdims=True)
    sums = jnp.where(lane == 0, first, jnp.where(lane == 1, second, 0.0)) + sum(ref[...] for ref in sums_refs)
    out_sums_ref[...] = sums
    if act_ref.shape[1] > hidden:
        act_ref[:, hidden:] = sums


def prepare_kernel(rows, columns, block, depth, weight_ref, gain_ref, *refs):
    *part_refs, sums_ref, landed, arrived, totals = refs
    totals[...] = jnp.zeros_like(totals)
    width = part_refs[0].shape[1]
    steps = rows[1] // block

    def fetch(step):
        start = pl.multiple_of(rows[0] + step * block, block)
        slot = lax.rem(step, depth)
        return pltpu.make_async_copy(
            weight_ref.at[pl.ds(start, block), pl.ds(*columns)], landed.at[slot], arrived.at[slot]
        )

    for step in range(min(depth, steps)):
        fetch(step).start()

    @pl.loop(0, steps)
    def _(step):
        fetch(step).wait()
        tile = landed[lax.rem(step, depth)]
        high, low = split(tile)
        at = pl.ds(pl.multiple_of(step * block, block), block)
        totals[...] += jnp.sum((tile * gain_ref[at, :]).reshape(block // 8, 8, columns[1]), axis=0)
        for n, part_ref in enumerate(part_refs):
            part_ref[at, :] = (low if n % 2 else high)[:, n // 2 * width : (n // 2 + 1) * width]

        @pl.when(step + depth < steps)
        def _():
            fetch(step + depth).start()

    sums_ref[...] = jnp.sum(totals[...], axis=0, keepdims=True)


def prepare(weight, gain, rows, columns, after):
    block = divisor(rows[1], *[b for b in (256, 128, 64, 32) if b <= max(256 * 1536 // columns[1], 32)])
    depth = 4
    outs = (pltpu.VMEM((rows[1], columns[1] // 2), jnp.bfloat16),) * 4
    inside, anywhere = pl.BlockSpec(memory_space=pltpu.VMEM), pl.BlockSpec(memory_space=pl.ANY)
    result = pl.pallas_call(
        lambda weight_ref, gain_ref, *refs: prepare_kernel(
            rows, columns, block, depth, weight_ref, gain_ref, *refs[len(after) :]
        ),
        out_shape=outs + (jax.ShapeDtypeStruct((1, columns[1]), jnp.float32),),
        in_specs=[anywhere, inside] + [anywhere] * len(after),
        out_specs=[inside] * 5,
        scratch_shapes=[
            pltpu.VMEM((depth, block, columns[1]), jnp.float32),
            pltpu.SemaphoreType.DMA((depth,)),
            pltpu.VMEM((8, columns[1]), jnp.float32),
        ],
        compiler_params=pltpu.CompilerParams(vmem_limit_bytes=VMEM_LIMIT),
        cost_estimate=SHORT,
    )(pltpu.with_memory_space_constraint(weight, pltpu.HBM), gain, *after)
    return list(result[:4]), result[4]


def three_pass(both, high, low, contract):
    rows = both.shape[0] // 2
    dot = functools.partial(
        lax.dot_general,
        dimension_numbers=(((1,), (contract,)), ((), ())),
        preferred_element_type=jnp.float32,
    )
    first = dot(both[...], high)
    return first[:rows] + first[rows:] + dot(both[:rows, :], low)


def fill(both, block_refs, place_ref):
    count = block_refs[0].shape[0]
    total = both.shape[0] // 2
    for index, ref in enumerate(block_refs):
        high, low = split(ref[...])
        row = pl.multiple_of(place_ref[index] * count, count)
        both[pl.ds(row, count), :] = high
        both[pl.ds(total + row, count), :] = low


def follow(earlier_refs, out_refs):
    for earlier_ref, out_ref in zip(earlier_refs, out_refs):
        out_ref[:, : earlier_ref.shape[1]] = earlier_ref[...]
    return earlier_refs[0].shape[1] if earlier_refs else 0


def put(out_refs, at, value):
    row = 0
    for out_ref in out_refs:
        out_ref[:, at] = value[row : row + out_ref.shape[0]]
        row += out_ref.shape[0]


def parts_of(tokens, chips, hidden):
    block = tokens // (2 * chips)
    return [jax.ShapeDtypeStruct((n, hidden), jnp.float32) for n in (block, block * (chips - 1))] * 2


def forward_kernel(place_ref, slot_refs, weight_refs, earlier_refs, out_refs, both):
    fill(both, slot_refs, place_ref)
    column = follow(earlier_refs, out_refs)
    for high_ref, low_ref in zip(weight_refs[::2], weight_refs[1::2]):
        width = divisor(high_ref.shape[1], 256, 128)

        @pl.loop(0, high_ref.shape[1] // width, unroll=2)
        def _(step):
            at = pl.ds(pl.multiple_of(step * width, width), width)
            part = three_pass(both, high_ref[:, at], low_ref[:, at], 0)
            put(out_refs, pl.ds(pl.multiple_of(column + step * width, width), width), part)

        column += high_ref.shape[1]


def forward(slots, weights, place, earlier, after):
    tokens, depth = slots[0].shape[0] * len(slots), slots[0].shape[1]
    hidden = sum(w.shape[1] for w in weights[::2]) + (earlier[0].shape[1] if earlier else 0)
    inside, anywhere = pl.BlockSpec(memory_space=pltpu.VMEM), pl.BlockSpec(memory_space=pl.ANY)
    ends = [1 + len(slots), 1 + len(slots) + len(weights), 1 + len(slots) + len(weights) + len(earlier)]
    return pl.pallas_call(
        lambda *refs: forward_kernel(
            refs[0], refs[1 : ends[0]], refs[ends[0] : ends[1]], refs[ends[1] : ends[2]], refs[-5:-1], refs[-1]
        ),
        out_shape=parts_of(tokens, len(slots) // 2, hidden),
        in_specs=[pl.BlockSpec(memory_space=pltpu.SMEM)] + [inside] * (ends[2] - 1) + [anywhere] * len(after),
        out_specs=[inside] * 4,
        scratch_shapes=[pltpu.VMEM((2 * tokens, depth), jnp.bfloat16)],
        compiler_params=pltpu.CompilerParams(vmem_limit_bytes=VMEM_LIMIT),
        cost_estimate=SHORT,
    )(place, *slots, *[pltpu.with_memory_space_constraint(w, pltpu.VMEM) for w in weights], *earlier, *after)


def stream_kernel(first, depth, place_ref, slot_refs, weight_ref, out_refs, both, landed, arrived):
    width = landed.shape[1]
    steps = out_refs[0].shape[1] // width

    def fetch(step):
        start = pl.multiple_of(first + step * width, width)
        slot = lax.rem(step, depth)
        return pltpu.make_async_copy(weight_ref.at[pl.ds(start, width), :], landed.at[slot], arrived.at[slot])

    for step in range(min(depth, steps)):
        fetch(step).start()
    fill(both, slot_refs, place_ref)

    @pl.loop(0, steps)
    def _(step):
        fetch(step).wait()
        high, low = split(landed[lax.rem(step, depth)])
        put(out_refs, pl.ds(pl.multiple_of(step * width, width), width), three_pass(both, high, low, 1))

        @pl.when(step + depth < steps)
        def _():
            fetch(step + depth).start()


def stream(slots, weight, place, first, hidden, after):
    tokens, columns = slots[0].shape[0] * len(slots), slots[0].shape[1]
    width, depth = divisor(hidden, 256, 128), 4
    inside, anywhere = pl.BlockSpec(memory_space=pltpu.VMEM), pl.BlockSpec(memory_space=pl.ANY)
    last = 1 + len(slots)
    return pl.pallas_call(
        lambda *refs: stream_kernel(first, depth, refs[0], refs[1:last], refs[last], refs[-7:-3], *refs[-3:]),
        out_shape=parts_of(tokens, len(slots) // 2, hidden),
        in_specs=[pl.BlockSpec(memory_space=pltpu.SMEM)] + [inside] * len(slots) + [anywhere] * (1 + len(after)),
        out_specs=[inside] * 4,
        scratch_shapes=[
            pltpu.VMEM((2 * tokens, columns), jnp.bfloat16),
            pltpu.VMEM((depth, width, columns), jnp.float32),
            pltpu.SemaphoreType.DMA((depth,)),
        ],
        compiler_params=pltpu.CompilerParams(vmem_limit_bytes=8 * 1024 * 1024),
        cost_estimate=SHORT,
    )(place, *slots, pltpu.with_memory_space_constraint(weight, pltpu.HBM), *after)


def backward_kernel(first, depth, place_ref, act_refs, weight_refs, earlier_refs, out_refs, both, result, riders):
    block = act_refs[0].shape[0]
    total = block * len(act_refs)
    hidden = both.shape[1]
    for p, act_ref in enumerate(act_refs):
        if act_ref.shape[1] > hidden:
            riders[p * block : (p + 1) * block, :] = act_ref[:, hidden:]
        high, low = split(act_ref[:, :hidden])
        both[p * block : (p + 1) * block, :] = high
        both[total + p * block : total + (p + 1) * block, :] = low
    width = result.shape[1]

    if out_refs[0].shape[1] > depth:
        for b, out_ref in enumerate(out_refs):
            out_ref[:, depth:] = riders[pl.ds(pl.multiple_of(place_ref[b] * block, block), block), :]

    @pl.loop(0, depth // width)
    def _(step):
        at = pl.ds(pl.multiple_of(first + step * width, width), width)
        value, column = 0.0, 0
        for high_ref, low_ref in zip(weight_refs[::2], weight_refs[1::2]):
            columns = slice(column, column + high_ref.shape[1])
            value += three_pass(both[:, columns], high_ref[at, :], low_ref[at, :], 1)
            column = columns.stop
        result[...] = value
        for b, out_ref in enumerate(out_refs):
            rows = result[pl.ds(pl.multiple_of(place_ref[b] * block, block), block), :]
            if earlier_refs:
                rows = rows + earlier_refs[b][:, at]
            out_ref[:, pl.ds(pl.multiple_of(step * width, width), width)] = rows


def backward(acts, weights, place, earlier, part, parts, after):
    slots, block, hidden = len(acts), acts[0].shape[0], sum(w.shape[1] for w in weights[::2])
    riding = acts[0].shape[1] - hidden if part == 0 else 0
    depth = weights[0].shape[0] // parts
    width = divisor(depth, 256, 128)
    out = jax.ShapeDtypeStruct((block, depth + riding), jnp.float32)
    inside, anywhere = pl.BlockSpec(memory_space=pltpu.VMEM), pl.BlockSpec(memory_space=pl.ANY)
    ends = [1 + slots, 1 + slots + len(weights), 1 + slots + len(weights) + len(earlier)]
    return pl.pallas_call(
        lambda *refs: backward_kernel(
            part * depth,
            depth,
            refs[0],
            refs[1 : ends[0]],
            refs[ends[0] : ends[1]],
            refs[ends[1] : ends[2]],
            refs[-3 - slots : -3],
            *refs[-3:],
        ),
        out_shape=[out] * slots,
        in_specs=[pl.BlockSpec(memory_space=pltpu.SMEM)] + [inside] * (ends[2] - 1) + [anywhere] * len(after),
        out_specs=[inside] * slots,
        scratch_shapes=[
            pltpu.VMEM((2 * block * slots, hidden), jnp.bfloat16),
            pltpu.VMEM((block * slots, width), jnp.float32),
            pltpu.VMEM((block * slots, 128), jnp.float32),
        ],
        compiler_params=pltpu.CompilerParams(vmem_limit_bytes=VMEM_LIMIT),
        cost_estimate=SHORT,
    )(place, *acts, *[pltpu.with_memory_space_constraint(w, pltpu.VMEM) for w in weights], *earlier, *after)


def body(hid_size, emb_size, inputs, out_grad, in_weight, in_bias, out_weight, norm_gain):
    chips = emb_size // 2
    tokens, depth = inputs.shape
    model_width = depth * emb_size
    hidden = in_weight.shape[1]
    me = lax.axis_index("emb")
    chip, core = me // 2, me % 2

    def along_hid(values, steps=1):
        return lax.ppermute(values, "hid", [(i, (i + steps) % hid_size) for i in range(hid_size)])

    def other_core(values):
        return lax.ppermute(values, "emb", [(i, i ^ 1) for i in range(emb_size)])

    def next_chip(values):
        return lax.ppermute(values, "emb", [(i, (i + 2) % emb_size) for i in range(emb_size)])

    owner = jnp.arange(emb_size, dtype=jnp.int32)
    place = ((owner % 2) ^ core) * chips + (owner // 2 - chip) % chips

    def gathered(values):
        return [values] + [along_hid(values, step) for step in range(1, hid_size)]

    def relayed(values):
        blocks = [values] + [None] * (hid_size - 1)
        for step in range(1, hid_size // 2 + 1):
            blocks[step] = along_hid(blocks[step - 1], 1)
        for step in range(1, hid_size - hid_size // 2):
            blocks[-step] = along_hid(blocks[(1 - step) % hid_size], -1)
        return blocks

    grads = gathered(out_grad)
    third = hidden // 3

    def tied(values, others):
        return lax.optimization_barrier((values, others))

    def halved(partial, behind=()):
        keep_own, keep, send_own, send = partial
        return keep + tied(other_core(send), behind)[0], (keep_own, other_core(send_own))

    def exchanged(half):
        summed, own = half
        terms = jnp.split(summed, chips - 1)
        arrival = next_chip(terms[chips - 2])
        for step in range(chips - 3, -1, -1):
            arrival = next_chip(arrival + terms[step])
        return arrival, *own

    def prepared(c, after):
        return prepare(in_weight, norm_gain[:, None], (0, depth), (c * third, third), after)

    moments = call(moments_kernel, jax.ShapeDtypeStruct((2 * tokens, 128), jnp.float32), (inputs,), ())
    in_parts, sums_0 = prepared(0, [place, moments])
    parts, sums_1 = prepared(1, [in_parts[0]])
    in_parts += parts
    moments = call(
        functools.partial(merge_kernel, depth), moments, (moments, other_core(moments)), (in_parts[4], *grads[1:])
    )
    parts = [moments]
    for _ in range(1, chips):
        parts.append(next_chip(parts[-1]))
    normed, scaled, inv_std = call(
        functools.partial(normalise_kernel, 2 * depth),
        (inputs, inputs, jax.ShapeDtypeStruct((tokens, 128), jnp.float32)),
        (inputs, norm_gain[None, :], *parts),
        (),
    )
    inv_std = inv_std[:, :1]
    scaled = relayed(scaled)
    back_0 = stream(grads, out_weight, place, 0, 2 * third, [scaled[0]])
    back_0, (scaled[1], scaled[-1]) = tied(back_0, (scaled[1], scaled[-1]))
    half_0 = halved(back_0)
    back_1 = stream(grads, out_weight, place, 2 * third, third, [half_0[0]])
    back_0 = exchanged(half_0)
    back_1, scaled = tied(back_1, scaled)
    pre_0 = forward(scaled, in_parts[:8], place, (), [back_1[0]])
    half_1 = halved(back_1, (pre_0, back_0[0]))
    back_1 = exchanged(half_1)
    half_0 = halved(pre_0)
    parts, sums_2 = prepared(2, [half_0[0], half_1[0]])
    in_parts += parts
    pre_1 = forward(scaled, in_parts[8:], place, (), [half_0[0], back_1[0]])
    pre_0 = exchanged(half_0)

    gain_sums, _ = tied(jnp.concatenate([sums_0, sums_1, sums_2], axis=1), pre_1)
    gain_sums = passing = gain_sums + other_core(gain_sums)
    for _ in range(1, chips):
        passing = next_chip(passing)
        gain_sums = gain_sums + passing

    def slope_product(span, back, pre, sums):
        width = span.stop - span.start
        return call(
            functools.partial(slope_kernel, len(back)),
            tuple(
                jax.ShapeDtypeStruct((tokens, n), jnp.float32) for n in (width + 128 * len(sums), 128)
            ),
            (*back, *pre, in_bias[None, span], gain_sums[:, span], *sums),
            (),
        )

    def spread_out(act):
        mine = [None] * chips
        mine[0] = act
        for step in range(1, chips):
            act = next_chip(act)
            mine[(chips - step) % chips] = act
        return mine

    def both_cores(mine):
        return mine + [other_core(block) for block in mine]

    def summed_along_hid(sums, behind=()):
        arrivals = [along_hid(sums[step], -step) for step in range(1, hid_size)]
        return sum(tied(arrivals, behind)[0], start=sums[0])

    half_1 = halved(pre_1, pre_0[0])
    pre_0 = tied(pre_0, half_1[0])[0]
    act_0, sums_0 = slope_product(slice(0, 2 * third), back_0, pre_0, ())
    pre_1 = exchanged(half_1)
    act_1, _ = slope_product(slice(2 * third, hidden), back_1, pre_1, (sums_0,))
    acts_0, acts_1 = spread_out(act_0), spread_out(act_1)
    sums = backward(both_cores(acts_0), in_parts[:8], place, (), 0, 1, [])
    acts_1[1:], sums = tied(acts_1[1:], sums)
    acts_1 = both_cores(acts_1)
    parts = 2 if depth % 512 == 0 else 1
    ends = []
    for part in range(parts):
        ends.append(backward(acts_1, in_parts[8:], place, sums, part, parts, [ends[-1][0]] if ends else []))
    first = summed_along_hid(ends[0])
    others = [summed_along_hid(end, first) for end in ends[1:]]
    width = depth // parts
    normed_grad = jnp.concatenate([first[:, :width], *others], axis=1) * norm_gain
    mean, slope = first[:, width : width + 1] / model_width, first[:, width + 1 : width + 2] / model_width
    return inv_std * (normed_grad - mean - normed * slope)


def solution(mesh):
    hid_size, emb_size = mesh.shape["hid"], mesh.shape["emb"]
    assert hid_size == emb_size and emb_size % 2 == 0
    return jax.shard_map(
        functools.partial(body, hid_size, emb_size),
        mesh=mesh,
        in_specs=(
            P(("groups", "hid"), "emb"),
            P(("groups", "hid"), "emb"),
            P("emb", "hid"),
            P("hid"),
            P("hid", "emb"),
            P("emb"),
        ),
        out_specs=P(("groups", "hid"), "emb"),
        check_vma=False,
    )
```

```python
import functools
import math

import jax
import jax.numpy as jnp
from jax import lax
from jax.experimental import pallas as pl
from jax.experimental.pallas import tpu as pltpu
from jax.sharding import PartitionSpec as P

VMEM_LIMIT = 5 * 1024 * 1024
SHORT = pl.CostEstimate(flops=1 << 20, bytes_accessed=1 << 18, transcendentals=0)


def gelu_slope(values):
    cdf = 0.5 * (1.0 + lax.erf(values * (1.0 / math.sqrt(2.0))))
    density = jnp.exp(-0.5 * values * values) * (1.0 / math.sqrt(2.0 * math.pi))
    return cdf + values * density


def split(values):
    high = values.astype(jnp.bfloat16)
    return high, (values - high.astype(jnp.float32)).astype(jnp.bfloat16)


def divisor(extent, *choices):
    return next(c for c in choices if extent % c == 0)


def call(kernel, out_shape, operands, after):
    outs = out_shape if isinstance(out_shape, tuple) else (out_shape,)

    def run(*refs):
        kernel(*refs[: len(operands)], *refs[len(operands) + len(after) :])

    inside = pl.BlockSpec(memory_space=pltpu.VMEM)
    result = pl.pallas_call(
        run,
        out_shape=tuple(jax.ShapeDtypeStruct(o.shape, o.dtype) for o in outs),
        in_specs=[inside] * len(operands) + [pl.BlockSpec(memory_space=pl.ANY)] * len(after),
        out_specs=[inside] * len(outs),
        compiler_params=pltpu.CompilerParams(vmem_limit_bytes=VMEM_LIMIT),
        cost_estimate=SHORT,
    )(*operands, *after)
    return result if isinstance(out_shape, tuple) else result[0]


def moments_kernel(inputs_ref, out_ref):
    rows, depth = inputs_ref.shape
    mean = jnp.sum(inputs_ref[...], axis=1, keepdims=True) * (1.0 / depth)
    square = jnp.sum(jnp.square(inputs_ref[...] - mean), axis=1, keepdims=True)
    out_ref[:rows] = jnp.broadcast_to(mean, (rows, 128))
    out_ref[rows:] = jnp.broadcast_to(square, (rows, 128))


def merge(moments, count):
    rows = moments[0].shape[0] // 2
    mean = sum(part[:rows] for part in moments) * (1.0 / len(moments))
    square = sum(part[rows:] + count * jnp.square(part[:rows] - mean) for part in moments)
    return mean, square


def merge_kernel(count, first_ref, second_ref, out_ref):
    rows = out_ref.shape[0] // 2
    out_ref[:rows], out_ref[rows:] = merge((first_ref[...], second_ref[...]), count)


def normalise_kernel(count, inputs_ref, gain_ref, *refs):
    *moment_refs, normed_ref, scaled_ref, inv_std_ref = refs
    mean, square = merge([ref[...] for ref in moment_refs], count)
    inv_std = 1.0 / jnp.sqrt(square * (1.0 / (count * len(moment_refs))) + 1e-06)
    normed = (inputs_ref[...] - mean[:, :1]) * inv_std[:, :1]
    normed_ref[...] = normed
    scaled_ref[...] = normed * gain_ref[...]
    inv_std_ref[...] = inv_std


def slope_kernel(terms, *refs):
    back_refs, pre_refs, bias_ref = refs[:terms], refs[terms : 2 * terms], refs[2 * terms]
    *others, act_ref, sums_ref = refs[2 * terms + 1 :]
    hidden = bias_ref.shape[1]
    product = sum(ref[...] for ref in pre_refs)
    act = sum(ref[...] for ref in back_refs) * gelu_slope(product + bias_ref[...])
    act_ref[:, :hidden] = act
    lane = lax.broadcasted_iota(jnp.int32, sums_ref.shape, 1)
    sums = jnp.where(lane == 1, jnp.sum(act * product, axis=1, keepdims=True), 0.0)
    if others:
        weight_ref, earlier_ref, earlier_weight_ref, earlier_sums_ref = others
        first = jnp.sum(act * weight_ref[...], axis=1, keepdims=True)
        first = first + jnp.sum(earlier_ref[...] * earlier_weight_ref[...], axis=1, keepdims=True)
        sums = sums + earlier_sums_ref[...] + jnp.where(lane == 0, first, 0.0)
        act_ref[:, hidden:] = sums
    sums_ref[...] = sums


def prepare_kernel(rows, columns, block, depth, weight_ref, gain_ref, *refs):
    *part_refs, sums_ref, landed, arrived, totals = refs
    totals[...] = jnp.zeros_like(totals)
    width = part_refs[0].shape[1]
    steps = rows[1] // block

    def fetch(step):
        start = pl.multiple_of(rows[0] + step * block, block)
        slot = lax.rem(step, depth)
        return pltpu.make_async_copy(
            weight_ref.at[pl.ds(start, block), pl.ds(*columns)], landed.at[slot], arrived.at[slot]
        )

    for step in range(min(depth, steps)):
        fetch(step).start()

    @pl.loop(0, steps)
    def _(step):
        fetch(step).wait()
        tile = landed[lax.rem(step, depth)]
        high, low = split(tile)
        at = pl.ds(pl.multiple_of(step * block, block), block)
        totals[...] += jnp.sum((tile * gain_ref[at, :]).reshape(block // 8, 8, columns[1]), axis=0)
        for n, part_ref in enumerate(part_refs):
            part_ref[at, :] = (low if n % 2 else high)[:, n // 2 * width : (n // 2 + 1) * width]

        @pl.when(step + depth < steps)
        def _():
            fetch(step + depth).start()

    sums_ref[...] = jnp.sum(totals[...], axis=0, keepdims=True)


def prepare(weight, gain, rows, columns, after):
    block = divisor(rows[1], *[b for b in (256, 128, 64, 32) if b <= max(256 * 1536 // columns[1], 32)])
    depth = 4
    outs = (pltpu.VMEM((rows[1], columns[1] // 2), jnp.bfloat16),) * 4
    inside, anywhere = pl.BlockSpec(memory_space=pltpu.VMEM), pl.BlockSpec(memory_space=pl.ANY)
    result = pl.pallas_call(
        lambda weight_ref, gain_ref, *refs: prepare_kernel(
            rows, columns, block, depth, weight_ref, gain_ref, *refs[len(after) :]
        ),
        out_shape=outs + (jax.ShapeDtypeStruct((1, columns[1]), jnp.float32),),
        in_specs=[anywhere, inside] + [anywhere] * len(after),
        out_specs=[inside] * 5,
        scratch_shapes=[
            pltpu.VMEM((depth, block, columns[1]), jnp.float32),
            pltpu.SemaphoreType.DMA((depth,)),
            pltpu.VMEM((8, columns[1]), jnp.float32),
        ],
        compiler_params=pltpu.CompilerParams(vmem_limit_bytes=VMEM_LIMIT),
        cost_estimate=SHORT,
    )(pltpu.with_memory_space_constraint(weight, pltpu.HBM), gain, *after)
    return list(result[:4]), result[4]


def three_pass(both, high, low, contract):
    rows = both.shape[0] // 2
    dot = functools.partial(
        lax.dot_general,
        dimension_numbers=(((1,), (contract,)), ((), ())),
        preferred_element_type=jnp.float32,
    )
    first = dot(both[...], high)
    return first[:rows] + first[rows:] + dot(both[:rows, :], low)


def fill(both, block_refs, place_ref):
    count = block_refs[0].shape[0]
    total = both.shape[0] // 2
    for index, ref in enumerate(block_refs):
        high, low = split(ref[...])
        row = pl.multiple_of(place_ref[index] * count, count)
        both[pl.ds(row, count), :] = high
        both[pl.ds(total + row, count), :] = low


def follow(earlier_refs, out_refs):
    for earlier_ref, out_ref in zip(earlier_refs, out_refs):
        out_ref[:, : earlier_ref.shape[1]] = earlier_ref[...]
    return earlier_refs[0].shape[1] if earlier_refs else 0


def put(out_refs, at, value):
    row = 0
    for out_ref in out_refs:
        out_ref[:, at] = value[row : row + out_ref.shape[0]]
        row += out_ref.shape[0]


def parts_of(tokens, chips, hidden):
    block = tokens // (2 * chips)
    return [jax.ShapeDtypeStruct((n, hidden), jnp.float32) for n in (block, block * (chips - 1))] * 2


def forward_kernel(place_ref, slot_refs, weight_refs, earlier_refs, out_refs, both):
    fill(both, slot_refs, place_ref)
    column = follow(earlier_refs, out_refs)
    for high_ref, low_ref in zip(weight_refs[::2], weight_refs[1::2]):
        width = divisor(high_ref.shape[1], 256, 128)

        @pl.loop(0, high_ref.shape[1] // width, unroll=2)
        def _(step):
            at = pl.ds(pl.multiple_of(step * width, width), width)
            part = three_pass(both, high_ref[:, at], low_ref[:, at], 0)
            put(out_refs, pl.ds(pl.multiple_of(column + step * width, width), width), part)

        column += high_ref.shape[1]


def forward(slots, weights, place, earlier, after):
    tokens, depth = slots[0].shape[0] * len(slots), slots[0].shape[1]
    hidden = sum(w.shape[1] for w in weights[::2]) + (earlier[0].shape[1] if earlier else 0)
    inside, anywhere = pl.BlockSpec(memory_space=pltpu.VMEM), pl.BlockSpec(memory_space=pl.ANY)
    ends = [1 + len(slots), 1 + len(slots) + len(weights), 1 + len(slots) + len(weights) + len(earlier)]
    return pl.pallas_call(
        lambda *refs: forward_kernel(
            refs[0], refs[1 : ends[0]], refs[ends[0] : ends[1]], refs[ends[1] : ends[2]], refs[-5:-1], refs[-1]
        ),
        out_shape=parts_of(tokens, len(slots) // 2, hidden),
        in_specs=[pl.BlockSpec(memory_space=pltpu.SMEM)] + [inside] * (ends[2] - 1) + [anywhere] * len(after),
        out_specs=[inside] * 4,
        scratch_shapes=[pltpu.VMEM((2 * tokens, depth), jnp.bfloat16)],
        compiler_params=pltpu.CompilerParams(vmem_limit_bytes=VMEM_LIMIT),
        cost_estimate=SHORT,
    )(place, *slots, *[pltpu.with_memory_space_constraint(w, pltpu.VMEM) for w in weights], *earlier, *after)


def stream_kernel(first, depth, place_ref, slot_refs, weight_ref, out_refs, both, landed, arrived):
    width = landed.shape[1]
    steps = out_refs[0].shape[1] // width

    def fetch(step):
        start = pl.multiple_of(first + step * width, width)
        slot = lax.rem(step, depth)
        return pltpu.make_async_copy(weight_ref.at[pl.ds(start, width), :], landed.at[slot], arrived.at[slot])

    for step in range(min(depth, steps)):
        fetch(step).start()
    fill(both, slot_refs, place_ref)

    @pl.loop(0, steps)
    def _(step):
        fetch(step).wait()
        high, low = split(landed[lax.rem(step, depth)])
        put(out_refs, pl.ds(pl.multiple_of(step * width, width), width), three_pass(both, high, low, 1))

        @pl.when(step + depth < steps)
        def _():
            fetch(step + depth).start()


def stream(slots, weight, place, first, hidden, after):
    tokens, columns = slots[0].shape[0] * len(slots), slots[0].shape[1]
    width, depth = divisor(hidden, 256, 128), 4
    inside, anywhere = pl.BlockSpec(memory_space=pltpu.VMEM), pl.BlockSpec(memory_space=pl.ANY)
    last = 1 + len(slots)
    return pl.pallas_call(
        lambda *refs: stream_kernel(first, depth, refs[0], refs[1:last], refs[last], refs[-7:-3], *refs[-3:]),
        out_shape=parts_of(tokens, len(slots) // 2, hidden),
        in_specs=[pl.BlockSpec(memory_space=pltpu.SMEM)] + [inside] * len(slots) + [anywhere] * (1 + len(after)),
        out_specs=[inside] * 4,
        scratch_shapes=[
            pltpu.VMEM((2 * tokens, columns), jnp.bfloat16),
            pltpu.VMEM((depth, width, columns), jnp.float32),
            pltpu.SemaphoreType.DMA((depth,)),
        ],
        compiler_params=pltpu.CompilerParams(vmem_limit_bytes=8 * 1024 * 1024),
        cost_estimate=SHORT,
    )(place, *slots, pltpu.with_memory_space_constraint(weight, pltpu.HBM), *after)


def backward_kernel(first, depth, place_ref, act_refs, weight_refs, earlier_refs, out_refs, both, result, riders):
    block = act_refs[0].shape[0]
    total = block * len(act_refs)
    hidden = both.shape[1]
    for p, act_ref in enumerate(act_refs):
        if act_ref.shape[1] > hidden:
            riders[p * block : (p + 1) * block, :] = act_ref[:, hidden:]
        high, low = split(act_ref[:, :hidden])
        both[p * block : (p + 1) * block, :] = high
        both[total + p * block : total + (p + 1) * block, :] = low
    width = result.shape[1]

    if out_refs[0].shape[1] > depth:
        for b, out_ref in enumerate(out_refs):
            out_ref[:, depth:] = riders[pl.ds(pl.multiple_of(place_ref[b] * block, block), block), :]

    @pl.loop(0, depth // width)
    def _(step):
        at = pl.ds(pl.multiple_of(first + step * width, width), width)
        value, column = 0.0, 0
        for high_ref, low_ref in zip(weight_refs[::2], weight_refs[1::2]):
            columns = slice(column, column + high_ref.shape[1])
            value += three_pass(both[:, columns], high_ref[at, :], low_ref[at, :], 1)
            column = columns.stop
        result[...] = value
        for b, out_ref in enumerate(out_refs):
            rows = result[pl.ds(pl.multiple_of(place_ref[b] * block, block), block), :]
            local = pl.ds(pl.multiple_of(step * width, width), width)
            out_ref[:, local] = rows + earlier_refs[b][:, local] if earlier_refs else rows


def backward(acts, weights, place, earlier, part, parts, after):
    slots, block, hidden = len(acts), acts[0].shape[0], sum(w.shape[1] for w in weights[::2])
    riding = acts[0].shape[1] - hidden if part == 0 else 0
    depth = weights[0].shape[0] // parts
    width = divisor(depth, 256, 128)
    out = jax.ShapeDtypeStruct((block, depth + riding), jnp.float32)
    inside, anywhere = pl.BlockSpec(memory_space=pltpu.VMEM), pl.BlockSpec(memory_space=pl.ANY)
    ends = [1 + slots, 1 + slots + len(weights), 1 + slots + len(weights) + len(earlier)]
    return pl.pallas_call(
        lambda *refs: backward_kernel(
            part * depth,
            depth,
            refs[0],
            refs[1 : ends[0]],
            refs[ends[0] : ends[1]],
            refs[ends[1] : ends[2]],
            refs[-3 - slots : -3],
            *refs[-3:],
        ),
        out_shape=[out] * slots,
        in_specs=[pl.BlockSpec(memory_space=pltpu.SMEM)] + [inside] * (ends[2] - 1) + [anywhere] * len(after),
        out_specs=[inside] * slots,
        scratch_shapes=[
            pltpu.VMEM((2 * block * slots, hidden), jnp.bfloat16),
            pltpu.VMEM((block * slots, width), jnp.float32),
            pltpu.VMEM((block * slots, 128), jnp.float32),
        ],
        compiler_params=pltpu.CompilerParams(vmem_limit_bytes=VMEM_LIMIT),
        cost_estimate=SHORT,
    )(place, *acts, *[pltpu.with_memory_space_constraint(w, pltpu.VMEM) for w in weights], *earlier, *after)


def body(hid_size, emb_size, inputs, out_grad, in_weight, in_bias, out_weight, norm_gain):
    chips = emb_size // 2
    tokens, depth = inputs.shape
    model_width = depth * emb_size
    hidden = in_weight.shape[1]
    me = lax.axis_index("emb")
    chip, core = me // 2, me % 2

    def along_hid(values, steps=1):
        return lax.ppermute(values, "hid", [(i, (i + steps) % hid_size) for i in range(hid_size)])

    def other_core(values):
        return lax.ppermute(values, "emb", [(i, i ^ 1) for i in range(emb_size)])

    def next_chip(values):
        return lax.ppermute(values, "emb", [(i, (i + 2) % emb_size) for i in range(emb_size)])

    owner = jnp.arange(emb_size, dtype=jnp.int32)
    place = ((owner % 2) ^ core) * chips + (owner // 2 - chip) % chips

    def gathered(values):
        return [values] + [along_hid(values, step) for step in range(1, hid_size)]

    def relayed(values):
        blocks = [values] + [None] * (hid_size - 1)
        for step in range(1, hid_size // 2 + 1):
            blocks[step] = along_hid(blocks[step - 1], 1)
        for step in range(1, hid_size - hid_size // 2):
            blocks[-step] = along_hid(blocks[(1 - step) % hid_size], -1)
        return blocks

    grads = gathered(out_grad)
    third = hidden // 3

    def tied(values, others):
        return lax.optimization_barrier((values, others))

    def halved(partial, behind=()):
        keep_own, keep, send_own, send = partial
        return keep + tied(other_core(send), behind)[0], (keep_own, other_core(send_own))

    def exchanged(half):
        summed, own = half
        terms = jnp.split(summed, chips - 1)
        arrival = next_chip(terms[chips - 2])
        for step in range(chips - 3, -1, -1):
            arrival = next_chip(arrival + terms[step])
        return arrival, *own

    def prepared(c, after):
        return prepare(in_weight, norm_gain[:, None], (0, depth), (c * third, third), after)

    moments = call(moments_kernel, jax.ShapeDtypeStruct((2 * tokens, 128), jnp.float32), (inputs,), ())
    in_parts, sums_0 = prepared(0, [place, moments])
    parts, sums_1 = prepared(1, [in_parts[0]])
    in_parts += parts
    moments = call(
        functools.partial(merge_kernel, depth), moments, (moments, other_core(moments)), (in_parts[4], *grads[1:])
    )
    parts = [moments]
    for _ in range(1, chips):
        parts.append(next_chip(parts[-1]))
    normed, scaled, inv_std = call(
        functools.partial(normalise_kernel, 2 * depth),
        (inputs, inputs, jax.ShapeDtypeStruct((tokens, 128), jnp.float32)),
        (inputs, norm_gain[None, :], *parts),
        (),
    )
    inv_std = inv_std[:, :1]
    scaled = relayed(scaled)
    back_0 = stream(grads, out_weight, place, 0, 2 * third, [scaled[0]])
    back_0, (scaled[1], scaled[-1]) = tied(back_0, (scaled[1], scaled[-1]))
    half_0 = halved(back_0)
    back_0 = exchanged(half_0)
    pre_0 = forward(scaled, in_parts, place, (), [half_0[0]])
    pre_0, back_0 = tied(pre_0, back_0)
    half_0 = halved(pre_0)
    pre_0 = exchanged(half_0)
    back_1 = stream(grads, out_weight, place, 2 * third, third, [half_0[0]])
    parts, sums_2 = prepared(2, [back_1[0]])
    in_parts += parts
    half_1 = halved(back_1, parts)
    back_1 = exchanged(half_1)

    def slope_product(span, back, pre, others, after):
        width = span.stop - span.start
        return call(
            functools.partial(slope_kernel, len(back)),
            tuple(
                jax.ShapeDtypeStruct((tokens, n), jnp.float32) for n in (width + 128 * bool(others), 128)
            ),
            (*back, *pre, in_bias[None, span], *others),
            after,
        )

    act_0, sums_act = slope_product(slice(0, 2 * third), back_0, pre_0, (), (parts[0],))
    pre_1 = forward(scaled, in_parts[8:], place, (), [act_0, half_1[0]])

    gain_sums, _ = tied(jnp.concatenate([sums_0, sums_1, sums_2], axis=1), pre_1)
    gain_sums = passing = gain_sums + other_core(gain_sums)
    for _ in range(1, chips):
        passing = next_chip(passing)
        gain_sums = gain_sums + passing
    half_1 = halved(pre_1, back_1[0])
    pre_1 = exchanged(half_1)

    def spread_out(act):
        mine = [None] * chips
        mine[0] = act
        for step in range(1, chips):
            act = next_chip(act)
            mine[(chips - step) % chips] = act
        return mine

    def both_cores(mine):
        return mine + [other_core(block) for block in mine]

    def summed_along_hid(sums, behind=()):
        arrivals = [along_hid(sums[step], -step) for step in range(1, hid_size)]
        return sum(tied(arrivals, behind)[0], start=sums[0])

    act_1, _ = slope_product(
        slice(2 * third, hidden),
        back_1,
        pre_1,
        (gain_sums[:, 2 * third :], act_0, gain_sums[:, : 2 * third], sums_act),
        (),
    )
    acts_0, acts_1 = spread_out(act_0), spread_out(act_1)
    acts_0[1:] = tied(acts_0[1:], act_1)[0]
    acts_0 = both_cores(acts_0)
    parts = 2 if depth % 512 == 0 else 1
    sums = [backward(acts_0, in_parts[:8], place, (), part, parts, ()) for part in range(parts)]
    acts_1[1:], sums = tied(acts_1[1:], sums)
    acts_1 = both_cores(acts_1)
    ends = []
    for part in range(parts):
        after = [ends[-1][0]] if ends else []
        ends.append(backward(acts_1, in_parts[8:], place, sums[part], part, parts, after))
    first = summed_along_hid(ends[0])
    others = [summed_along_hid(end, first) for end in ends[1:]]
    width = depth // parts
    normed_grad = jnp.concatenate([first[:, :width], *others], axis=1) * norm_gain
    mean, slope = first[:, width : width + 1] / model_width, first[:, width + 1 : width + 2] / model_width
    return inv_std * (normed_grad - mean - normed * slope)


def solution(mesh):
    hid_size, emb_size = mesh.shape["hid"], mesh.shape["emb"]
    assert hid_size == emb_size and emb_size % 2 == 0
    return jax.shard_map(
        functools.partial(body, hid_size, emb_size),
        mesh=mesh,
        in_specs=(
            P(("groups", "hid"), "emb"),
            P(("groups", "hid"), "emb"),
            P("emb", "hid"),
            P("hid"),
            P("hid", "emb"),
            P("emb"),
        ),
        out_specs=P(("groups", "hid"), "emb"),
        check_vma=False,
    )
```

```python
import functools
import math

import jax
import jax.numpy as jnp
from jax import lax
from jax.experimental import pallas as pl
from jax.experimental.pallas import tpu as pltpu
from jax.sharding import PartitionSpec as P

VMEM_LIMIT = 5 * 1024 * 1024
SHORT = pl.CostEstimate(flops=1 << 20, bytes_accessed=1 << 18, transcendentals=0)


def gelu_slope(values):
    cdf = 0.5 * (1.0 + lax.erf(values * (1.0 / math.sqrt(2.0))))
    density = jnp.exp(-0.5 * values * values) * (1.0 / math.sqrt(2.0 * math.pi))
    return cdf + values * density


def split(values):
    high = values.astype(jnp.bfloat16)
    return high, (values - high.astype(jnp.float32)).astype(jnp.bfloat16)


def divisor(extent, *choices):
    return next(c for c in choices if extent % c == 0)


def call(kernel, out_shape, operands, after):
    outs = out_shape if isinstance(out_shape, tuple) else (out_shape,)

    def run(*refs):
        kernel(*refs[: len(operands)], *refs[len(operands) + len(after) :])

    inside = pl.BlockSpec(memory_space=pltpu.VMEM)
    result = pl.pallas_call(
        run,
        out_shape=tuple(jax.ShapeDtypeStruct(o.shape, o.dtype) for o in outs),
        in_specs=[inside] * len(operands) + [pl.BlockSpec(memory_space=pl.ANY)] * len(after),
        out_specs=[inside] * len(outs),
        compiler_params=pltpu.CompilerParams(vmem_limit_bytes=VMEM_LIMIT),
        cost_estimate=SHORT,
    )(*operands, *after)
    return result if isinstance(out_shape, tuple) else result[0]


def moments_kernel(inputs_ref, out_ref):
    rows, depth = inputs_ref.shape
    mean = jnp.sum(inputs_ref[...], axis=1, keepdims=True) * (1.0 / depth)
    square = jnp.sum(jnp.square(inputs_ref[...] - mean), axis=1, keepdims=True)
    out_ref[:rows] = jnp.broadcast_to(mean, (rows, 128))
    out_ref[rows:] = jnp.broadcast_to(square, (rows, 128))


def merge(moments, count):
    rows = moments[0].shape[0] // 2
    mean = sum(part[:rows] for part in moments) * (1.0 / len(moments))
    square = sum(part[rows:] + count * jnp.square(part[:rows] - mean) for part in moments)
    return mean, square


def merge_kernel(count, first_ref, second_ref, out_ref):
    rows = out_ref.shape[0] // 2
    out_ref[:rows], out_ref[rows:] = merge((first_ref[...], second_ref[...]), count)


def normalise_kernel(count, inputs_ref, gain_ref, *refs):
    *moment_refs, normed_ref, scaled_ref, inv_std_ref = refs
    mean, square = merge([ref[...] for ref in moment_refs], count)
    inv_std = 1.0 / jnp.sqrt(square * (1.0 / (count * len(moment_refs))) + 1e-06)
    normed = (inputs_ref[...] - mean[:, :1]) * inv_std[:, :1]
    normed_ref[...] = normed
    scaled_ref[...] = normed * gain_ref[...]
    inv_std_ref[...] = inv_std


def slope_kernel(terms, *refs):
    back_refs, pre_refs, bias_ref = refs[:terms], refs[terms : 2 * terms], refs[2 * terms]
    *others, act_ref, sums_ref = refs[2 * terms + 1 :]
    hidden = bias_ref.shape[1]
    product = sum(ref[...] for ref in pre_refs)
    act = sum(ref[...] for ref in back_refs) * gelu_slope(product + bias_ref[...])
    act_ref[:, :hidden] = act
    lane = lax.broadcasted_iota(jnp.int32, sums_ref.shape, 1)
    sums = jnp.where(lane == 1, jnp.sum(act * product, axis=1, keepdims=True), 0.0)
    if others:
        weight_ref, earlier_ref, earlier_weight_ref, earlier_sums_ref = others
        first = jnp.sum(act * weight_ref[...], axis=1, keepdims=True)
        first = first + jnp.sum(earlier_ref[...] * earlier_weight_ref[...], axis=1, keepdims=True)
        sums = sums + earlier_sums_ref[...] + jnp.where(lane == 0, first, 0.0)
        act_ref[:, hidden:] = sums
    sums_ref[...] = sums


def prepare_kernel(rows, columns, block, depth, weight_ref, gain_ref, *refs):
    *part_refs, sums_ref, landed, arrived, totals = refs
    totals[...] = jnp.zeros_like(totals)
    width = part_refs[0].shape[1]
    steps = rows[1] // block

    def fetch(step):
        start = pl.multiple_of(rows[0] + step * block, block)
        slot = lax.rem(step, depth)
        return pltpu.make_async_copy(
            weight_ref.at[pl.ds(start, block), pl.ds(*columns)], landed.at[slot], arrived.at[slot]
        )

    for step in range(min(depth, steps)):
        fetch(step).start()

    @pl.loop(0, steps)
    def _(step):
        fetch(step).wait()
        tile = landed[lax.rem(step, depth)]
        high, low = split(tile)
        at = pl.ds(pl.multiple_of(step * block, block), block)
        totals[...] += jnp.sum((tile * gain_ref[at, :]).reshape(block // 8, 8, columns[1]), axis=0)
        for n, part_ref in enumerate(part_refs):
            part_ref[at, :] = (low if n % 2 else high)[:, n // 2 * width : (n // 2 + 1) * width]

        @pl.when(step + depth < steps)
        def _():
            fetch(step + depth).start()

    sums_ref[...] = jnp.sum(totals[...], axis=0, keepdims=True)


def prepare(weight, gain, rows, columns, after):
    block = divisor(rows[1], *[b for b in (256, 128, 64, 32) if b <= max(256 * 1536 // columns[1], 32)])
    depth = 4
    outs = (pltpu.VMEM((rows[1], columns[1] // 2), jnp.bfloat16),) * 4
    inside, anywhere = pl.BlockSpec(memory_space=pltpu.VMEM), pl.BlockSpec(memory_space=pl.ANY)
    result = pl.pallas_call(
        lambda weight_ref, gain_ref, *refs: prepare_kernel(
            rows, columns, block, depth, weight_ref, gain_ref, *refs[len(after) :]
        ),
        out_shape=outs + (jax.ShapeDtypeStruct((1, columns[1]), jnp.float32),),
        in_specs=[anywhere, inside] + [anywhere] * len(after),
        out_specs=[inside] * 5,
        scratch_shapes=[
            pltpu.VMEM((depth, block, columns[1]), jnp.float32),
            pltpu.SemaphoreType.DMA((depth,)),
            pltpu.VMEM((8, columns[1]), jnp.float32),
        ],
        compiler_params=pltpu.CompilerParams(vmem_limit_bytes=VMEM_LIMIT),
        cost_estimate=SHORT,
    )(pltpu.with_memory_space_constraint(weight, pltpu.HBM), gain, *after)
    return list(result[:4]), result[4]


def three_pass(both, high, low, contract):
    rows = both.shape[0] // 2
    dot = functools.partial(
        lax.dot_general,
        dimension_numbers=(((1,), (contract,)), ((), ())),
        preferred_element_type=jnp.float32,
    )
    first = dot(both[...], high)
    return first[:rows] + first[rows:] + dot(both[:rows, :], low)


def fill(both, block_refs, place_ref):
    count = block_refs[0].shape[0]
    total = both.shape[0] // 2
    for index, ref in enumerate(block_refs):
        high, low = split(ref[...])
        row = pl.multiple_of(place_ref[index] * count, count)
        both[pl.ds(row, count), :] = high
        both[pl.ds(total + row, count), :] = low


def follow(earlier_refs, out_refs):
    for earlier_ref, out_ref in zip(earlier_refs, out_refs):
        out_ref[:, : earlier_ref.shape[1]] = earlier_ref[...]
    return earlier_refs[0].shape[1] if earlier_refs else 0


def put(out_refs, at, value):
    row = 0
    for out_ref in out_refs:
        out_ref[:, at] = value[row : row + out_ref.shape[0]]
        row += out_ref.shape[0]


def parts_of(tokens, chips, hidden):
    block = tokens // (2 * chips)
    return [jax.ShapeDtypeStruct((n, hidden), jnp.float32) for n in (block, block * (chips - 1))] * 2


def forward_kernel(place_ref, slot_refs, weight_refs, earlier_refs, out_refs, both):
    fill(both, slot_refs, place_ref)
    column = follow(earlier_refs, out_refs)
    for high_ref, low_ref in zip(weight_refs[::2], weight_refs[1::2]):
        width = divisor(high_ref.shape[1], 256, 128)

        @pl.loop(0, high_ref.shape[1] // width, unroll=2)
        def _(step):
            at = pl.ds(pl.multiple_of(step * width, width), width)
            part = three_pass(both, high_ref[:, at], low_ref[:, at], 0)
            put(out_refs, pl.ds(pl.multiple_of(column + step * width, width), width), part)

        column += high_ref.shape[1]


def forward(slots, weights, place, earlier, after):
    tokens, depth = slots[0].shape[0] * len(slots), slots[0].shape[1]
    hidden = sum(w.shape[1] for w in weights[::2]) + (earlier[0].shape[1] if earlier else 0)
    inside, anywhere = pl.BlockSpec(memory_space=pltpu.VMEM), pl.BlockSpec(memory_space=pl.ANY)
    ends = [1 + len(slots), 1 + len(slots) + len(weights), 1 + len(slots) + len(weights) + len(earlier)]
    return pl.pallas_call(
        lambda *refs: forward_kernel(
            refs[0], refs[1 : ends[0]], refs[ends[0] : ends[1]], refs[ends[1] : ends[2]], refs[-5:-1], refs[-1]
        ),
        out_shape=parts_of(tokens, len(slots) // 2, hidden),
        in_specs=[pl.BlockSpec(memory_space=pltpu.SMEM)] + [inside] * (ends[2] - 1) + [anywhere] * len(after),
        out_specs=[inside] * 4,
        scratch_shapes=[pltpu.VMEM((2 * tokens, depth), jnp.bfloat16)],
        compiler_params=pltpu.CompilerParams(vmem_limit_bytes=VMEM_LIMIT),
        cost_estimate=SHORT,
    )(place, *slots, *[pltpu.with_memory_space_constraint(w, pltpu.VMEM) for w in weights], *earlier, *after)


def stream_kernel(first, depth, place_ref, slot_refs, weight_ref, out_refs, both, landed, arrived):
    width = landed.shape[1]
    steps = out_refs[0].shape[1] // width

    def fetch(step):
        start = pl.multiple_of(first + step * width, width)
        slot = lax.rem(step, depth)
        return pltpu.make_async_copy(weight_ref.at[pl.ds(start, width), :], landed.at[slot], arrived.at[slot])

    for step in range(min(depth, steps)):
        fetch(step).start()
    fill(both, slot_refs, place_ref)

    @pl.loop(0, steps)
    def _(step):
        fetch(step).wait()
        high, low = split(landed[lax.rem(step, depth)])
        put(out_refs, pl.ds(pl.multiple_of(step * width, width), width), three_pass(both, high, low, 1))

        @pl.when(step + depth < steps)
        def _():
            fetch(step + depth).start()


def stream(slots, weight, place, first, hidden, after):
    tokens, columns = slots[0].shape[0] * len(slots), slots[0].shape[1]
    width, depth = divisor(hidden, 256, 128), 4
    inside, anywhere = pl.BlockSpec(memory_space=pltpu.VMEM), pl.BlockSpec(memory_space=pl.ANY)
    last = 1 + len(slots)
    return pl.pallas_call(
        lambda *refs: stream_kernel(first, depth, refs[0], refs[1:last], refs[last], refs[-7:-3], *refs[-3:]),
        out_shape=parts_of(tokens, len(slots) // 2, hidden),
        in_specs=[pl.BlockSpec(memory_space=pltpu.SMEM)] + [inside] * len(slots) + [anywhere] * (1 + len(after)),
        out_specs=[inside] * 4,
        scratch_shapes=[
            pltpu.VMEM((2 * tokens, columns), jnp.bfloat16),
            pltpu.VMEM((depth, width, columns), jnp.float32),
            pltpu.SemaphoreType.DMA((depth,)),
        ],
        compiler_params=pltpu.CompilerParams(vmem_limit_bytes=8 * 1024 * 1024),
        cost_estimate=SHORT,
    )(place, *slots, pltpu.with_memory_space_constraint(weight, pltpu.HBM), *after)


def backward_kernel(first, depth, place_ref, act_refs, weight_refs, earlier_refs, out_refs, both, result, riders):
    block = act_refs[0].shape[0]
    total = block * len(act_refs)
    hidden = both.shape[1]
    for p, act_ref in enumerate(act_refs):
        if act_ref.shape[1] > hidden:
            riders[p * block : (p + 1) * block, :] = act_ref[:, hidden:]
        high, low = split(act_ref[:, :hidden])
        both[p * block : (p + 1) * block, :] = high
        both[total + p * block : total + (p + 1) * block, :] = low
    width = result.shape[1]

    if out_refs[0].shape[1] > depth:
        for b, out_ref in enumerate(out_refs):
            out_ref[:, depth:] = riders[pl.ds(pl.multiple_of(place_ref[b] * block, block), block), :]

    @pl.loop(0, depth // width)
    def _(step):
        at = pl.ds(pl.multiple_of(first + step * width, width), width)
        value, column = 0.0, 0
        for high_ref, low_ref in zip(weight_refs[::2], weight_refs[1::2]):
            columns = slice(column, column + high_ref.shape[1])
            value += three_pass(both[:, columns], high_ref[at, :], low_ref[at, :], 1)
            column = columns.stop
        result[...] = value
        for b, out_ref in enumerate(out_refs):
            rows = result[pl.ds(pl.multiple_of(place_ref[b] * block, block), block), :]
            local = pl.ds(pl.multiple_of(step * width, width), width)
            out_ref[:, local] = rows + earlier_refs[b][:, local] if earlier_refs else rows


def backward(acts, weights, place, earlier, part, parts, after):
    slots, block, hidden = len(acts), acts[0].shape[0], sum(w.shape[1] for w in weights[::2])
    riding = acts[0].shape[1] - hidden if part == 0 else 0
    depth = weights[0].shape[0] // parts
    width = divisor(depth, 256, 128)
    out = jax.ShapeDtypeStruct((block, depth + riding), jnp.float32)
    inside, anywhere = pl.BlockSpec(memory_space=pltpu.VMEM), pl.BlockSpec(memory_space=pl.ANY)
    ends = [1 + slots, 1 + slots + len(weights), 1 + slots + len(weights) + len(earlier)]
    return pl.pallas_call(
        lambda *refs: backward_kernel(
            part * depth,
            depth,
            refs[0],
            refs[1 : ends[0]],
            refs[ends[0] : ends[1]],
            refs[ends[1] : ends[2]],
            refs[-3 - slots : -3],
            *refs[-3:],
        ),
        out_shape=[out] * slots,
        in_specs=[pl.BlockSpec(memory_space=pltpu.SMEM)] + [inside] * (ends[2] - 1) + [anywhere] * len(after),
        out_specs=[inside] * slots,
        scratch_shapes=[
            pltpu.VMEM((2 * block * slots, hidden), jnp.bfloat16),
            pltpu.VMEM((block * slots, width), jnp.float32),
            pltpu.VMEM((block * slots, 128), jnp.float32),
        ],
        compiler_params=pltpu.CompilerParams(vmem_limit_bytes=VMEM_LIMIT),
        cost_estimate=SHORT,
    )(place, *acts, *[pltpu.with_memory_space_constraint(w, pltpu.VMEM) for w in weights], *earlier, *after)


def body(hid_size, emb_size, inputs, out_grad, in_weight, in_bias, out_weight, norm_gain):
    chips = emb_size // 2
    tokens, depth = inputs.shape
    model_width = depth * emb_size
    hidden = in_weight.shape[1]
    me = lax.axis_index("emb")
    chip, core = me // 2, me % 2

    def along_hid(values, steps=1):
        return lax.ppermute(values, "hid", [(i, (i + steps) % hid_size) for i in range(hid_size)])

    def other_core(values):
        return lax.ppermute(values, "emb", [(i, i ^ 1) for i in range(emb_size)])

    def next_chip(values):
        return lax.ppermute(values, "emb", [(i, (i + 2) % emb_size) for i in range(emb_size)])

    owner = jnp.arange(emb_size, dtype=jnp.int32)
    place = ((owner % 2) ^ core) * chips + (owner // 2 - chip) % chips

    def gathered(values):
        return [values] + [along_hid(values, step) for step in range(1, hid_size)]

    def relayed(values):
        blocks = [values] + [None] * (hid_size - 1)
        for step in range(1, hid_size // 2 + 1):
            blocks[step] = along_hid(blocks[step - 1], 1)
        for step in range(1, hid_size - hid_size // 2):
            blocks[-step] = along_hid(blocks[(1 - step) % hid_size], -1)
        return blocks

    grads = gathered(out_grad)
    third = hidden // 3

    def tied(values, others):
        return lax.optimization_barrier((values, others))

    def halved(partial, behind=()):
        keep_own, keep, send_own, send = partial
        return keep + tied(other_core(send), behind)[0], (keep_own, other_core(send_own))

    def exchanged(half):
        summed, own = half
        terms = jnp.split(summed, chips - 1)
        arrival = next_chip(terms[chips - 2])
        for step in range(chips - 3, -1, -1):
            arrival = next_chip(arrival + terms[step])
        return arrival, *own

    def prepared(c, after):
        return prepare(in_weight, norm_gain[:, None], (0, depth), (c * third, third), after)

    moments = call(moments_kernel, jax.ShapeDtypeStruct((2 * tokens, 128), jnp.float32), (inputs,), ())
    in_parts, sums_0 = prepared(0, [place, moments])
    parts, sums_1 = prepared(1, [in_parts[0]])
    in_parts += parts
    moments = call(
        functools.partial(merge_kernel, depth), moments, (moments, other_core(moments)), (in_parts[4], *grads[1:])
    )
    parts = [moments]
    for _ in range(1, chips):
        parts.append(next_chip(parts[-1]))
    normed, scaled, inv_std = call(
        functools.partial(normalise_kernel, 2 * depth),
        (inputs, inputs, jax.ShapeDtypeStruct((tokens, 128), jnp.float32)),
        (inputs, norm_gain[None, :], *parts),
        (),
    )
    inv_std = inv_std[:, :1]
    scaled = relayed(scaled)
    back_0 = stream(grads, out_weight, place, 0, 2 * third, [scaled[0]])
    back_0, (scaled[1], scaled[-1]) = tied(back_0, (scaled[1], scaled[-1]))
    half_0 = halved(back_0)
    back_0 = exchanged(half_0)
    parts, sums_2 = prepared(2, [half_0[0]])
    in_parts += parts

    gain_sums = jnp.concatenate([sums_0, sums_1, sums_2], axis=1)
    gain_sums = passing = gain_sums + other_core(gain_sums)
    for _ in range(1, chips):
        passing = next_chip(passing)
        gain_sums = gain_sums + passing

    pre_0 = forward(scaled, in_parts[:8], place, (), [parts[0]])
    pre_0, (back_0, gain_sums) = tied(pre_0, (back_0, gain_sums))
    half_0 = halved(pre_0)
    pre_0 = exchanged(half_0)
    back_1 = stream(grads, out_weight, place, 2 * third, third, [half_0[0]])
    pre_1 = forward(scaled, in_parts[8:], place, (), [back_1[0]])
    half_1 = halved(back_1, pre_1)
    back_1 = exchanged(half_1)

    def slope_product(span, back, pre, others, after):
        width = span.stop - span.start
        return call(
            functools.partial(slope_kernel, len(back)),
            tuple(
                jax.ShapeDtypeStruct((tokens, n), jnp.float32) for n in (width + 128 * bool(others), 128)
            ),
            (*back, *pre, in_bias[None, span], *others),
            after,
        )

    act_0, sums_act = slope_product(slice(0, 2 * third), back_0, pre_0, (), (half_1[0],))
    half_1 = halved(pre_1, back_1[0])
    pre_1 = exchanged(half_1)

    def spread_out(act):
        mine = [None] * chips
        mine[0] = act
        for step in range(1, chips):
            act = next_chip(act)
            mine[(chips - step) % chips] = act
        return mine

    def both_cores(mine):
        return mine + [other_core(block) for block in mine]

    def summed_along_hid(sums, behind=()):
        arrivals = [along_hid(sums[step], -step) for step in range(1, hid_size)]
        return sum(tied(arrivals, behind)[0], start=sums[0])

    act_1, _ = slope_product(
        slice(2 * third, hidden),
        back_1,
        pre_1,
        (gain_sums[:, 2 * third :], act_0, gain_sums[:, : 2 * third], sums_act),
        (),
    )
    acts_0, acts_1 = spread_out(act_0), spread_out(act_1)
    acts_0[1:] = tied(acts_0[1:], act_1)[0]
    acts_0 = both_cores(acts_0)
    parts = 2 if depth % 512 == 0 else 1
    sums = [backward(acts_0, in_parts[:8], place, (), part, parts, ()) for part in range(parts)]
    acts_1[1:], sums = tied(acts_1[1:], sums)
    acts_1 = both_cores(acts_1)
    ends = []
    for part in range(parts):
        after = [ends[-1][0]] if ends else []
        ends.append(backward(acts_1, in_parts[8:], place, sums[part], part, parts, after))
    first = summed_along_hid(ends[0])
    others = [summed_along_hid(end, first) for end in ends[1:]]
    width = depth // parts
    normed_grad = jnp.concatenate([first[:, :width], *others], axis=1) * norm_gain
    mean, slope = first[:, width : width + 1] / model_width, first[:, width + 1 : width + 2] / model_width
    return inv_std * (normed_grad - mean - normed * slope)


def solution(mesh):
    hid_size, emb_size = mesh.shape["hid"], mesh.shape["emb"]
    assert hid_size == emb_size and emb_size % 2 == 0
    return jax.shard_map(
        functools.partial(body, hid_size, emb_size),
        mesh=mesh,
        in_specs=(
            P(("groups", "hid"), "emb"),
            P(("groups", "hid"), "emb"),
            P("emb", "hid"),
            P("hid"),
            P("hid", "emb"),
            P("emb"),
        ),
        out_specs=P(("groups", "hid"), "emb"),
        check_vma=False,
    )
```

```python
import functools
import math

import jax
import jax.numpy as jnp
from jax import lax
from jax.experimental import pallas as pl
from jax.experimental.pallas import tpu as pltpu
from jax.sharding import PartitionSpec as P

VMEM_LIMIT = 5 * 1024 * 1024
SHORT = pl.CostEstimate(flops=1 << 20, bytes_accessed=1 << 18, transcendentals=0)


def gelu_slope(values):
    cdf = 0.5 * (1.0 + lax.erf(values * (1.0 / math.sqrt(2.0))))
    density = jnp.exp(-0.5 * values * values) * (1.0 / math.sqrt(2.0 * math.pi))
    return cdf + values * density


def split(values):
    high = values.astype(jnp.bfloat16)
    return high, (values - high.astype(jnp.float32)).astype(jnp.bfloat16)


def divisor(extent, *choices):
    return next(c for c in choices if extent % c == 0)


def call(kernel, out_shape, operands, after):
    outs = out_shape if isinstance(out_shape, tuple) else (out_shape,)

    def run(*refs):
        kernel(*refs[: len(operands)], *refs[len(operands) + len(after) :])

    inside = pl.BlockSpec(memory_space=pltpu.VMEM)
    result = pl.pallas_call(
        run,
        out_shape=tuple(jax.ShapeDtypeStruct(o.shape, o.dtype) for o in outs),
        in_specs=[inside] * len(operands) + [pl.BlockSpec(memory_space=pl.ANY)] * len(after),
        out_specs=[inside] * len(outs),
        compiler_params=pltpu.CompilerParams(vmem_limit_bytes=VMEM_LIMIT),
        cost_estimate=SHORT,
    )(*operands, *after)
    return result if isinstance(out_shape, tuple) else result[0]


def moments_kernel(inputs_ref, out_ref):
    rows, depth = inputs_ref.shape
    mean = jnp.sum(inputs_ref[...], axis=1, keepdims=True) * (1.0 / depth)
    square = jnp.sum(jnp.square(inputs_ref[...] - mean), axis=1, keepdims=True)
    out_ref[:rows] = jnp.broadcast_to(mean, (rows, 128))
    out_ref[rows:] = jnp.broadcast_to(square, (rows, 128))


def merge(moments, count):
    rows = moments[0].shape[0] // 2
    mean = sum(part[:rows] for part in moments) * (1.0 / len(moments))
    square = sum(part[rows:] + count * jnp.square(part[:rows] - mean) for part in moments)
    return mean, square


def merge_kernel(count, first_ref, second_ref, out_ref):
    rows = out_ref.shape[0] // 2
    out_ref[:rows], out_ref[rows:] = merge((first_ref[...], second_ref[...]), count)


def normalise_kernel(count, inputs_ref, gain_ref, *refs):
    *moment_refs, normed_ref, scaled_ref, inv_std_ref = refs
    mean, square = merge([ref[...] for ref in moment_refs], count)
    inv_std = 1.0 / jnp.sqrt(square * (1.0 / (count * len(moment_refs))) + 1e-06)
    normed = (inputs_ref[...] - mean[:, :1]) * inv_std[:, :1]
    normed_ref[...] = normed
    scaled_ref[...] = normed * gain_ref[...]
    inv_std_ref[...] = inv_std


def slope_kernel(terms, *refs):
    back_refs, pre_refs, bias_ref = refs[:terms], refs[terms : 2 * terms], refs[2 * terms]
    *others, act_ref, sums_ref = refs[2 * terms + 1 :]
    hidden = bias_ref.shape[1]
    product = sum(ref[...] for ref in pre_refs)
    act = sum(ref[...] for ref in back_refs) * gelu_slope(product + bias_ref[...])
    act_ref[:, :hidden] = act
    lane = lax.broadcasted_iota(jnp.int32, sums_ref.shape, 1)
    sums = jnp.where(lane == 1, jnp.sum(act * product, axis=1, keepdims=True), 0.0)
    if others:
        weight_ref, earlier_ref, earlier_weight_ref, earlier_sums_ref = others
        first = jnp.sum(act * weight_ref[...], axis=1, keepdims=True)
        first = first + jnp.sum(earlier_ref[...] * earlier_weight_ref[...], axis=1, keepdims=True)
        sums = sums + earlier_sums_ref[...] + jnp.where(lane == 0, first, 0.0)
        act_ref[:, hidden:] = sums
    sums_ref[...] = sums


def prepare_kernel(rows, columns, block, depth, weight_ref, gain_ref, *refs):
    *part_refs, sums_ref, landed, arrived, totals = refs
    totals[...] = jnp.zeros_like(totals)
    width = part_refs[0].shape[1]
    steps = rows[1] // block

    def fetch(step):
        start = pl.multiple_of(rows[0] + step * block, block)
        slot = lax.rem(step, depth)
        return pltpu.make_async_copy(
            weight_ref.at[pl.ds(start, block), pl.ds(*columns)], landed.at[slot], arrived.at[slot]
        )

    for step in range(min(depth, steps)):
        fetch(step).start()

    @pl.loop(0, steps)
    def _(step):
        fetch(step).wait()
        tile = landed[lax.rem(step, depth)]
        high, low = split(tile)
        at = pl.ds(pl.multiple_of(step * block, block), block)
        totals[...] += jnp.sum((tile * gain_ref[at, :]).reshape(block // 8, 8, columns[1]), axis=0)
        for n, part_ref in enumerate(part_refs):
            part_ref[at, :] = (low if n % 2 else high)[:, n // 2 * width : (n // 2 + 1) * width]

        @pl.when(step + depth < steps)
        def _():
            fetch(step + depth).start()

    sums_ref[...] = jnp.sum(totals[...], axis=0, keepdims=True)


def prepare(weight, gain, rows, columns, after):
    block = divisor(rows[1], *[b for b in (256, 128, 64, 32) if b <= max(256 * 1536 // columns[1], 32)])
    depth = 4
    outs = (pltpu.VMEM((rows[1], columns[1] // 2), jnp.bfloat16),) * 4
    inside, anywhere = pl.BlockSpec(memory_space=pltpu.VMEM), pl.BlockSpec(memory_space=pl.ANY)
    result = pl.pallas_call(
        lambda weight_ref, gain_ref, *refs: prepare_kernel(
            rows, columns, block, depth, weight_ref, gain_ref, *refs[len(after) :]
        ),
        out_shape=outs + (jax.ShapeDtypeStruct((1, columns[1]), jnp.float32),),
        in_specs=[anywhere, inside] + [anywhere] * len(after),
        out_specs=[inside] * 5,
        scratch_shapes=[
            pltpu.VMEM((depth, block, columns[1]), jnp.float32),
            pltpu.SemaphoreType.DMA((depth,)),
            pltpu.VMEM((8, columns[1]), jnp.float32),
        ],
        compiler_params=pltpu.CompilerParams(vmem_limit_bytes=VMEM_LIMIT),
        cost_estimate=SHORT,
    )(pltpu.with_memory_space_constraint(weight, pltpu.HBM), gain, *after)
    return list(result[:4]), result[4]


def three_pass(both, high, low, contract):
    rows = both.shape[0] // 2
    dot = functools.partial(
        lax.dot_general,
        dimension_numbers=(((1,), (contract,)), ((), ())),
        preferred_element_type=jnp.float32,
    )
    first = dot(both[...], high)
    return first[:rows] + first[rows:] + dot(both[:rows, :], low)


def fill(both, block_refs, place_ref):
    count = block_refs[0].shape[0]
    total = both.shape[0] // 2
    for index, ref in enumerate(block_refs):
        high, low = split(ref[...])
        row = pl.multiple_of(place_ref[index] * count, count)
        both[pl.ds(row, count), :] = high
        both[pl.ds(total + row, count), :] = low


def follow(earlier_refs, out_refs):
    for earlier_ref, out_ref in zip(earlier_refs, out_refs):
        out_ref[:, : earlier_ref.shape[1]] = earlier_ref[...]
    return earlier_refs[0].shape[1] if earlier_refs else 0


def put(out_refs, at, value):
    row = 0
    for out_ref in out_refs:
        out_ref[:, at] = value[row : row + out_ref.shape[0]]
        row += out_ref.shape[0]


def parts_of(tokens, chips, hidden):
    block = tokens // (2 * chips)
    return [jax.ShapeDtypeStruct((n, hidden), jnp.float32) for n in (block, block * (chips - 1))] * 2


def forward_kernel(place_ref, slot_refs, weight_refs, earlier_refs, out_refs, both):
    fill(both, slot_refs, place_ref)
    column = follow(earlier_refs, out_refs)
    for high_ref, low_ref in zip(weight_refs[::2], weight_refs[1::2]):
        width = divisor(high_ref.shape[1], 256, 128)

        @pl.loop(0, high_ref.shape[1] // width, unroll=2)
        def _(step):
            at = pl.ds(pl.multiple_of(step * width, width), width)
            part = three_pass(both, high_ref[:, at], low_ref[:, at], 0)
            put(out_refs, pl.ds(pl.multiple_of(column + step * width, width), width), part)

        column += high_ref.shape[1]


def forward(slots, weights, place, earlier, after):
    tokens, depth = slots[0].shape[0] * len(slots), slots[0].shape[1]
    hidden = sum(w.shape[1] for w in weights[::2]) + (earlier[0].shape[1] if earlier else 0)
    inside, anywhere = pl.BlockSpec(memory_space=pltpu.VMEM), pl.BlockSpec(memory_space=pl.ANY)
    ends = [1 + len(slots), 1 + len(slots) + len(weights), 1 + len(slots) + len(weights) + len(earlier)]
    return pl.pallas_call(
        lambda *refs: forward_kernel(
            refs[0], refs[1 : ends[0]], refs[ends[0] : ends[1]], refs[ends[1] : ends[2]], refs[-5:-1], refs[-1]
        ),
        out_shape=parts_of(tokens, len(slots) // 2, hidden),
        in_specs=[pl.BlockSpec(memory_space=pltpu.SMEM)] + [inside] * (ends[2] - 1) + [anywhere] * len(after),
        out_specs=[inside] * 4,
        scratch_shapes=[pltpu.VMEM((2 * tokens, depth), jnp.bfloat16)],
        compiler_params=pltpu.CompilerParams(vmem_limit_bytes=VMEM_LIMIT),
        cost_estimate=SHORT,
    )(place, *slots, *[pltpu.with_memory_space_constraint(w, pltpu.VMEM) for w in weights], *earlier, *after)


def stream_kernel(first, depth, place_ref, slot_refs, weight_ref, out_refs, both, landed, arrived):
    width = landed.shape[1]
    steps = out_refs[0].shape[1] // width

    def fetch(step):
        start = pl.multiple_of(first + step * width, width)
        slot = lax.rem(step, depth)
        return pltpu.make_async_copy(weight_ref.at[pl.ds(start, width), :], landed.at[slot], arrived.at[slot])

    for step in range(min(depth, steps)):
        fetch(step).start()
    fill(both, slot_refs, place_ref)

    @pl.loop(0, steps)
    def _(step):
        fetch(step).wait()
        high, low = split(landed[lax.rem(step, depth)])
        put(out_refs, pl.ds(pl.multiple_of(step * width, width), width), three_pass(both, high, low, 1))

        @pl.when(step + depth < steps)
        def _():
            fetch(step + depth).start()


def stream(slots, weight, place, first, hidden, after):
    tokens, columns = slots[0].shape[0] * len(slots), slots[0].shape[1]
    width, depth = divisor(hidden, 256, 128), 4
    inside, anywhere = pl.BlockSpec(memory_space=pltpu.VMEM), pl.BlockSpec(memory_space=pl.ANY)
    last = 1 + len(slots)
    return pl.pallas_call(
        lambda *refs: stream_kernel(first, depth, refs[0], refs[1:last], refs[last], refs[-7:-3], *refs[-3:]),
        out_shape=parts_of(tokens, len(slots) // 2, hidden),
        in_specs=[pl.BlockSpec(memory_space=pltpu.SMEM)] + [inside] * len(slots) + [anywhere] * (1 + len(after)),
        out_specs=[inside] * 4,
        scratch_shapes=[
            pltpu.VMEM((2 * tokens, columns), jnp.bfloat16),
            pltpu.VMEM((depth, width, columns), jnp.float32),
            pltpu.SemaphoreType.DMA((depth,)),
        ],
        compiler_params=pltpu.CompilerParams(vmem_limit_bytes=8 * 1024 * 1024),
        cost_estimate=SHORT,
    )(place, *slots, pltpu.with_memory_space_constraint(weight, pltpu.HBM), *after)


def backward_kernel(first, depth, place_ref, act_refs, weight_refs, earlier_refs, out_refs, both, result, riders):
    block = act_refs[0].shape[0]
    total = block * len(act_refs)
    hidden = both.shape[1]
    for p, act_ref in enumerate(act_refs):
        if act_ref.shape[1] > hidden:
            riders[p * block : (p + 1) * block, :] = act_ref[:, hidden:]
        high, low = split(act_ref[:, :hidden])
        both[p * block : (p + 1) * block, :] = high
        both[total + p * block : total + (p + 1) * block, :] = low
    width = result.shape[1]

    if out_refs[0].shape[1] > depth:
        for b, out_ref in enumerate(out_refs):
            out_ref[:, depth:] = riders[pl.ds(pl.multiple_of(place_ref[b] * block, block), block), :]

    @pl.loop(0, depth // width)
    def _(step):
        at = pl.ds(pl.multiple_of(first + step * width, width), width)
        value, column = 0.0, 0
        for high_ref, low_ref in zip(weight_refs[::2], weight_refs[1::2]):
            columns = slice(column, column + high_ref.shape[1])
            value += three_pass(both[:, columns], high_ref[at, :], low_ref[at, :], 1)
            column = columns.stop
        result[...] = value
        for b, out_ref in enumerate(out_refs):
            rows = result[pl.ds(pl.multiple_of(place_ref[b] * block, block), block), :]
            local = pl.ds(pl.multiple_of(step * width, width), width)
            out_ref[:, local] = rows + earlier_refs[b][:, at] if earlier_refs else rows


def backward(acts, weights, place, earlier, part, parts, after):
    slots, block, hidden = len(acts), acts[0].shape[0], sum(w.shape[1] for w in weights[::2])
    riding = acts[0].shape[1] - hidden if part == 0 else 0
    depth = weights[0].shape[0] // parts
    width = divisor(depth, 256, 128)
    out = jax.ShapeDtypeStruct((block, depth + riding), jnp.float32)
    inside, anywhere = pl.BlockSpec(memory_space=pltpu.VMEM), pl.BlockSpec(memory_space=pl.ANY)
    ends = [1 + slots, 1 + slots + len(weights), 1 + slots + len(weights) + len(earlier)]
    return pl.pallas_call(
        lambda *refs: backward_kernel(
            part * depth,
            depth,
            refs[0],
            refs[1 : ends[0]],
            refs[ends[0] : ends[1]],
            refs[ends[1] : ends[2]],
            refs[-3 - slots : -3],
            *refs[-3:],
        ),
        out_shape=[out] * slots,
        in_specs=[pl.BlockSpec(memory_space=pltpu.SMEM)] + [inside] * (ends[2] - 1) + [anywhere] * len(after),
        out_specs=[inside] * slots,
        scratch_shapes=[
            pltpu.VMEM((2 * block * slots, hidden), jnp.bfloat16),
            pltpu.VMEM((block * slots, width), jnp.float32),
            pltpu.VMEM((block * slots, 128), jnp.float32),
        ],
        compiler_params=pltpu.CompilerParams(vmem_limit_bytes=VMEM_LIMIT),
        cost_estimate=SHORT,
    )(place, *acts, *[pltpu.with_memory_space_constraint(w, pltpu.VMEM) for w in weights], *earlier, *after)


def body(hid_size, emb_size, inputs, out_grad, in_weight, in_bias, out_weight, norm_gain):
    chips = emb_size // 2
    tokens, depth = inputs.shape
    model_width = depth * emb_size
    hidden = in_weight.shape[1]
    me = lax.axis_index("emb")
    chip, core = me // 2, me % 2

    def along_hid(values, steps=1):
        return lax.ppermute(values, "hid", [(i, (i + steps) % hid_size) for i in range(hid_size)])

    def other_core(values):
        return lax.ppermute(values, "emb", [(i, i ^ 1) for i in range(emb_size)])

    def next_chip(values):
        return lax.ppermute(values, "emb", [(i, (i + 2) % emb_size) for i in range(emb_size)])

    owner = jnp.arange(emb_size, dtype=jnp.int32)
    place = ((owner % 2) ^ core) * chips + (owner // 2 - chip) % chips

    def gathered(values):
        return [values] + [along_hid(values, step) for step in range(1, hid_size)]

    def relayed(values):
        blocks = [values] + [None] * (hid_size - 1)
        for step in range(1, hid_size // 2 + 1):
            blocks[step] = along_hid(blocks[step - 1], 1)
        for step in range(1, hid_size - hid_size // 2):
            blocks[-step] = along_hid(blocks[(1 - step) % hid_size], -1)
        return blocks

    grads = gathered(out_grad)
    third = hidden // 3

    def tied(values, others):
        return lax.optimization_barrier((values, others))

    def halved(partial, behind=()):
        keep_own, keep, send_own, send = partial
        return keep + tied(other_core(send), behind)[0], (keep_own, other_core(send_own))

    def exchanged(half):
        summed, own = half
        terms = jnp.split(summed, chips - 1)
        arrival = next_chip(terms[chips - 2])
        for step in range(chips - 3, -1, -1):
            arrival = next_chip(arrival + terms[step])
        return arrival, *own

    def prepared(c, after):
        return prepare(in_weight, norm_gain[:, None], (0, depth), (c * third, third), after)

    moments = call(moments_kernel, jax.ShapeDtypeStruct((2 * tokens, 128), jnp.float32), (inputs,), ())
    in_parts, sums_0 = prepared(0, [place, moments])
    parts, sums_1 = prepared(1, [in_parts[0]])
    in_parts += parts
    moments = call(
        functools.partial(merge_kernel, depth), moments, (moments, other_core(moments)), (in_parts[4], *grads[1:])
    )
    parts = [moments]
    for _ in range(1, chips):
        parts.append(next_chip(parts[-1]))
    normed, scaled, inv_std = call(
        functools.partial(normalise_kernel, 2 * depth),
        (inputs, inputs, jax.ShapeDtypeStruct((tokens, 128), jnp.float32)),
        (inputs, norm_gain[None, :], *parts),
        (),
    )
    inv_std = inv_std[:, :1]
    scaled = relayed(scaled)
    back_0 = stream(grads, out_weight, place, 0, 2 * third, [scaled[0]])
    back_0, (scaled[1], scaled[-1]) = tied(back_0, (scaled[1], scaled[-1]))
    half_0 = halved(back_0)
    back_0 = exchanged(half_0)
    back_1 = stream(grads, out_weight, place, 2 * third, third, [half_0[0]])
    back_1, scaled = tied(back_1, scaled)
    half_1 = halved(back_1, back_0[0])
    back_1 = exchanged(half_1)
    pre_0 = forward(scaled, in_parts, place, (), [half_1[0]])
    pre_0, back_1 = tied(pre_0, back_1)
    half_0 = halved(pre_0)
    pre_0 = exchanged(half_0)
    parts, sums_2 = prepared(2, [half_0[0]])
    in_parts += parts
    pre_1 = forward(scaled, parts, place, (), [])

    gain_sums = jnp.concatenate([sums_0, sums_1, sums_2], axis=1)
    gain_sums = passing = gain_sums + other_core(gain_sums)
    for _ in range(1, chips):
        passing = next_chip(passing)
        gain_sums = gain_sums + passing
    pre_1, gain_sums = tied(pre_1, gain_sums)

    def slope_product(span, back, pre, others, after):
        width = span.stop - span.start
        return call(
            functools.partial(slope_kernel, len(back)),
            tuple(
                jax.ShapeDtypeStruct((tokens, n), jnp.float32) for n in (width + 128 * bool(others), 128)
            ),
            (*back, *pre, in_bias[None, span], *others),
            after,
        )

    act_0, sums_act = slope_product(slice(0, 2 * third), back_0, pre_0, (), (pre_1[0],))
    pre_1 = exchanged(halved(pre_1))

    def spread_out(act):
        mine = [None] * chips
        mine[0] = act
        for step in range(1, chips):
            act = next_chip(act)
            mine[(chips - step) % chips] = act
        return mine

    def both_cores(mine):
        return mine + [other_core(block) for block in mine]

    def summed_along_hid(sums, behind=()):
        arrivals = [along_hid(sums[step], -step) for step in range(1, hid_size)]
        return sum(tied(arrivals, behind)[0], start=sums[0])

    act_1, _ = slope_product(
        slice(2 * third, hidden),
        back_1,
        pre_1,
        (gain_sums[:, 2 * third :], act_0, gain_sums[:, : 2 * third], sums_act),
        (),
    )
    acts_0, acts_1 = spread_out(act_0), spread_out(act_1)
    acts_0[1:] = tied(acts_0[1:], act_1)[0]
    acts_0 = both_cores(acts_0)
    parts = 2 if depth % 512 == 0 else 1
    sums = backward(acts_0, in_parts[:8], place, (), 0, 1, ())
    acts_1[1:], sums = tied(acts_1[1:], sums)
    acts_1 = both_cores(acts_1)
    ends = []
    for part in range(parts):
        after = [ends[-1][0]] if ends else []
        ends.append(backward(acts_1, in_parts[8:], place, sums, part, parts, after))
    first = summed_along_hid(ends[0])
    others = [summed_along_hid(end, first) for end in ends[1:]]
    width = depth // parts
    normed_grad = jnp.concatenate([first[:, :width], *others], axis=1) * norm_gain
    mean, slope = first[:, width : width + 1] / model_width, first[:, width + 1 : width + 2] / model_width
    return inv_std * (normed_grad - mean - normed * slope)


def solution(mesh):
    hid_size, emb_size = mesh.shape["hid"], mesh.shape["emb"]
    assert hid_size == emb_size and emb_size % 2 == 0
    return jax.shard_map(
        functools.partial(body, hid_size, emb_size),
        mesh=mesh,
        in_specs=(
            P(("groups", "hid"), "emb"),
            P(("groups", "hid"), "emb"),
            P("emb", "hid"),
            P("hid"),
            P("hid", "emb"),
            P("emb"),
        ),
        out_specs=P(("groups", "hid"), "emb"),
        check_vma=False,
    )
```

```python
import functools
import math

import jax
import jax.numpy as jnp
from jax import lax
from jax.experimental import pallas as pl
from jax.experimental.pallas import tpu as pltpu
from jax.sharding import PartitionSpec as P

VMEM_LIMIT = 5 * 1024 * 1024
SHORT = pl.CostEstimate(flops=1 << 20, bytes_accessed=1 << 18, transcendentals=0)


def gelu_slope(values):
    cdf = 0.5 * (1.0 + lax.erf(values * (1.0 / math.sqrt(2.0))))
    density = jnp.exp(-0.5 * values * values) * (1.0 / math.sqrt(2.0 * math.pi))
    return cdf + values * density


def split(values):
    high = values.astype(jnp.bfloat16)
    return high, (values - high.astype(jnp.float32)).astype(jnp.bfloat16)


def divisor(extent, *choices):
    return next(c for c in choices if extent % c == 0)


def call(kernel, out_shape, operands, after):
    outs = out_shape if isinstance(out_shape, tuple) else (out_shape,)

    def run(*refs):
        kernel(*refs[: len(operands)], *refs[len(operands) + len(after) :])

    inside = pl.BlockSpec(memory_space=pltpu.VMEM)
    result = pl.pallas_call(
        run,
        out_shape=tuple(jax.ShapeDtypeStruct(o.shape, o.dtype) for o in outs),
        in_specs=[inside] * len(operands) + [pl.BlockSpec(memory_space=pl.ANY)] * len(after),
        out_specs=[inside] * len(outs),
        compiler_params=pltpu.CompilerParams(vmem_limit_bytes=VMEM_LIMIT),
        cost_estimate=SHORT,
    )(*operands, *after)
    return result if isinstance(out_shape, tuple) else result[0]


def moments_kernel(inputs_ref, out_ref):
    rows, depth = inputs_ref.shape
    mean = jnp.sum(inputs_ref[...], axis=1, keepdims=True) * (1.0 / depth)
    square = jnp.sum(jnp.square(inputs_ref[...] - mean), axis=1, keepdims=True)
    out_ref[:rows] = jnp.broadcast_to(mean, (rows, 128))
    out_ref[rows:] = jnp.broadcast_to(square, (rows, 128))


def merge(moments, count):
    rows = moments[0].shape[0] // 2
    mean = sum(part[:rows] for part in moments) * (1.0 / len(moments))
    square = sum(part[rows:] + count * jnp.square(part[:rows] - mean) for part in moments)
    return mean, square


def merge_kernel(count, first_ref, second_ref, out_ref):
    rows = out_ref.shape[0] // 2
    out_ref[:rows], out_ref[rows:] = merge((first_ref[...], second_ref[...]), count)


def normalise_kernel(count, inputs_ref, gain_ref, *refs):
    *moment_refs, normed_ref, scaled_ref, inv_std_ref = refs
    mean, square = merge([ref[...] for ref in moment_refs], count)
    inv_std = 1.0 / jnp.sqrt(square * (1.0 / (count * len(moment_refs))) + 1e-06)
    normed = (inputs_ref[...] - mean[:, :1]) * inv_std[:, :1]
    normed_ref[...] = normed
    scaled_ref[...] = normed * gain_ref[...]
    inv_std_ref[...] = inv_std


def slope_kernel(terms, earlier, *refs):
    back_refs, pre_refs, (bias_ref, weight_ref) = refs[:terms], refs[terms : 2 * terms], refs[2 * terms : 2 * terms + 2]
    sums_refs, act_refs = refs[2 * terms + 2 : 2 * terms + 2 + earlier], refs[2 * terms + 2 + earlier : -1]
    out_sums_ref = refs[-1]
    hidden = bias_ref.shape[1]
    product = sum(ref[...] for ref in pre_refs)
    act = sum(ref[...] for ref in back_refs) * gelu_slope(product + bias_ref[...])
    width = hidden // len(act_refs)
    for n, act_ref in enumerate(act_refs):
        act_ref[:, :width] = act[:, n * width : (n + 1) * width]
    lane = lax.broadcasted_iota(jnp.int32, out_sums_ref.shape, 1)
    first = jnp.sum(act * weight_ref[...], axis=1, keepdims=True)
    second = jnp.sum(act * product, axis=1, keepdims=True)
    sums = jnp.where(lane == 0, first, jnp.where(lane == 1, second, 0.0)) + sum(ref[...] for ref in sums_refs)
    out_sums_ref[...] = sums
    if act_refs[-1].shape[1] > width:
        act_refs[-1][:, width:] = sums


def prepare_kernel(rows, columns, block, depth, weight_ref, gain_ref, *refs):
    *part_refs, sums_ref, landed, arrived, totals = refs
    totals[...] = jnp.zeros_like(totals)
    width = part_refs[0].shape[1]
    steps = rows[1] // block

    def fetch(step):
        start = pl.multiple_of(rows[0] + step * block, block)
        slot = lax.rem(step, depth)
        return pltpu.make_async_copy(
            weight_ref.at[pl.ds(start, block), pl.ds(*columns)], landed.at[slot], arrived.at[slot]
        )

    for step in range(min(depth, steps)):
        fetch(step).start()

    @pl.loop(0, steps)
    def _(step):
        fetch(step).wait()
        tile = landed[lax.rem(step, depth)]
        high, low = split(tile)
        at = pl.ds(pl.multiple_of(step * block, block), block)
        totals[...] += jnp.sum((tile * gain_ref[at, :]).reshape(block // 8, 8, columns[1]), axis=0)
        for n, part_ref in enumerate(part_refs):
            part_ref[at, :] = (low if n % 2 else high)[:, n // 2 * width : (n // 2 + 1) * width]

        @pl.when(step + depth < steps)
        def _():
            fetch(step + depth).start()

    sums_ref[...] = jnp.sum(totals[...], axis=0, keepdims=True)


def prepare(weight, gain, rows, columns, after):
    block = divisor(rows[1], *[b for b in (256, 128, 64, 32) if b <= max(256 * 1536 // columns[1], 32)])
    depth = 4
    outs = (pltpu.VMEM((rows[1], columns[1] // 2), jnp.bfloat16),) * 4
    inside, anywhere = pl.BlockSpec(memory_space=pltpu.VMEM), pl.BlockSpec(memory_space=pl.ANY)
    result = pl.pallas_call(
        lambda weight_ref, gain_ref, *refs: prepare_kernel(
            rows, columns, block, depth, weight_ref, gain_ref, *refs[len(after) :]
        ),
        out_shape=outs + (jax.ShapeDtypeStruct((1, columns[1]), jnp.float32),),
        in_specs=[anywhere, inside] + [anywhere] * len(after),
        out_specs=[inside] * 5,
        scratch_shapes=[
            pltpu.VMEM((depth, block, columns[1]), jnp.float32),
            pltpu.SemaphoreType.DMA((depth,)),
            pltpu.VMEM((8, columns[1]), jnp.float32),
        ],
        compiler_params=pltpu.CompilerParams(vmem_limit_bytes=VMEM_LIMIT),
        cost_estimate=SHORT,
    )(pltpu.with_memory_space_constraint(weight, pltpu.HBM), gain, *after)
    return list(result[:4]), result[4]


def three_pass(both, high, low, contract):
    rows = both.shape[0] // 2
    dot = functools.partial(
        lax.dot_general,
        dimension_numbers=(((1,), (contract,)), ((), ())),
        preferred_element_type=jnp.float32,
    )
    first = dot(both[...], high)
    return first[:rows] + first[rows:] + dot(both[:rows, :], low)


def fill(both, block_refs, place_ref):
    count = block_refs[0].shape[0]
    total = both.shape[0] // 2
    for index, ref in enumerate(block_refs):
        high, low = split(ref[...])
        row = pl.multiple_of(place_ref[index] * count, count)
        both[pl.ds(row, count), :] = high
        both[pl.ds(total + row, count), :] = low


def follow(earlier_refs, out_refs):
    for earlier_ref, out_ref in zip(earlier_refs, out_refs):
        out_ref[:, : earlier_ref.shape[1]] = earlier_ref[...]
    return earlier_refs[0].shape[1] if earlier_refs else 0


def put(out_refs, at, value):
    row = 0
    for out_ref in out_refs:
        out_ref[:, at] = value[row : row + out_ref.shape[0]]
        row += out_ref.shape[0]


def parts_of(tokens, chips, hidden):
    block = tokens // (2 * chips)
    return [jax.ShapeDtypeStruct((n, hidden), jnp.float32) for n in (block, block * (chips - 1))] * 2


def forward_kernel(place_ref, slot_refs, weight_refs, earlier_refs, out_refs, both):
    fill(both, slot_refs, place_ref)
    column = follow(earlier_refs, out_refs)
    for high_ref, low_ref in zip(weight_refs[::2], weight_refs[1::2]):
        width = divisor(high_ref.shape[1], 256, 128)

        @pl.loop(0, high_ref.shape[1] // width, unroll=2)
        def _(step):
            at = pl.ds(pl.multiple_of(step * width, width), width)
            part = three_pass(both, high_ref[:, at], low_ref[:, at], 0)
            put(out_refs, pl.ds(pl.multiple_of(column + step * width, width), width), part)

        column += high_ref.shape[1]


def forward(slots, weights, place, earlier, after):
    tokens, depth = slots[0].shape[0] * len(slots), slots[0].shape[1]
    hidden = sum(w.shape[1] for w in weights[::2]) + (earlier[0].shape[1] if earlier else 0)
    inside, anywhere = pl.BlockSpec(memory_space=pltpu.VMEM), pl.BlockSpec(memory_space=pl.ANY)
    ends = [1 + len(slots), 1 + len(slots) + len(weights), 1 + len(slots) + len(weights) + len(earlier)]
    return pl.pallas_call(
        lambda *refs: forward_kernel(
            refs[0], refs[1 : ends[0]], refs[ends[0] : ends[1]], refs[ends[1] : ends[2]], refs[-5:-1], refs[-1]
        ),
        out_shape=parts_of(tokens, len(slots) // 2, hidden),
        in_specs=[pl.BlockSpec(memory_space=pltpu.SMEM)] + [inside] * (ends[2] - 1) + [anywhere] * len(after),
        out_specs=[inside] * 4,
        scratch_shapes=[pltpu.VMEM((2 * tokens, depth), jnp.bfloat16)],
        compiler_params=pltpu.CompilerParams(vmem_limit_bytes=VMEM_LIMIT),
        cost_estimate=SHORT,
    )(place, *slots, *[pltpu.with_memory_space_constraint(w, pltpu.VMEM) for w in weights], *earlier, *after)


def stream_kernel(first, depth, place_ref, slot_refs, weight_ref, out_refs, both, landed, arrived):
    width = landed.shape[1]
    steps = out_refs[0].shape[1] // width

    def fetch(step):
        start = pl.multiple_of(first + step * width, width)
        slot = lax.rem(step, depth)
        return pltpu.make_async_copy(weight_ref.at[pl.ds(start, width), :], landed.at[slot], arrived.at[slot])

    for step in range(min(depth, steps)):
        fetch(step).start()
    fill(both, slot_refs, place_ref)

    @pl.loop(0, steps)
    def _(step):
        fetch(step).wait()
        high, low = split(landed[lax.rem(step, depth)])
        put(out_refs, pl.ds(pl.multiple_of(step * width, width), width), three_pass(both, high, low, 1))

        @pl.when(step + depth < steps)
        def _():
            fetch(step + depth).start()


def stream(slots, weight, place, first, hidden, after):
    tokens, columns = slots[0].shape[0] * len(slots), slots[0].shape[1]
    width, depth = divisor(hidden, 256, 128), 4
    inside, anywhere = pl.BlockSpec(memory_space=pltpu.VMEM), pl.BlockSpec(memory_space=pl.ANY)
    last = 1 + len(slots)
    return pl.pallas_call(
        lambda *refs: stream_kernel(first, depth, refs[0], refs[1:last], refs[last], refs[-7:-3], *refs[-3:]),
        out_shape=parts_of(tokens, len(slots) // 2, hidden),
        in_specs=[pl.BlockSpec(memory_space=pltpu.SMEM)] + [inside] * len(slots) + [anywhere] * (1 + len(after)),
        out_specs=[inside] * 4,
        scratch_shapes=[
            pltpu.VMEM((2 * tokens, columns), jnp.bfloat16),
            pltpu.VMEM((depth, width, columns), jnp.float32),
            pltpu.SemaphoreType.DMA((depth,)),
        ],
        compiler_params=pltpu.CompilerParams(vmem_limit_bytes=8 * 1024 * 1024),
        cost_estimate=SHORT,
    )(place, *slots, pltpu.with_memory_space_constraint(weight, pltpu.HBM), *after)


def backward_kernel(first, depth, place_ref, act_refs, weight_refs, earlier_refs, out_refs, both, result, riders):
    block = act_refs[0].shape[0]
    total = block * len(act_refs)
    hidden = both.shape[1]
    for p, act_ref in enumerate(act_refs):
        if act_ref.shape[1] > hidden:
            riders[p * block : (p + 1) * block, :] = act_ref[:, hidden:]
        high, low = split(act_ref[:, :hidden])
        both[p * block : (p + 1) * block, :] = high
        both[total + p * block : total + (p + 1) * block, :] = low
    width = result.shape[1]

    if out_refs[0].shape[1] > depth:
        for b, out_ref in enumerate(out_refs):
            out_ref[:, depth:] = riders[pl.ds(pl.multiple_of(place_ref[b] * block, block), block), :]

    @pl.loop(0, depth // width)
    def _(step):
        at = pl.ds(pl.multiple_of(first + step * width, width), width)
        value, column = 0.0, 0
        for high_ref, low_ref in zip(weight_refs[::2], weight_refs[1::2]):
            columns = slice(column, column + high_ref.shape[1])
            value += three_pass(both[:, columns], high_ref[at, :], low_ref[at, :], 1)
            column = columns.stop
        result[...] = value
        for b, out_ref in enumerate(out_refs):
            rows = result[pl.ds(pl.multiple_of(place_ref[b] * block, block), block), :]
            if earlier_refs:
                rows = rows + earlier_refs[b][:, at]
            out_ref[:, pl.ds(pl.multiple_of(step * width, width), width)] = rows


def backward(acts, weights, place, earlier, part, parts, after):
    slots, block, hidden = len(acts), acts[0].shape[0], sum(w.shape[1] for w in weights[::2])
    riding = acts[0].shape[1] - hidden if part == 0 else 0
    depth = weights[0].shape[0] // parts
    width = divisor(depth, 256, 128)
    out = jax.ShapeDtypeStruct((block, depth + riding), jnp.float32)
    inside, anywhere = pl.BlockSpec(memory_space=pltpu.VMEM), pl.BlockSpec(memory_space=pl.ANY)
    ends = [1 + slots, 1 + slots + len(weights), 1 + slots + len(weights) + len(earlier)]
    return pl.pallas_call(
        lambda *refs: backward_kernel(
            part * depth,
            depth,
            refs[0],
            refs[1 : ends[0]],
            refs[ends[0] : ends[1]],
            refs[ends[1] : ends[2]],
            refs[-3 - slots : -3],
            *refs[-3:],
        ),
        out_shape=[out] * slots,
        in_specs=[pl.BlockSpec(memory_space=pltpu.SMEM)] + [inside] * (ends[2] - 1) + [anywhere] * len(after),
        out_specs=[inside] * slots,
        scratch_shapes=[
            pltpu.VMEM((2 * block * slots, hidden), jnp.bfloat16),
            pltpu.VMEM((block * slots, width), jnp.float32),
            pltpu.VMEM((block * slots, 128), jnp.float32),
        ],
        compiler_params=pltpu.CompilerParams(vmem_limit_bytes=VMEM_LIMIT),
        cost_estimate=SHORT,
    )(place, *acts, *[pltpu.with_memory_space_constraint(w, pltpu.VMEM) for w in weights], *earlier, *after)


def body(hid_size, emb_size, inputs, out_grad, in_weight, in_bias, out_weight, norm_gain):
    chips = emb_size // 2
    tokens, depth = inputs.shape
    model_width = depth * emb_size
    hidden = in_weight.shape[1]
    me = lax.axis_index("emb")
    chip, core = me // 2, me % 2

    def along_hid(values, steps=1):
        return lax.ppermute(values, "hid", [(i, (i + steps) % hid_size) for i in range(hid_size)])

    def other_core(values):
        return lax.ppermute(values, "emb", [(i, i ^ 1) for i in range(emb_size)])

    def next_chip(values):
        return lax.ppermute(values, "emb", [(i, (i + 2) % emb_size) for i in range(emb_size)])

    owner = jnp.arange(emb_size, dtype=jnp.int32)
    place = ((owner % 2) ^ core) * chips + (owner // 2 - chip) % chips

    def gathered(values):
        return [values] + [along_hid(values, step) for step in range(1, hid_size)]

    def relayed(values):
        blocks = [values] + [None] * (hid_size - 1)
        for step in range(1, hid_size // 2 + 1):
            blocks[step] = along_hid(blocks[step - 1], 1)
        for step in range(1, hid_size - hid_size // 2):
            blocks[-step] = along_hid(blocks[(1 - step) % hid_size], -1)
        return blocks

    grads = gathered(out_grad)
    third = hidden // 3

    def tied(values, others):
        return lax.optimization_barrier((values, others))

    def halved(partial, behind=()):
        keep_own, keep, send_own, send = partial
        return keep + tied(other_core(send), behind)[0], (keep_own, other_core(send_own))

    def exchanged(half):
        summed, own = half
        terms = jnp.split(summed, chips - 1)
        arrival = next_chip(terms[chips - 2])
        for step in range(chips - 3, -1, -1):
            arrival = next_chip(arrival + terms[step])
        return arrival, *own

    def prepared(c, after):
        return prepare(in_weight, norm_gain[:, None], (0, depth), (c * third, third), after)

    moments = call(moments_kernel, jax.ShapeDtypeStruct((2 * tokens, 128), jnp.float32), (inputs,), ())
    in_parts, sums_0 = prepared(0, [place, moments])
    parts, sums_1 = prepared(1, [in_parts[0]])
    in_parts += parts
    moments = call(
        functools.partial(merge_kernel, depth), moments, (moments, other_core(moments)), (in_parts[4], *grads[1:])
    )
    parts = [moments]
    for _ in range(1, chips):
        parts.append(next_chip(parts[-1]))
    normed, scaled, inv_std = call(
        functools.partial(normalise_kernel, 2 * depth),
        (inputs, inputs, jax.ShapeDtypeStruct((tokens, 128), jnp.float32)),
        (inputs, norm_gain[None, :], *parts),
        (),
    )
    inv_std = inv_std[:, :1]
    scaled = relayed(scaled)
    back_0 = stream(grads, out_weight, place, 0, 2 * third, [scaled[0]])
    back_0, (scaled[1], scaled[-1]) = tied(back_0, (scaled[1], scaled[-1]))
    half_0 = halved(back_0)
    back_1 = stream(grads, out_weight, place, 2 * third, third, [half_0[0]])
    back_0 = exchanged(half_0)
    back_1, scaled = tied(back_1, scaled)
    pre_0 = forward(scaled, in_parts[:8], place, (), [back_1[0]])
    half_1 = halved(back_1, (pre_0, back_0[0]))
    back_1 = exchanged(half_1)
    half_0 = halved(pre_0)
    parts, sums_2 = prepared(2, [half_0[0], half_1[0]])
    in_parts += parts
    pre_1 = forward(scaled, in_parts[8:], place, (), [half_0[0], back_1[0]])
    pre_0 = exchanged(half_0)

    gain_sums, _ = tied(jnp.concatenate([sums_0, sums_1, sums_2], axis=1), pre_1)
    gain_sums = passing = gain_sums + other_core(gain_sums)
    for _ in range(1, chips):
        passing = next_chip(passing)
        gain_sums = gain_sums + passing

    def slope_product(span, back, pre, sums, after):
        pieces, room = (span.stop - span.start) // third, 128 * len(sums)
        widths = [third] * (pieces - 1) + [third + room, 128]
        return call(
            functools.partial(slope_kernel, len(back), len(sums)),
            tuple(jax.ShapeDtypeStruct((tokens, n), jnp.float32) for n in widths),
            (*back, *pre, in_bias[None, span], gain_sums[:, span], *sums),
            after,
        )

    def spread_out(act):
        mine = [None] * chips
        mine[0] = act
        for step in range(1, chips):
            act = next_chip(act)
            mine[(chips - step) % chips] = act
        return mine

    def both_cores(mine):
        return mine + [other_core(block) for block in mine]

    def summed_along_hid(sums, behind=()):
        arrivals = [along_hid(sums[step], -step) for step in range(1, hid_size)]
        return sum(tied(arrivals, behind)[0], start=sums[0])

    half_1 = halved(pre_1, pre_0[0])
    pre_0 = tied(pre_0, half_1[0])[0]
    act_0, act_1, sums_0 = slope_product(slice(0, 2 * third), back_0, pre_0, (), ())
    pre_1 = exchanged(half_1)
    sums = backward(both_cores(spread_out(act_0)), in_parts[:4], place, (), 0, 1, [])
    act_2, _ = slope_product(slice(2 * third, hidden), back_1, pre_1, (sums_0,), (sums[0],))
    acts_0, acts_1 = spread_out(act_1), spread_out(act_2)
    sums = backward(both_cores(acts_0), in_parts[4:8], place, sums, 0, 1, [act_2])
    acts_1[1:], sums = tied(acts_1[1:], sums)
    acts_1 = both_cores(acts_1)
    parts = 2 if depth % 512 == 0 else 1
    ends = []
    for part in range(parts):
        ends.append(backward(acts_1, in_parts[8:], place, sums, part, parts, [ends[-1][0]] if ends else []))
    first = summed_along_hid(ends[0])
    others = [summed_along_hid(end, first) for end in ends[1:]]
    width = depth // parts
    normed_grad = jnp.concatenate([first[:, :width], *others], axis=1) * norm_gain
    mean, slope = first[:, width : width + 1] / model_width, first[:, width + 1 : width + 2] / model_width
    return inv_std * (normed_grad - mean - normed * slope)


def solution(mesh):
    hid_size, emb_size = mesh.shape["hid"], mesh.shape["emb"]
    assert hid_size == emb_size and emb_size % 2 == 0
    return jax.shard_map(
        functools.partial(body, hid_size, emb_size),
        mesh=mesh,
        in_specs=(
            P(("groups", "hid"), "emb"),
            P(("groups", "hid"), "emb"),
            P("emb", "hid"),
            P("hid"),
            P("hid", "emb"),
            P("emb"),
        ),
        out_specs=P(("groups", "hid"), "emb"),
        check_vma=False,
    )
```

```python
import functools
import math

import jax
import jax.numpy as jnp
from jax import lax
from jax.experimental import pallas as pl
from jax.experimental.pallas import tpu as pltpu
from jax.sharding import PartitionSpec as P

VMEM_LIMIT = 5 * 1024 * 1024
SHORT = pl.CostEstimate(flops=1 << 20, bytes_accessed=1 << 18, transcendentals=0)


def gelu_slope(values):
    cdf = 0.5 * (1.0 + lax.erf(values * (1.0 / math.sqrt(2.0))))
    density = jnp.exp(-0.5 * values * values) * (1.0 / math.sqrt(2.0 * math.pi))
    return cdf + values * density


def split(values):
    high = values.astype(jnp.bfloat16)
    return high, (values - high.astype(jnp.float32)).astype(jnp.bfloat16)


def divisor(extent, *choices):
    return next(c for c in choices if extent % c == 0)


def call(kernel, out_shape, operands, after):
    outs = out_shape if isinstance(out_shape, tuple) else (out_shape,)

    def run(*refs):
        kernel(*refs[: len(operands)], *refs[len(operands) + len(after) :])

    inside = pl.BlockSpec(memory_space=pltpu.VMEM)
    result = pl.pallas_call(
        run,
        out_shape=tuple(jax.ShapeDtypeStruct(o.shape, o.dtype) for o in outs),
        in_specs=[inside] * len(operands) + [pl.BlockSpec(memory_space=pl.ANY)] * len(after),
        out_specs=[inside] * len(outs),
        compiler_params=pltpu.CompilerParams(vmem_limit_bytes=VMEM_LIMIT),
        cost_estimate=SHORT,
    )(*operands, *after)
    return result if isinstance(out_shape, tuple) else result[0]


def moments_kernel(inputs_ref, out_ref):
    rows, depth = inputs_ref.shape
    mean = jnp.sum(inputs_ref[...], axis=1, keepdims=True) * (1.0 / depth)
    square = jnp.sum(jnp.square(inputs_ref[...] - mean), axis=1, keepdims=True)
    out_ref[:rows] = jnp.broadcast_to(mean, (rows, 128))
    out_ref[rows:] = jnp.broadcast_to(square, (rows, 128))


def merge(moments, count):
    rows = moments[0].shape[0] // 2
    mean = sum(part[:rows] for part in moments) * (1.0 / len(moments))
    square = sum(part[rows:] + count * jnp.square(part[:rows] - mean) for part in moments)
    return mean, square


def merge_kernel(count, first_ref, second_ref, out_ref):
    rows = out_ref.shape[0] // 2
    out_ref[:rows], out_ref[rows:] = merge((first_ref[...], second_ref[...]), count)


def normalise_kernel(count, inputs_ref, gain_ref, *refs):
    *moment_refs, normed_ref, scaled_ref, inv_std_ref = refs
    mean, square = merge([ref[...] for ref in moment_refs], count)
    inv_std = 1.0 / jnp.sqrt(square * (1.0 / (count * len(moment_refs))) + 1e-06)
    normed = (inputs_ref[...] - mean[:, :1]) * inv_std[:, :1]
    normed_ref[...] = normed
    scaled_ref[...] = normed * gain_ref[...]
    inv_std_ref[...] = inv_std


def slope_kernel(terms, earlier, *refs):
    back_refs, pre_refs, (bias_ref, weight_ref) = refs[:terms], refs[terms : 2 * terms], refs[2 * terms : 2 * terms + 2]
    sums_refs, act_refs = refs[2 * terms + 2 : 2 * terms + 2 + earlier], refs[2 * terms + 2 + earlier : -1]
    out_sums_ref = refs[-1]
    hidden = bias_ref.shape[1]
    product = sum(ref[...] for ref in pre_refs)
    act = sum(ref[...] for ref in back_refs) * gelu_slope(product + bias_ref[...])
    width = hidden // len(act_refs)
    for n, act_ref in enumerate(act_refs):
        act_ref[:, :width] = act[:, n * width : (n + 1) * width]
    lane = lax.broadcasted_iota(jnp.int32, out_sums_ref.shape, 1)
    first = jnp.sum(act * weight_ref[...], axis=1, keepdims=True)
    second = jnp.sum(act * product, axis=1, keepdims=True)
    sums = jnp.where(lane == 0, first, jnp.where(lane == 1, second, 0.0)) + sum(ref[...] for ref in sums_refs)
    out_sums_ref[...] = sums
    if act_refs[-1].shape[1] > width:
        act_refs[-1][:, width:] = sums


def prepare_kernel(rows, columns, block, depth, weight_ref, gain_ref, *refs):
    *part_refs, sums_ref, landed, arrived, totals = refs
    totals[...] = jnp.zeros_like(totals)
    width = part_refs[0].shape[1]
    steps = rows[1] // block

    def fetch(step):
        start = pl.multiple_of(rows[0] + step * block, block)
        slot = lax.rem(step, depth)
        return pltpu.make_async_copy(
            weight_ref.at[pl.ds(start, block), pl.ds(*columns)], landed.at[slot], arrived.at[slot]
        )

    for step in range(min(depth, steps)):
        fetch(step).start()

    @pl.loop(0, steps)
    def _(step):
        fetch(step).wait()
        tile = landed[lax.rem(step, depth)]
        high, low = split(tile)
        at = pl.ds(pl.multiple_of(step * block, block), block)
        totals[...] += jnp.sum((tile * gain_ref[at, :]).reshape(block // 8, 8, columns[1]), axis=0)
        for n, part_ref in enumerate(part_refs):
            part_ref[at, :] = (low if n % 2 else high)[:, n // 2 * width : (n // 2 + 1) * width]

        @pl.when(step + depth < steps)
        def _():
            fetch(step + depth).start()

    sums_ref[...] = jnp.sum(totals[...], axis=0, keepdims=True)


def prepare(weight, gain, rows, columns, after):
    block = divisor(rows[1], *[b for b in (256, 128, 64, 32) if b <= max(256 * 1536 // columns[1], 32)])
    depth = 4
    outs = (pltpu.VMEM((rows[1], columns[1] // 2), jnp.bfloat16),) * 4
    inside, anywhere = pl.BlockSpec(memory_space=pltpu.VMEM), pl.BlockSpec(memory_space=pl.ANY)
    result = pl.pallas_call(
        lambda weight_ref, gain_ref, *refs: prepare_kernel(
            rows, columns, block, depth, weight_ref, gain_ref, *refs[len(after) :]
        ),
        out_shape=outs + (jax.ShapeDtypeStruct((1, columns[1]), jnp.float32),),
        in_specs=[anywhere, inside] + [anywhere] * len(after),
        out_specs=[inside] * 5,
        scratch_shapes=[
            pltpu.VMEM((depth, block, columns[1]), jnp.float32),
            pltpu.SemaphoreType.DMA((depth,)),
            pltpu.VMEM((8, columns[1]), jnp.float32),
        ],
        compiler_params=pltpu.CompilerParams(vmem_limit_bytes=VMEM_LIMIT),
        cost_estimate=SHORT,
    )(pltpu.with_memory_space_constraint(weight, pltpu.HBM), gain, *after)
    return list(result[:4]), result[4]


def three_pass(both, high, low, contract):
    rows = both.shape[0] // 2
    dot = functools.partial(
        lax.dot_general,
        dimension_numbers=(((1,), (contract,)), ((), ())),
        preferred_element_type=jnp.float32,
    )
    first = dot(both[...], high)
    return first[:rows] + first[rows:] + dot(both[:rows, :], low)


def fill(both, block_refs, place_ref):
    count = block_refs[0].shape[0]
    total = both.shape[0] // 2
    for index, ref in enumerate(block_refs):
        high, low = split(ref[...])
        row = pl.multiple_of(place_ref[index] * count, count)
        both[pl.ds(row, count), :] = high
        both[pl.ds(total + row, count), :] = low


def follow(earlier_refs, out_refs):
    for earlier_ref, out_ref in zip(earlier_refs, out_refs):
        out_ref[:, : earlier_ref.shape[1]] = earlier_ref[...]
    return earlier_refs[0].shape[1] if earlier_refs else 0


def put(out_refs, at, value):
    row = 0
    for out_ref in out_refs:
        out_ref[:, at] = value[row : row + out_ref.shape[0]]
        row += out_ref.shape[0]


def parts_of(tokens, chips, hidden):
    block = tokens // (2 * chips)
    return [jax.ShapeDtypeStruct((n, hidden), jnp.float32) for n in (block, block * (chips - 1))] * 2


def forward_kernel(place_ref, slot_refs, weight_refs, earlier_refs, out_refs, both):
    fill(both, slot_refs, place_ref)
    column = follow(earlier_refs, out_refs)
    for high_ref, low_ref in zip(weight_refs[::2], weight_refs[1::2]):
        width = divisor(high_ref.shape[1], 256, 128)

        @pl.loop(0, high_ref.shape[1] // width, unroll=2)
        def _(step):
            at = pl.ds(pl.multiple_of(step * width, width), width)
            part = three_pass(both, high_ref[:, at], low_ref[:, at], 0)
            put(out_refs, pl.ds(pl.multiple_of(column + step * width, width), width), part)

        column += high_ref.shape[1]


def forward(slots, weights, place, earlier, after):
    tokens, depth = slots[0].shape[0] * len(slots), slots[0].shape[1]
    hidden = sum(w.shape[1] for w in weights[::2]) + (earlier[0].shape[1] if earlier else 0)
    inside, anywhere = pl.BlockSpec(memory_space=pltpu.VMEM), pl.BlockSpec(memory_space=pl.ANY)
    ends = [1 + len(slots), 1 + len(slots) + len(weights), 1 + len(slots) + len(weights) + len(earlier)]
    return pl.pallas_call(
        lambda *refs: forward_kernel(
            refs[0], refs[1 : ends[0]], refs[ends[0] : ends[1]], refs[ends[1] : ends[2]], refs[-5:-1], refs[-1]
        ),
        out_shape=parts_of(tokens, len(slots) // 2, hidden),
        in_specs=[pl.BlockSpec(memory_space=pltpu.SMEM)] + [inside] * (ends[2] - 1) + [anywhere] * len(after),
        out_specs=[inside] * 4,
        scratch_shapes=[pltpu.VMEM((2 * tokens, depth), jnp.bfloat16)],
        compiler_params=pltpu.CompilerParams(vmem_limit_bytes=VMEM_LIMIT),
        cost_estimate=SHORT,
    )(place, *slots, *[pltpu.with_memory_space_constraint(w, pltpu.VMEM) for w in weights], *earlier, *after)


def stream_kernel(first, depth, place_ref, slot_refs, weight_ref, out_refs, both, landed, arrived):
    width = landed.shape[1]
    steps = out_refs[0].shape[1] // width

    def fetch(step):
        start = pl.multiple_of(first + step * width, width)
        slot = lax.rem(step, depth)
        return pltpu.make_async_copy(weight_ref.at[pl.ds(start, width), :], landed.at[slot], arrived.at[slot])

    for step in range(min(depth, steps)):
        fetch(step).start()
    fill(both, slot_refs, place_ref)

    @pl.loop(0, steps)
    def _(step):
        fetch(step).wait()
        high, low = split(landed[lax.rem(step, depth)])
        put(out_refs, pl.ds(pl.multiple_of(step * width, width), width), three_pass(both, high, low, 1))

        @pl.when(step + depth < steps)
        def _():
            fetch(step + depth).start()


def stream(slots, weight, place, first, hidden, after):
    tokens, columns = slots[0].shape[0] * len(slots), slots[0].shape[1]
    width, depth = divisor(hidden, 256, 128), 4
    inside, anywhere = pl.BlockSpec(memory_space=pltpu.VMEM), pl.BlockSpec(memory_space=pl.ANY)
    last = 1 + len(slots)
    return pl.pallas_call(
        lambda *refs: stream_kernel(first, depth, refs[0], refs[1:last], refs[last], refs[-7:-3], *refs[-3:]),
        out_shape=parts_of(tokens, len(slots) // 2, hidden),
        in_specs=[pl.BlockSpec(memory_space=pltpu.SMEM)] + [inside] * len(slots) + [anywhere] * (1 + len(after)),
        out_specs=[inside] * 4,
        scratch_shapes=[
            pltpu.VMEM((2 * tokens, columns), jnp.bfloat16),
            pltpu.VMEM((depth, width, columns), jnp.float32),
            pltpu.SemaphoreType.DMA((depth,)),
        ],
        compiler_params=pltpu.CompilerParams(vmem_limit_bytes=8 * 1024 * 1024),
        cost_estimate=SHORT,
    )(place, *slots, pltpu.with_memory_space_constraint(weight, pltpu.HBM), *after)


def backward_kernel(first, depth, place_ref, act_refs, weight_refs, earlier_refs, out_refs, both, result, riders):
    block = act_refs[0].shape[0]
    total = block * len(act_refs)
    hidden = both.shape[1]
    for p, act_ref in enumerate(act_refs):
        if act_ref.shape[1] > hidden:
            riders[p * block : (p + 1) * block, :] = act_ref[:, hidden:]
        high, low = split(act_ref[:, :hidden])
        both[p * block : (p + 1) * block, :] = high
        both[total + p * block : total + (p + 1) * block, :] = low
    width = result.shape[1]

    if out_refs[0].shape[1] > depth:
        for b, out_ref in enumerate(out_refs):
            out_ref[:, depth:] = riders[pl.ds(pl.multiple_of(place_ref[b] * block, block), block), :]

    @pl.loop(0, depth // width)
    def _(step):
        at = pl.ds(pl.multiple_of(first + step * width, width), width)
        value, column = 0.0, 0
        for high_ref, low_ref in zip(weight_refs[::2], weight_refs[1::2]):
            columns = slice(column, column + high_ref.shape[1])
            value += three_pass(both[:, columns], high_ref[at, :], low_ref[at, :], 1)
            column = columns.stop
        result[...] = value
        for b, out_ref in enumerate(out_refs):
            rows = result[pl.ds(pl.multiple_of(place_ref[b] * block, block), block), :]
            if earlier_refs:
                rows = rows + earlier_refs[b][:, at]
            out_ref[:, pl.ds(pl.multiple_of(step * width, width), width)] = rows


def backward(acts, weights, place, earlier, part, parts, after):
    slots, outs = len(acts), place.shape[0]
    block, hidden = acts[0].shape[0], sum(w.shape[1] for w in weights[::2])
    riding = acts[0].shape[1] - hidden if part == 0 else 0
    depth = weights[0].shape[0] // parts
    width = divisor(depth, 256, 128)
    out = jax.ShapeDtypeStruct((block, depth + riding), jnp.float32)
    inside, anywhere = pl.BlockSpec(memory_space=pltpu.VMEM), pl.BlockSpec(memory_space=pl.ANY)
    ends = [1 + slots, 1 + slots + len(weights), 1 + slots + len(weights) + len(earlier)]
    return pl.pallas_call(
        lambda *refs: backward_kernel(
            part * depth,
            depth,
            refs[0],
            refs[1 : ends[0]],
            refs[ends[0] : ends[1]],
            refs[ends[1] : ends[2]],
            refs[-3 - outs : -3],
            *refs[-3:],
        ),
        out_shape=[out] * outs,
        in_specs=[pl.BlockSpec(memory_space=pltpu.SMEM)] + [inside] * (ends[2] - 1) + [anywhere] * len(after),
        out_specs=[inside] * outs,
        scratch_shapes=[
            pltpu.VMEM((2 * block * slots, hidden), jnp.bfloat16),
            pltpu.VMEM((block * slots, width), jnp.float32),
            pltpu.VMEM((block * slots, 128), jnp.float32),
        ],
        compiler_params=pltpu.CompilerParams(vmem_limit_bytes=VMEM_LIMIT),
        cost_estimate=SHORT,
    )(place, *acts, *[pltpu.with_memory_space_constraint(w, pltpu.VMEM) for w in weights], *earlier, *after)


def body(hid_size, emb_size, inputs, out_grad, in_weight, in_bias, out_weight, norm_gain):
    chips = emb_size // 2
    tokens, depth = inputs.shape
    model_width = depth * emb_size
    hidden = in_weight.shape[1]
    me = lax.axis_index("emb")
    chip, core = me // 2, me % 2

    def along_hid(values, steps=1):
        return lax.ppermute(values, "hid", [(i, (i + steps) % hid_size) for i in range(hid_size)])

    def other_core(values):
        return lax.ppermute(values, "emb", [(i, i ^ 1) for i in range(emb_size)])

    def next_chip(values):
        return lax.ppermute(values, "emb", [(i, (i + 2) % emb_size) for i in range(emb_size)])

    owner = jnp.arange(emb_size, dtype=jnp.int32)
    if hid_size == 4:
        owner = jnp.append(owner, jnp.where(lax.axis_index("hid") == 0, 1, 3).astype(jnp.int32))
    place = ((owner % 2) ^ core) * chips + (owner // 2 - chip) % chips

    def gathered(values):
        return [values] + [along_hid(values, step) for step in range(1, hid_size)]

    def relayed(values):
        blocks = [values] + [None] * (hid_size - 1)
        for step in range(1, hid_size // 2 + 1):
            blocks[step] = along_hid(blocks[step - 1], 1)
        for step in range(1, hid_size - hid_size // 2):
            blocks[-step] = along_hid(blocks[(1 - step) % hid_size], -1)
        return blocks

    grads = gathered(out_grad)
    third = hidden // 3

    def tied(values, others):
        return lax.optimization_barrier((values, others))

    def halved(partial, behind=()):
        keep_own, keep, send_own, send = partial
        return keep + tied(other_core(send), behind)[0], (keep_own, other_core(send_own))

    def exchanged(half):
        summed, own = half
        terms = jnp.split(summed, chips - 1)
        arrival = next_chip(terms[chips - 2])
        for step in range(chips - 3, -1, -1):
            arrival = next_chip(arrival + terms[step])
        return arrival, *own

    def prepared(c, after):
        return prepare(in_weight, norm_gain[:, None], (0, depth), (c * third, third), after)

    moments = call(moments_kernel, jax.ShapeDtypeStruct((2 * tokens, 128), jnp.float32), (inputs,), ())
    in_parts, sums_0 = prepared(0, [place, moments])
    parts, sums_1 = prepared(1, [in_parts[0]])
    in_parts += parts
    moments = call(
        functools.partial(merge_kernel, depth), moments, (moments, other_core(moments)), (in_parts[4], *grads[1:])
    )
    parts = [moments]
    for _ in range(1, chips):
        parts.append(next_chip(parts[-1]))
    normed, scaled, inv_std = call(
        functools.partial(normalise_kernel, 2 * depth),
        (inputs, inputs, jax.ShapeDtypeStruct((tokens, 128), jnp.float32)),
        (inputs, norm_gain[None, :], *parts),
        (),
    )
    inv_std = inv_std[:, :1]
    scaled = relayed(scaled)
    back_0 = stream(grads, out_weight, place, 0, 2 * third, [scaled[0]])
    back_0, (scaled[1], scaled[-1]) = tied(back_0, (scaled[1], scaled[-1]))
    half_0 = halved(back_0)
    back_1 = stream(grads, out_weight, place, 2 * third, third, [half_0[0]])
    back_0 = exchanged(half_0)
    back_1, scaled = tied(back_1, scaled)
    pre_0 = forward(scaled, in_parts[:8], place, (), [back_1[0]])
    half_1 = halved(back_1, (pre_0, back_0[0]))
    back_1 = exchanged(half_1)
    half_0 = halved(pre_0)
    parts, sums_2 = prepared(2, [half_0[0], half_1[0]])
    in_parts += parts
    pre_1 = forward(scaled, in_parts[8:], place, (), [half_0[0], back_1[0]])
    pre_0 = exchanged(half_0)

    gain_sums, _ = tied(jnp.concatenate([sums_0, sums_1, sums_2], axis=1), pre_1)
    gain_sums = passing = gain_sums + other_core(gain_sums)
    for _ in range(1, chips):
        passing = next_chip(passing)
        gain_sums = gain_sums + passing

    def slope_product(span, back, pre, sums, after):
        pieces, room = (span.stop - span.start) // third, 128 * len(sums)
        widths = [third] * (pieces - 1) + [third + room, 128]
        return call(
            functools.partial(slope_kernel, len(back), len(sums)),
            tuple(jax.ShapeDtypeStruct((tokens, n), jnp.float32) for n in widths),
            (*back, *pre, in_bias[None, span], gain_sums[:, span], *sums),
            after,
        )

    def spread_out(act):
        mine = [None] * chips
        mine[0] = act
        for step in range(1, chips):
            act = next_chip(act)
            mine[(chips - step) % chips] = act
        return mine

    def both_cores(mine):
        return mine + [other_core(block) for block in mine]

    def handed_on(sums, behind):
        if hid_size != 4:
            return sums
        farthest = tied(lax.ppermute(sums[4], "hid", [(0, 1), (3, 2)]), behind)[0]
        return [sums[0], sums[1], sums[2] + farthest, sums[3]]

    def summed_along_hid(sums, behind=()):
        if hid_size == 4:
            arrivals = [
                lax.ppermute(sums[1], "hid", [(1, 0), (2, 1), (3, 2)]),
                lax.ppermute(sums[3], "hid", [(0, 1), (1, 2), (2, 3)]),
                along_hid(sums[2], 2),
            ]
        else:
            arrivals = [along_hid(sums[step], -step) for step in range(1, hid_size)]
        return sum(tied(arrivals, behind)[0], start=sums[0])

    half_1 = halved(pre_1, pre_0[0])
    pre_0 = tied(pre_0, half_1[0])[0]
    act_0, act_1, sums_0 = slope_product(slice(0, 2 * third), back_0, pre_0, (), ())
    pre_1 = exchanged(half_1)
    sums = backward(both_cores(spread_out(act_0)), in_parts[:4], place, (), 0, 1, [])
    act_2, _ = slope_product(slice(2 * third, hidden), back_1, pre_1, (sums_0,), (sums[0],))
    acts_0, acts_1 = spread_out(act_1), spread_out(act_2)
    sums = backward(both_cores(acts_0), in_parts[4:8], place, sums, 0, 1, [act_2])
    acts_1[1:], sums = tied(acts_1[1:], sums)
    acts_1 = both_cores(acts_1)
    parts = 2 if depth % 512 == 0 else 1
    ends = []
    for part in range(parts):
        ends.append(backward(acts_1, in_parts[8:], place, sums, part, parts, [ends[-1][0]] if ends else []))
    for part in range(parts):
        ends[part] = handed_on(tied(ends[part], ends[part - 1][2])[0] if part else ends[part], ends[part + 1 :])
    first = summed_along_hid(ends[0])
    others = [summed_along_hid(end, first) for end in ends[1:]]
    width = depth // parts
    normed_grad = jnp.concatenate([first[:, :width], *others], axis=1) * norm_gain
    mean, slope = first[:, width : width + 1] / model_width, first[:, width + 1 : width + 2] / model_width
    return inv_std * (normed_grad - mean - normed * slope)


def solution(mesh):
    hid_size, emb_size = mesh.shape["hid"], mesh.shape["emb"]
    assert hid_size == emb_size and emb_size % 2 == 0
    return jax.shard_map(
        functools.partial(body, hid_size, emb_size),
        mesh=mesh,
        in_specs=(
            P(("groups", "hid"), "emb"),
            P(("groups", "hid"), "emb"),
            P("emb", "hid"),
            P("hid"),
            P("hid", "emb"),
            P("emb"),
        ),
        out_specs=P(("groups", "hid"), "emb"),
        check_vma=False,
    )
```

```python
import functools
import math

import jax
import jax.numpy as jnp
from jax import lax
from jax.experimental import pallas as pl
from jax.experimental.pallas import tpu as pltpu
from jax.sharding import PartitionSpec as P

VMEM_LIMIT = 5 * 1024 * 1024
SHORT = pl.CostEstimate(flops=1 << 20, bytes_accessed=1 << 18, transcendentals=0)


def gelu_slope(values):
    cdf = 0.5 * (1.0 + lax.erf(values * (1.0 / math.sqrt(2.0))))
    density = jnp.exp(-0.5 * values * values) * (1.0 / math.sqrt(2.0 * math.pi))
    return cdf + values * density


def split(values):
    high = values.astype(jnp.bfloat16)
    return high, (values - high.astype(jnp.float32)).astype(jnp.bfloat16)


def divisor(extent, *choices):
    return next(c for c in choices if extent % c == 0)


def call(kernel, out_shape, operands, after):
    outs = out_shape if isinstance(out_shape, tuple) else (out_shape,)

    def run(*refs):
        kernel(*refs[: len(operands)], *refs[len(operands) + len(after) :])

    inside = pl.BlockSpec(memory_space=pltpu.VMEM)
    result = pl.pallas_call(
        run,
        out_shape=tuple(jax.ShapeDtypeStruct(o.shape, o.dtype) for o in outs),
        in_specs=[inside] * len(operands) + [pl.BlockSpec(memory_space=pl.ANY)] * len(after),
        out_specs=[inside] * len(outs),
        compiler_params=pltpu.CompilerParams(vmem_limit_bytes=VMEM_LIMIT),
        cost_estimate=SHORT,
    )(*operands, *after)
    return result if isinstance(out_shape, tuple) else result[0]


def moments_kernel(inputs_ref, out_ref):
    rows, depth = inputs_ref.shape
    mean = jnp.sum(inputs_ref[...], axis=1, keepdims=True) * (1.0 / depth)
    square = jnp.sum(jnp.square(inputs_ref[...] - mean), axis=1, keepdims=True)
    out_ref[:rows] = jnp.broadcast_to(mean, (rows, 128))
    out_ref[rows:] = jnp.broadcast_to(square, (rows, 128))


def merge(moments, count):
    rows = moments[0].shape[0] // 2
    mean = sum(part[:rows] for part in moments) * (1.0 / len(moments))
    square = sum(part[rows:] + count * jnp.square(part[:rows] - mean) for part in moments)
    return mean, square


def merge_kernel(count, first_ref, second_ref, out_ref):
    rows = out_ref.shape[0] // 2
    out_ref[:rows], out_ref[rows:] = merge((first_ref[...], second_ref[...]), count)


def normalise_kernel(count, inputs_ref, gain_ref, *refs):
    *moment_refs, normed_ref, scaled_ref, inv_std_ref = refs
    mean, square = merge([ref[...] for ref in moment_refs], count)
    inv_std = 1.0 / jnp.sqrt(square * (1.0 / (count * len(moment_refs))) + 1e-06)
    normed = (inputs_ref[...] - mean[:, :1]) * inv_std[:, :1]
    normed_ref[...] = normed
    scaled_ref[...] = normed * gain_ref[...]
    inv_std_ref[...] = inv_std


def slope_kernel(terms, outs, *refs):
    back_refs, pre_refs, bias_ref = refs[:terms], refs[terms : 2 * terms], refs[2 * terms]
    others, act_refs, sums_ref = refs[2 * terms + 1 : -1 - outs], refs[-1 - outs : -1], refs[-1]
    hidden = bias_ref.shape[1]
    width = hidden // outs
    product = sum(ref[...] for ref in pre_refs)
    act = sum(ref[...] for ref in back_refs) * gelu_slope(product + bias_ref[...])
    for n, act_ref in enumerate(act_refs):
        act_ref[:, :width] = act[:, n * width : (n + 1) * width]
    lane = lax.broadcasted_iota(jnp.int32, sums_ref.shape, 1)
    sums = jnp.where(lane == 1, jnp.sum(act * product, axis=1, keepdims=True), 0.0)
    if others:
        weight_ref, earlier_sums_ref, *earlier_refs = others
        first, column = 0.0, 0
        for piece in (*[ref[...] for ref in earlier_refs], act):
            end = column + piece.shape[1]
            first = first + jnp.sum(piece * weight_ref[:, column:end], axis=1, keepdims=True)
            column = end
        sums = sums + earlier_sums_ref[...] + jnp.where(lane == 0, first, 0.0)
        act_refs[-1][:, width:] = sums
    sums_ref[...] = sums


def prepare_kernel(rows, columns, block, depth, weight_ref, gain_ref, *refs):
    *part_refs, sums_ref, landed, arrived, totals = refs
    totals[...] = jnp.zeros_like(totals)
    width = part_refs[0].shape[1]
    steps = rows[1] // block

    def fetch(step):
        start = pl.multiple_of(rows[0] + step * block, block)
        slot = lax.rem(step, depth)
        return pltpu.make_async_copy(
            weight_ref.at[pl.ds(start, block), pl.ds(*columns)], landed.at[slot], arrived.at[slot]
        )

    for step in range(min(depth, steps)):
        fetch(step).start()

    @pl.loop(0, steps)
    def _(step):
        fetch(step).wait()
        tile = landed[lax.rem(step, depth)]
        high, low = split(tile)
        at = pl.ds(pl.multiple_of(step * block, block), block)
        totals[...] += jnp.sum((tile * gain_ref[at, :]).reshape(block // 8, 8, columns[1]), axis=0)
        for n, part_ref in enumerate(part_refs):
            part_ref[at, :] = (low if n % 2 else high)[:, n // 2 * width : (n // 2 + 1) * width]

        @pl.when(step + depth < steps)
        def _():
            fetch(step + depth).start()

    sums_ref[...] = jnp.sum(totals[...], axis=0, keepdims=True)


def prepare(weight, gain, rows, columns, after):
    block = divisor(rows[1], *[b for b in (256, 128, 64, 32) if b <= max(256 * 1536 // columns[1], 32)])
    depth = 4
    outs = (pltpu.VMEM((rows[1], columns[1] // 2), jnp.bfloat16),) * 4
    inside, anywhere = pl.BlockSpec(memory_space=pltpu.VMEM), pl.BlockSpec(memory_space=pl.ANY)
    result = pl.pallas_call(
        lambda weight_ref, gain_ref, *refs: prepare_kernel(
            rows, columns, block, depth, weight_ref, gain_ref, *refs[len(after) :]
        ),
        out_shape=outs + (jax.ShapeDtypeStruct((1, columns[1]), jnp.float32),),
        in_specs=[anywhere, inside] + [anywhere] * len(after),
        out_specs=[inside] * 5,
        scratch_shapes=[
            pltpu.VMEM((depth, block, columns[1]), jnp.float32),
            pltpu.SemaphoreType.DMA((depth,)),
            pltpu.VMEM((8, columns[1]), jnp.float32),
        ],
        compiler_params=pltpu.CompilerParams(vmem_limit_bytes=VMEM_LIMIT),
        cost_estimate=SHORT,
    )(pltpu.with_memory_space_constraint(weight, pltpu.HBM), gain, *after)
    return list(result[:4]), result[4]


def three_pass(both, high, low, contract):
    rows = both.shape[0] // 2
    dot = functools.partial(
        lax.dot_general,
        dimension_numbers=(((1,), (contract,)), ((), ())),
        preferred_element_type=jnp.float32,
    )
    first = dot(both[...], high)
    return first[:rows] + first[rows:] + dot(both[:rows, :], low)


def fill(both, block_refs, place_ref):
    count = block_refs[0].shape[0]
    total = both.shape[0] // 2
    for index, ref in enumerate(block_refs):
        high, low = split(ref[...])
        row = pl.multiple_of(place_ref[index] * count, count)
        both[pl.ds(row, count), :] = high
        both[pl.ds(total + row, count), :] = low


def follow(earlier_refs, out_refs):
    for earlier_ref, out_ref in zip(earlier_refs, out_refs):
        out_ref[:, : earlier_ref.shape[1]] = earlier_ref[...]
    return earlier_refs[0].shape[1] if earlier_refs else 0


def put(out_refs, at, value):
    row = 0
    for out_ref in out_refs:
        out_ref[:, at] = value[row : row + out_ref.shape[0]]
        row += out_ref.shape[0]


def parts_of(tokens, chips, hidden):
    block = tokens // (2 * chips)
    return [jax.ShapeDtypeStruct((n, hidden), jnp.float32) for n in (block, block * (chips - 1))] * 2


def forward_kernel(place_ref, slot_refs, weight_refs, earlier_refs, out_refs, both):
    fill(both, slot_refs, place_ref)
    column = follow(earlier_refs, out_refs)
    for high_ref, low_ref in zip(weight_refs[::2], weight_refs[1::2]):
        width = divisor(high_ref.shape[1], 256, 128)

        @pl.loop(0, high_ref.shape[1] // width, unroll=2)
        def _(step):
            at = pl.ds(pl.multiple_of(step * width, width), width)
            part = three_pass(both, high_ref[:, at], low_ref[:, at], 0)
            put(out_refs, pl.ds(pl.multiple_of(column + step * width, width), width), part)

        column += high_ref.shape[1]


def forward(slots, weights, place, earlier, after):
    tokens, depth = slots[0].shape[0] * len(slots), slots[0].shape[1]
    hidden = sum(w.shape[1] for w in weights[::2]) + (earlier[0].shape[1] if earlier else 0)
    inside, anywhere = pl.BlockSpec(memory_space=pltpu.VMEM), pl.BlockSpec(memory_space=pl.ANY)
    ends = [1 + len(slots), 1 + len(slots) + len(weights), 1 + len(slots) + len(weights) + len(earlier)]
    return pl.pallas_call(
        lambda *refs: forward_kernel(
            refs[0], refs[1 : ends[0]], refs[ends[0] : ends[1]], refs[ends[1] : ends[2]], refs[-5:-1], refs[-1]
        ),
        out_shape=parts_of(tokens, len(slots) // 2, hidden),
        in_specs=[pl.BlockSpec(memory_space=pltpu.SMEM)] + [inside] * (ends[2] - 1) + [anywhere] * len(after),
        out_specs=[inside] * 4,
        scratch_shapes=[pltpu.VMEM((2 * tokens, depth), jnp.bfloat16)],
        compiler_params=pltpu.CompilerParams(vmem_limit_bytes=VMEM_LIMIT),
        cost_estimate=SHORT,
    )(place, *slots, *[pltpu.with_memory_space_constraint(w, pltpu.VMEM) for w in weights], *earlier, *after)


def stream_kernel(first, depth, place_ref, slot_refs, weight_ref, out_refs, both, landed, arrived):
    width = landed.shape[1]
    steps = out_refs[0].shape[1] // width

    def fetch(step):
        start = pl.multiple_of(first + step * width, width)
        slot = lax.rem(step, depth)
        return pltpu.make_async_copy(weight_ref.at[pl.ds(start, width), :], landed.at[slot], arrived.at[slot])

    for step in range(min(depth, steps)):
        fetch(step).start()
    fill(both, slot_refs, place_ref)

    @pl.loop(0, steps)
    def _(step):
        fetch(step).wait()
        high, low = split(landed[lax.rem(step, depth)])
        put(out_refs, pl.ds(pl.multiple_of(step * width, width), width), three_pass(both, high, low, 1))

        @pl.when(step + depth < steps)
        def _():
            fetch(step + depth).start()


def stream(slots, weight, place, first, hidden, after):
    tokens, columns = slots[0].shape[0] * len(slots), slots[0].shape[1]
    width, depth = divisor(hidden, 256, 128), 4
    inside, anywhere = pl.BlockSpec(memory_space=pltpu.VMEM), pl.BlockSpec(memory_space=pl.ANY)
    last = 1 + len(slots)
    return pl.pallas_call(
        lambda *refs: stream_kernel(first, depth, refs[0], refs[1:last], refs[last], refs[-7:-3], *refs[-3:]),
        out_shape=parts_of(tokens, len(slots) // 2, hidden),
        in_specs=[pl.BlockSpec(memory_space=pltpu.SMEM)] + [inside] * len(slots) + [anywhere] * (1 + len(after)),
        out_specs=[inside] * 4,
        scratch_shapes=[
            pltpu.VMEM((2 * tokens, columns), jnp.bfloat16),
            pltpu.VMEM((depth, width, columns), jnp.float32),
            pltpu.SemaphoreType.DMA((depth,)),
        ],
        compiler_params=pltpu.CompilerParams(vmem_limit_bytes=8 * 1024 * 1024),
        cost_estimate=SHORT,
    )(place, *slots, pltpu.with_memory_space_constraint(weight, pltpu.HBM), *after)


def backward_kernel(first, depth, place_ref, act_refs, weight_refs, earlier_refs, out_refs, both, result, riders):
    block = act_refs[0].shape[0]
    total = block * len(act_refs)
    hidden = both.shape[1]
    for p, act_ref in enumerate(act_refs):
        if act_ref.shape[1] > hidden:
            riders[p * block : (p + 1) * block, :] = act_ref[:, hidden:]
        high, low = split(act_ref[:, :hidden])
        both[p * block : (p + 1) * block, :] = high
        both[total + p * block : total + (p + 1) * block, :] = low
    width = result.shape[1]

    if out_refs[0].shape[1] > depth:
        for b, out_ref in enumerate(out_refs):
            out_ref[:, depth:] = riders[pl.ds(pl.multiple_of(place_ref[b] * block, block), block), :]

    @pl.loop(0, depth // width)
    def _(step):
        at = pl.ds(pl.multiple_of(first + step * width, width), width)
        value, column = 0.0, 0
        for high_ref, low_ref in zip(weight_refs[::2], weight_refs[1::2]):
            columns = slice(column, column + high_ref.shape[1])
            value += three_pass(both[:, columns], high_ref[at, :], low_ref[at, :], 1)
            column = columns.stop
        result[...] = value
        for b, out_ref in enumerate(out_refs):
            rows = result[pl.ds(pl.multiple_of(place_ref[b] * block, block), block), :]
            if earlier_refs:
                rows = rows + earlier_refs[b][:, at]
            out_ref[:, pl.ds(pl.multiple_of(step * width, width), width)] = rows


def backward(acts, weights, place, earlier, part, parts, after):
    slots, block, hidden = len(acts), acts[0].shape[0], sum(w.shape[1] for w in weights[::2])
    riding = acts[0].shape[1] - hidden if part == 0 else 0
    depth = weights[0].shape[0] // parts
    width = divisor(depth, 256, 128)
    out = jax.ShapeDtypeStruct((block, depth + riding), jnp.float32)
    inside, anywhere = pl.BlockSpec(memory_space=pltpu.VMEM), pl.BlockSpec(memory_space=pl.ANY)
    ends = [1 + slots, 1 + slots + len(weights), 1 + slots + len(weights) + len(earlier)]
    return pl.pallas_call(
        lambda *refs: backward_kernel(
            part * depth,
            depth,
            refs[0],
            refs[1 : ends[0]],
            refs[ends[0] : ends[1]],
            refs[ends[1] : ends[2]],
            refs[-3 - slots : -3],
            *refs[-3:],
        ),
        out_shape=[out] * slots,
        in_specs=[pl.BlockSpec(memory_space=pltpu.SMEM)] + [inside] * (ends[2] - 1) + [anywhere] * len(after),
        out_specs=[inside] * slots,
        scratch_shapes=[
            pltpu.VMEM((2 * block * slots, hidden), jnp.bfloat16),
            pltpu.VMEM((block * slots, width), jnp.float32),
            pltpu.VMEM((block * slots, 128), jnp.float32),
        ],
        compiler_params=pltpu.CompilerParams(vmem_limit_bytes=VMEM_LIMIT),
        cost_estimate=SHORT,
    )(place, *acts, *[pltpu.with_memory_space_constraint(w, pltpu.VMEM) for w in weights], *earlier, *after)


def body(hid_size, emb_size, inputs, out_grad, in_weight, in_bias, out_weight, norm_gain):
    chips = emb_size // 2
    tokens, depth = inputs.shape
    model_width = depth * emb_size
    hidden = in_weight.shape[1]
    me = lax.axis_index("emb")
    chip, core = me // 2, me % 2

    def along_hid(values, steps=1):
        return lax.ppermute(values, "hid", [(i, (i + steps) % hid_size) for i in range(hid_size)])

    def other_core(values):
        return lax.ppermute(values, "emb", [(i, i ^ 1) for i in range(emb_size)])

    def next_chip(values):
        return lax.ppermute(values, "emb", [(i, (i + 2) % emb_size) for i in range(emb_size)])

    owner = jnp.arange(emb_size, dtype=jnp.int32)
    place = ((owner % 2) ^ core) * chips + (owner // 2 - chip) % chips

    def gathered(values):
        return [values] + [along_hid(values, step) for step in range(1, hid_size)]

    def relayed(values):
        blocks = [values] + [None] * (hid_size - 1)
        for step in range(1, hid_size // 2 + 1):
            blocks[step] = along_hid(blocks[step - 1], 1)
        for step in range(1, hid_size - hid_size // 2):
            blocks[-step] = along_hid(blocks[(1 - step) % hid_size], -1)
        return blocks

    grads = gathered(out_grad)
    third = hidden // 3

    def tied(values, others):
        return lax.optimization_barrier((values, others))

    def halved(partial, behind=()):
        keep_own, keep, send_own, send = partial
        return keep + tied(other_core(send), behind)[0], (keep_own, other_core(send_own))

    def exchanged(half):
        summed, own = half
        terms = jnp.split(summed, chips - 1)
        arrival = next_chip(terms[chips - 2])
        for step in range(chips - 3, -1, -1):
            arrival = next_chip(arrival + terms[step])
        return arrival, *own

    def prepared(c, after):
        return prepare(in_weight, norm_gain[:, None], (0, depth), (c * third, third), after)

    moments = call(moments_kernel, jax.ShapeDtypeStruct((2 * tokens, 128), jnp.float32), (inputs,), ())
    in_parts, sums_0 = prepared(0, [place, moments])
    parts, sums_1 = prepared(1, [in_parts[0]])
    in_parts += parts
    moments = call(
        functools.partial(merge_kernel, depth), moments, (moments, other_core(moments)), (in_parts[4], *grads[1:])
    )
    parts = [moments]
    for _ in range(1, chips):
        parts.append(next_chip(parts[-1]))
    normed, scaled, inv_std = call(
        functools.partial(normalise_kernel, 2 * depth),
        (inputs, inputs, jax.ShapeDtypeStruct((tokens, 128), jnp.float32)),
        (inputs, norm_gain[None, :], *parts),
        (),
    )
    inv_std = inv_std[:, :1]
    scaled = relayed(scaled)
    back_0 = stream(grads, out_weight, place, 0, 2 * third, [scaled[0]])
    back_0, (scaled[1], scaled[-1]) = tied(back_0, (scaled[1], scaled[-1]))
    half_0 = halved(back_0)
    back_1 = stream(grads, out_weight, place, 2 * third, third, [half_0[0]])
    back_0 = exchanged(half_0)
    back_1, scaled = tied(back_1, scaled)
    pre_0 = forward(scaled, in_parts[:8], place, (), [back_1[0]])
    half_1 = halved(back_1, (pre_0, back_0[0]))
    back_1 = exchanged(half_1)
    half_0 = halved(pre_0)
    parts, sums_2 = prepared(2, [half_0[0], half_1[0]])
    in_parts += parts
    pre_1 = forward(scaled, in_parts[8:], place, (), [half_0[0], back_1[0]])
    pre_0 = exchanged(half_0)

    gain_sums, _ = tied(jnp.concatenate([sums_0, sums_1, sums_2], axis=1), pre_1)
    gain_sums = passing = gain_sums + other_core(gain_sums)
    for _ in range(1, chips):
        passing = next_chip(passing)
        gain_sums = gain_sums + passing

    def slope_product(span, back, pre, others, after):
        pieces = (span.stop - span.start) // third
        widths = [third] * (pieces - 1) + [third + 128 * bool(others), 128]
        return call(
            functools.partial(slope_kernel, len(back), pieces),
            tuple(jax.ShapeDtypeStruct((tokens, n), jnp.float32) for n in widths),
            (*back, *pre, in_bias[None, span], *others),
            after,
        )

    def spread_out(act):
        mine = [None] * chips
        mine[0] = act
        for step in range(1, chips):
            act = next_chip(act)
            mine[(chips - step) % chips] = act
        return mine

    def both_cores(mine):
        return mine + [other_core(block) for block in mine]

    def summed_along_hid(sums, behind=()):
        arrivals = [along_hid(sums[step], -step) for step in range(1, hid_size)]
        return sum(tied(arrivals, behind)[0], start=sums[0])

    half_1 = halved(pre_1, pre_0[0])
    pre_0 = tied(pre_0, half_1[0])[0]
    act_0, act_1, sums_0 = slope_product(slice(0, 2 * third), back_0, pre_0, (), ())
    pre_1 = exchanged(half_1)
    sums = backward(both_cores(spread_out(act_0)), in_parts[:4], place, (), 0, 1, [])
    act_2, _ = slope_product(
        slice(2 * third, hidden), back_1, pre_1, (gain_sums, sums_0, act_0, act_1), (sums[0],)
    )
    acts_0, acts_1 = spread_out(act_1), spread_out(act_2)
    sums = backward(both_cores(acts_0), in_parts[4:8], place, sums, 0, 1, [act_2])
    acts_1[1:], sums = tied(acts_1[1:], sums)
    acts_1 = both_cores(acts_1)
    parts = 2 if depth % 512 == 0 else 1
    ends = []
    for part in range(parts):
        ends.append(backward(acts_1, in_parts[8:], place, sums, part, parts, [ends[-1][0]] if ends else []))
    first = summed_along_hid(ends[0])
    others = [summed_along_hid(end, first) for end in ends[1:]]
    width = depth // parts
    normed_grad = jnp.concatenate([first[:, :width], *others], axis=1) * norm_gain
    mean, slope = first[:, width : width + 1] / model_width, first[:, width + 1 : width + 2] / model_width
    return inv_std * (normed_grad - mean - normed * slope)


def solution(mesh):
    hid_size, emb_size = mesh.shape["hid"], mesh.shape["emb"]
    assert hid_size == emb_size and emb_size % 2 == 0
    return jax.shard_map(
        functools.partial(body, hid_size, emb_size),
        mesh=mesh,
        in_specs=(
            P(("groups", "hid"), "emb"),
            P(("groups", "hid"), "emb"),
            P("emb", "hid"),
            P("hid"),
            P("hid", "emb"),
            P("emb"),
        ),
        out_specs=P(("groups", "hid"), "emb"),
        check_vma=False,
    )
```

```python
import functools
import math

import jax
import jax.numpy as jnp
from jax import lax
from jax.experimental import pallas as pl
from jax.experimental.pallas import tpu as pltpu
from jax.sharding import PartitionSpec as P

VMEM_LIMIT = 5 * 1024 * 1024
SHORT = pl.CostEstimate(flops=1 << 20, bytes_accessed=1 << 18, transcendentals=0)


def gelu_slope(values):
    cdf = 0.5 * (1.0 + lax.erf(values * (1.0 / math.sqrt(2.0))))
    density = jnp.exp(-0.5 * values * values) * (1.0 / math.sqrt(2.0 * math.pi))
    return cdf + values * density


def split(values):
    high = values.astype(jnp.bfloat16)
    return high, (values - high.astype(jnp.float32)).astype(jnp.bfloat16)


def divisor(extent, *choices):
    return next(c for c in choices if extent % c == 0)


def call(kernel, out_shape, operands, after):
    outs = out_shape if isinstance(out_shape, tuple) else (out_shape,)

    def run(*refs):
        kernel(*refs[: len(operands)], *refs[len(operands) + len(after) :])

    inside = pl.BlockSpec(memory_space=pltpu.VMEM)
    result = pl.pallas_call(
        run,
        out_shape=tuple(jax.ShapeDtypeStruct(o.shape, o.dtype) for o in outs),
        in_specs=[inside] * len(operands) + [pl.BlockSpec(memory_space=pl.ANY)] * len(after),
        out_specs=[inside] * len(outs),
        compiler_params=pltpu.CompilerParams(vmem_limit_bytes=VMEM_LIMIT),
        cost_estimate=SHORT,
    )(*operands, *after)
    return result if isinstance(out_shape, tuple) else result[0]


def moments_kernel(inputs_ref, out_ref):
    rows, depth = inputs_ref.shape
    mean = jnp.sum(inputs_ref[...], axis=1, keepdims=True) * (1.0 / depth)
    square = jnp.sum(jnp.square(inputs_ref[...] - mean), axis=1, keepdims=True)
    out_ref[:rows] = jnp.broadcast_to(mean, (rows, 128))
    out_ref[rows:] = jnp.broadcast_to(square, (rows, 128))


def merge(moments, count):
    rows = moments[0].shape[0] // 2
    mean = sum(part[:rows] for part in moments) * (1.0 / len(moments))
    square = sum(part[rows:] + count * jnp.square(part[:rows] - mean) for part in moments)
    return mean, square


def merge_kernel(count, first_ref, second_ref, out_ref):
    rows = out_ref.shape[0] // 2
    out_ref[:rows], out_ref[rows:] = merge((first_ref[...], second_ref[...]), count)


def normalise_kernel(count, inputs_ref, gain_ref, *refs):
    *moment_refs, normed_ref, scaled_ref, inv_std_ref = refs
    mean, square = merge([ref[...] for ref in moment_refs], count)
    inv_std = 1.0 / jnp.sqrt(square * (1.0 / (count * len(moment_refs))) + 1e-06)
    normed = (inputs_ref[...] - mean[:, :1]) * inv_std[:, :1]
    normed_ref[...] = normed
    scaled_ref[...] = normed * gain_ref[...]
    inv_std_ref[...] = inv_std


def slope_kernel(terms, earlier, *refs):
    back_refs, pre_refs, (bias_ref, weight_ref) = refs[:terms], refs[terms : 2 * terms], refs[2 * terms : 2 * terms + 2]
    sums_refs, act_refs = refs[2 * terms + 2 : 2 * terms + 2 + earlier], refs[2 * terms + 2 + earlier : -1]
    out_sums_ref = refs[-1]
    hidden = bias_ref.shape[1]
    product = sum(ref[...] for ref in pre_refs)
    act = sum(ref[...] for ref in back_refs) * gelu_slope(product + bias_ref[...])
    width = hidden // len(act_refs)
    for n, act_ref in enumerate(act_refs):
        act_ref[:, :width] = act[:, n * width : (n + 1) * width]
    lane = lax.broadcasted_iota(jnp.int32, out_sums_ref.shape, 1)
    first = jnp.sum(act * weight_ref[...], axis=1, keepdims=True)
    second = jnp.sum(act * product, axis=1, keepdims=True)
    sums = jnp.where(lane == 0, first, jnp.where(lane == 1, second, 0.0)) + sum(ref[...] for ref in sums_refs)
    out_sums_ref[...] = sums
    if act_refs[-1].shape[1] > width:
        act_refs[-1][:, width:] = sums


def prepare_kernel(rows, columns, block, depth, weight_ref, gain_ref, *refs):
    *part_refs, sums_ref, landed, arrived, totals = refs
    totals[...] = jnp.zeros_like(totals)
    width = part_refs[0].shape[1]
    steps = rows[1] // block

    def fetch(step):
        start = pl.multiple_of(rows[0] + step * block, block)
        slot = lax.rem(step, depth)
        return pltpu.make_async_copy(
            weight_ref.at[pl.ds(start, block), pl.ds(*columns)], landed.at[slot], arrived.at[slot]
        )

    for step in range(min(depth, steps)):
        fetch(step).start()

    @pl.loop(0, steps)
    def _(step):
        fetch(step).wait()
        tile = landed[lax.rem(step, depth)]
        high, low = split(tile)
        at = pl.ds(pl.multiple_of(step * block, block), block)
        totals[...] += jnp.sum((tile * gain_ref[at, :]).reshape(block // 8, 8, columns[1]), axis=0)
        for n, part_ref in enumerate(part_refs):
            part_ref[at, :] = (low if n % 2 else high)[:, n // 2 * width : (n // 2 + 1) * width]

        @pl.when(step + depth < steps)
        def _():
            fetch(step + depth).start()

    sums_ref[...] = jnp.sum(totals[...], axis=0, keepdims=True)


def prepare(weight, gain, rows, columns, after):
    block = divisor(rows[1], *[b for b in (256, 128, 64, 32) if b <= max(256 * 1536 // columns[1], 32)])
    depth = 4
    outs = (pltpu.VMEM((rows[1], columns[1] // 2), jnp.bfloat16),) * 4
    inside, anywhere = pl.BlockSpec(memory_space=pltpu.VMEM), pl.BlockSpec(memory_space=pl.ANY)
    result = pl.pallas_call(
        lambda weight_ref, gain_ref, *refs: prepare_kernel(
            rows, columns, block, depth, weight_ref, gain_ref, *refs[len(after) :]
        ),
        out_shape=outs + (jax.ShapeDtypeStruct((1, columns[1]), jnp.float32),),
        in_specs=[anywhere, inside] + [anywhere] * len(after),
        out_specs=[inside] * 5,
        scratch_shapes=[
            pltpu.VMEM((depth, block, columns[1]), jnp.float32),
            pltpu.SemaphoreType.DMA((depth,)),
            pltpu.VMEM((8, columns[1]), jnp.float32),
        ],
        compiler_params=pltpu.CompilerParams(vmem_limit_bytes=VMEM_LIMIT),
        cost_estimate=SHORT,
    )(pltpu.with_memory_space_constraint(weight, pltpu.HBM), gain, *after)
    return list(result[:4]), result[4]


def three_pass(both, high, low, contract):
    rows = both.shape[0] // 2
    dot = functools.partial(
        lax.dot_general,
        dimension_numbers=(((1,), (contract,)), ((), ())),
        preferred_element_type=jnp.float32,
    )
    first = dot(both[...], high)
    return first[:rows] + first[rows:] + dot(both[:rows, :], low)


def fill(both, block_refs, place_ref):
    count = block_refs[0].shape[0]
    total = both.shape[0] // 2
    for index, ref in enumerate(block_refs):
        high, low = split(ref[...])
        row = pl.multiple_of(place_ref[index] * count, count)
        both[pl.ds(row, count), :] = high
        both[pl.ds(total + row, count), :] = low


def follow(earlier_refs, out_refs):
    for earlier_ref, out_ref in zip(earlier_refs, out_refs):
        out_ref[:, : earlier_ref.shape[1]] = earlier_ref[...]
    return earlier_refs[0].shape[1] if earlier_refs else 0


def put(out_refs, at, value):
    row = 0
    for out_ref in out_refs:
        out_ref[:, at] = value[row : row + out_ref.shape[0]]
        row += out_ref.shape[0]


def parts_of(tokens, chips, hidden):
    block = tokens // (2 * chips)
    return [jax.ShapeDtypeStruct((n, hidden), jnp.float32) for n in (block, block * (chips - 1))] * 2


def forward_kernel(place_ref, slot_refs, weight_refs, earlier_refs, out_refs, both):
    fill(both, slot_refs, place_ref)
    column = follow(earlier_refs, out_refs)
    for high_ref, low_ref in zip(weight_refs[::2], weight_refs[1::2]):
        width = divisor(high_ref.shape[1], 256, 128)

        @pl.loop(0, high_ref.shape[1] // width, unroll=2)
        def _(step):
            at = pl.ds(pl.multiple_of(step * width, width), width)
            part = three_pass(both, high_ref[:, at], low_ref[:, at], 0)
            put(out_refs, pl.ds(pl.multiple_of(column + step * width, width), width), part)

        column += high_ref.shape[1]


def forward(slots, weights, place, earlier, after):
    tokens, depth = slots[0].shape[0] * len(slots), slots[0].shape[1]
    hidden = sum(w.shape[1] for w in weights[::2]) + (earlier[0].shape[1] if earlier else 0)
    inside, anywhere = pl.BlockSpec(memory_space=pltpu.VMEM), pl.BlockSpec(memory_space=pl.ANY)
    ends = [1 + len(slots), 1 + len(slots) + len(weights), 1 + len(slots) + len(weights) + len(earlier)]
    return pl.pallas_call(
        lambda *refs: forward_kernel(
            refs[0], refs[1 : ends[0]], refs[ends[0] : ends[1]], refs[ends[1] : ends[2]], refs[-5:-1], refs[-1]
        ),
        out_shape=parts_of(tokens, len(slots) // 2, hidden),
        in_specs=[pl.BlockSpec(memory_space=pltpu.SMEM)] + [inside] * (ends[2] - 1) + [anywhere] * len(after),
        out_specs=[inside] * 4,
        scratch_shapes=[pltpu.VMEM((2 * tokens, depth), jnp.bfloat16)],
        compiler_params=pltpu.CompilerParams(vmem_limit_bytes=VMEM_LIMIT),
        cost_estimate=SHORT,
    )(place, *slots, *[pltpu.with_memory_space_constraint(w, pltpu.VMEM) for w in weights], *earlier, *after)


def stream_kernel(first, depth, place_ref, slot_refs, weight_ref, out_refs, both, landed, arrived):
    width = landed.shape[1]
    steps = out_refs[0].shape[1] // width

    def fetch(step):
        start = pl.multiple_of(first + step * width, width)
        slot = lax.rem(step, depth)
        return pltpu.make_async_copy(weight_ref.at[pl.ds(start, width), :], landed.at[slot], arrived.at[slot])

    for step in range(min(depth, steps)):
        fetch(step).start()
    fill(both, slot_refs, place_ref)

    @pl.loop(0, steps)
    def _(step):
        fetch(step).wait()
        high, low = split(landed[lax.rem(step, depth)])
        put(out_refs, pl.ds(pl.multiple_of(step * width, width), width), three_pass(both, high, low, 1))

        @pl.when(step + depth < steps)
        def _():
            fetch(step + depth).start()


def stream(slots, weight, place, first, hidden, after):
    tokens, columns = slots[0].shape[0] * len(slots), slots[0].shape[1]
    width, depth = divisor(hidden, 256, 128), 4
    inside, anywhere = pl.BlockSpec(memory_space=pltpu.VMEM), pl.BlockSpec(memory_space=pl.ANY)
    last = 1 + len(slots)
    return pl.pallas_call(
        lambda *refs: stream_kernel(first, depth, refs[0], refs[1:last], refs[last], refs[-7:-3], *refs[-3:]),
        out_shape=parts_of(tokens, len(slots) // 2, hidden),
        in_specs=[pl.BlockSpec(memory_space=pltpu.SMEM)] + [inside] * len(slots) + [anywhere] * (1 + len(after)),
        out_specs=[inside] * 4,
        scratch_shapes=[
            pltpu.VMEM((2 * tokens, columns), jnp.bfloat16),
            pltpu.VMEM((depth, width, columns), jnp.float32),
            pltpu.SemaphoreType.DMA((depth,)),
        ],
        compiler_params=pltpu.CompilerParams(vmem_limit_bytes=8 * 1024 * 1024),
        cost_estimate=SHORT,
    )(place, *slots, pltpu.with_memory_space_constraint(weight, pltpu.HBM), *after)


def backward_kernel(first, depth, place_ref, act_refs, weight_refs, earlier_refs, out_refs, both, result, riders):
    block = act_refs[0].shape[0]
    total = block * len(act_refs)
    hidden = both.shape[1]
    for p, act_ref in enumerate(act_refs):
        if act_ref.shape[1] > hidden:
            riders[p * block : (p + 1) * block, :] = act_ref[:, hidden:]
        high, low = split(act_ref[:, :hidden])
        both[p * block : (p + 1) * block, :] = high
        both[total + p * block : total + (p + 1) * block, :] = low
    width = result.shape[1]

    if out_refs[0].shape[1] > depth:
        for b, out_ref in enumerate(out_refs):
            out_ref[:, depth:] = riders[pl.ds(pl.multiple_of(place_ref[b] * block, block), block), :]

    @pl.loop(0, depth // width)
    def _(step):
        at = pl.ds(pl.multiple_of(first + step * width, width), width)
        value, column = 0.0, 0
        for high_ref, low_ref in zip(weight_refs[::2], weight_refs[1::2]):
            columns = slice(column, column + high_ref.shape[1])
            value += three_pass(both[:, columns], high_ref[at, :], low_ref[at, :], 1)
            column = columns.stop
        result[...] = value
        for b, out_ref in enumerate(out_refs):
            rows = result[pl.ds(pl.multiple_of(place_ref[b] * block, block), block), :]
            if earlier_refs:
                rows = rows + earlier_refs[b][:, at]
            out_ref[:, pl.ds(pl.multiple_of(step * width, width), width)] = rows


def backward(acts, weights, place, earlier, first, depth, after):
    slots, block, hidden = len(acts), acts[0].shape[0], sum(w.shape[1] for w in weights[::2])
    riding = acts[0].shape[1] - hidden if first == 0 else 0
    width = divisor(depth, 256, 128)
    out = jax.ShapeDtypeStruct((block, depth + riding), jnp.float32)
    inside, anywhere = pl.BlockSpec(memory_space=pltpu.VMEM), pl.BlockSpec(memory_space=pl.ANY)
    ends = [1 + slots, 1 + slots + len(weights), 1 + slots + len(weights) + len(earlier)]
    return pl.pallas_call(
        lambda *refs: backward_kernel(
            first,
            depth,
            refs[0],
            refs[1 : ends[0]],
            refs[ends[0] : ends[1]],
            refs[ends[1] : ends[2]],
            refs[-3 - slots : -3],
            *refs[-3:],
        ),
        out_shape=[out] * slots,
        in_specs=[pl.BlockSpec(memory_space=pltpu.SMEM)] + [inside] * (ends[2] - 1) + [anywhere] * len(after),
        out_specs=[inside] * slots,
        scratch_shapes=[
            pltpu.VMEM((2 * block * slots, hidden), jnp.bfloat16),
            pltpu.VMEM((block * slots, width), jnp.float32),
            pltpu.VMEM((block * slots, 128), jnp.float32),
        ],
        compiler_params=pltpu.CompilerParams(vmem_limit_bytes=VMEM_LIMIT),
        cost_estimate=SHORT,
    )(place, *acts, *[pltpu.with_memory_space_constraint(w, pltpu.VMEM) for w in weights], *earlier, *after)


def body(hid_size, emb_size, inputs, out_grad, in_weight, in_bias, out_weight, norm_gain):
    chips = emb_size // 2
    tokens, depth = inputs.shape
    model_width = depth * emb_size
    hidden = in_weight.shape[1]
    me = lax.axis_index("emb")
    chip, core = me // 2, me % 2

    def along_hid(values, steps=1):
        return lax.ppermute(values, "hid", [(i, (i + steps) % hid_size) for i in range(hid_size)])

    def other_core(values):
        return lax.ppermute(values, "emb", [(i, i ^ 1) for i in range(emb_size)])

    def next_chip(values):
        return lax.ppermute(values, "emb", [(i, (i + 2) % emb_size) for i in range(emb_size)])

    owner = jnp.arange(emb_size, dtype=jnp.int32)
    place = ((owner % 2) ^ core) * chips + (owner // 2 - chip) % chips

    def gathered(values):
        return [values] + [along_hid(values, step) for step in range(1, hid_size)]

    def relayed(values):
        blocks = [values] + [None] * (hid_size - 1)
        for step in range(1, hid_size // 2 + 1):
            blocks[step] = along_hid(blocks[step - 1], 1)
        for step in range(1, hid_size - hid_size // 2):
            blocks[-step] = along_hid(blocks[(1 - step) % hid_size], -1)
        return blocks

    grads = gathered(out_grad)
    third = hidden // 3

    def tied(values, others):
        return lax.optimization_barrier((values, others))

    def halved(partial, behind=()):
        keep_own, keep, send_own, send = partial
        return keep + tied(other_core(send), behind)[0], (keep_own, other_core(send_own))

    def exchanged(half):
        summed, own = half
        terms = jnp.split(summed, chips - 1)
        arrival = next_chip(terms[chips - 2])
        for step in range(chips - 3, -1, -1):
            arrival = next_chip(arrival + terms[step])
        return arrival, *own

    def prepared(c, after):
        return prepare(in_weight, norm_gain[:, None], (0, depth), (c * third, third), after)

    moments = call(moments_kernel, jax.ShapeDtypeStruct((2 * tokens, 128), jnp.float32), (inputs,), ())
    in_parts, sums_0 = prepared(0, [place, moments])
    parts, sums_1 = prepared(1, [in_parts[0]])
    in_parts += parts
    moments = call(
        functools.partial(merge_kernel, depth), moments, (moments, other_core(moments)), (in_parts[4], *grads[1:])
    )
    parts = [moments]
    for _ in range(1, chips):
        parts.append(next_chip(parts[-1]))
    normed, scaled, inv_std = call(
        functools.partial(normalise_kernel, 2 * depth),
        (inputs, inputs, jax.ShapeDtypeStruct((tokens, 128), jnp.float32)),
        (inputs, norm_gain[None, :], *parts),
        (),
    )
    inv_std = inv_std[:, :1]
    scaled = relayed(scaled)
    back_0 = stream(grads, out_weight, place, 0, 2 * third, [scaled[0]])
    back_0, (scaled[1], scaled[-1]) = tied(back_0, (scaled[1], scaled[-1]))
    half_0 = halved(back_0)
    back_1 = stream(grads, out_weight, place, 2 * third, third, [half_0[0]])
    back_0 = exchanged(half_0)
    back_1, scaled = tied(back_1, scaled)
    pre_0 = forward(scaled, in_parts[:8], place, (), [back_1[0]])
    half_1 = halved(back_1, (pre_0, back_0[0]))
    back_1 = exchanged(half_1)
    half_0 = halved(pre_0)
    parts, sums_2 = prepared(2, [half_0[0], half_1[0]])
    in_parts += parts
    pre_1 = forward(scaled, in_parts[8:], place, (), [half_0[0], back_1[0]])
    pre_0 = exchanged(half_0)

    gain_sums, _ = tied(jnp.concatenate([sums_0, sums_1, sums_2], axis=1), pre_1)
    gain_sums = passing = gain_sums + other_core(gain_sums)
    for _ in range(1, chips):
        passing = next_chip(passing)
        gain_sums = gain_sums + passing

    def slope_product(span, back, pre, sums, after):
        pieces, room = (span.stop - span.start) // third, 128 * len(sums)
        widths = [third] * (pieces - 1) + [third + room, 128]
        return call(
            functools.partial(slope_kernel, len(back), len(sums)),
            tuple(jax.ShapeDtypeStruct((tokens, n), jnp.float32) for n in widths),
            (*back, *pre, in_bias[None, span], gain_sums[:, span], *sums),
            after,
        )

    def spread_out(act):
        mine = [None] * chips
        mine[0] = act
        for step in range(1, chips):
            act = next_chip(act)
            mine[(chips - step) % chips] = act
        return mine

    def both_cores(mine):
        return mine + [other_core(block) for block in mine]

    def summed_along_hid(sums, behind=()):
        arrivals = [along_hid(sums[step], -step) for step in range(1, hid_size)]
        return sum(tied(arrivals, behind)[0], start=sums[0])

    half_1 = halved(pre_1, pre_0[0])
    pre_0 = tied(pre_0, half_1[0])[0]
    act_0, act_1, sums_0 = slope_product(slice(0, 2 * third), back_0, pre_0, (), ())
    pre_1 = exchanged(half_1)
    sums = backward(both_cores(spread_out(act_0)), in_parts[:4], place, (), 0, depth, [])
    act_2, _ = slope_product(slice(2 * third, hidden), back_1, pre_1, (sums_0,), (sums[0],))
    acts_0, acts_1 = spread_out(act_1), spread_out(act_2)
    sums = backward(both_cores(acts_0), in_parts[4:8], place, sums, 0, depth, [act_2])
    acts_1[1:], sums = tied(acts_1[1:], sums)
    acts_1 = both_cores(acts_1)
    width = depth // 3 if depth % 768 == 0 else depth
    ends = []
    for start, extent in ((0, width), (width, depth - width))[: 1 if width == depth else 2]:
        after = [ends[-1][0]] if ends else []
        ends.append(backward(acts_1, in_parts[8:], place, sums, start, extent, after))
    first = summed_along_hid(ends[0])
    others = [summed_along_hid(end, first) for end in ends[1:]]
    normed_grad = jnp.concatenate([first[:, :width], *others], axis=1) * norm_gain
    mean, slope = first[:, width : width + 1] / model_width, first[:, width + 1 : width + 2] / model_width
    return inv_std * (normed_grad - mean - normed * slope)


def solution(mesh):
    hid_size, emb_size = mesh.shape["hid"], mesh.shape["emb"]
    assert hid_size == emb_size and emb_size % 2 == 0
    return jax.shard_map(
        functools.partial(body, hid_size, emb_size),
        mesh=mesh,
        in_specs=(
            P(("groups", "hid"), "emb"),
            P(("groups", "hid"), "emb"),
            P("emb", "hid"),
            P("hid"),
            P("hid", "emb"),
            P("emb"),
        ),
        out_specs=P(("groups", "hid"), "emb"),
        check_vma=False,
    )
```
